32 devices in a mesh: grp: 2 (over y), wide: 4 (over z), narrow: 2 (over x), tile: 2 (over core).
Axes of the slice: x: 2, y: 2, z: 4, core: 2. Of those that a mesh axis runs over, the one named last changes fastest.
Arguments:
- green: bfloat16 [32768, 1024], P(('grp', 'wide', 'narrow', 'tile')), parts along dimension 0, may hold values from -0.52734375 to 0.52734375
- log_strength: float32 [32768], P(('grp', 'wide', 'narrow', 'tile')), parts along dimension 0, may hold values from -1 to 1
- observed: float32 [1056, 512], P('grp'), parts along dimension 0, may hold values from -6 to 6
- owner_map: int32 [1056], P('grp'), parts along dimension 0, may hold values from 0 to 527, each once
Outputs:
- new_log_strength: float32 [32768], P(('grp', 'wide', 'narrow', 'tile')), parts along dimension 0
- residual: float32 [1056, 512], P(('grp', 'wide')), parts along dimension 0
The draws below stay inside these ranges and needn't reach their ends.
There are 2 independent parts, one for each index of `grp`. The reference program is written for one: setup_inputs(seed, part) draws one part's arguments, and reference() takes and returns one part's arrays. A program takes and returns all parts, laid end to end along the dimension named above; each array names one. Nothing has to cross between parts.
Inputs may be any that keep to these rules, and one draw needn't show every extreme that they name: `owner_map`: every tile number appears once; the slots form 4 equal runs in order, the k-th run owned by the k-th index of wide.
All inputs are finite; a program needn't handle non-finite values.
Results may differ from the reference program's by a relative error of at most 0.0018.
Values may be sent and summed in bfloat16 or wider, within the bound.
No kernel may reach another device: no remote copies, remote signals or barrier semaphores. Data moves between devices by JAX's collectives and lax.ppermute only.
A program may use at most 64 MiB of HBM per device.

```python
import jax
import jax.numpy as jnp
import numpy as np
from jax import lax

NS = 512
NB = 32
STEPS = 2
NPTS = 16384
B = 16
TILES = 528


def block_levels(key, shape, pieces, least, top_value):
    loudness, own = 1.0, jax.random.fold_in(key, 6)
    for dim, shards_of in pieces:
        steps = jnp.exp(jax.random.uniform(jax.random.fold_in(own, dim), (shards_of,), jnp.float32, least / len(pieces), top_value / len(pieces)))
        loudness = loudness * jnp.repeat(steps, shape[dim] // shards_of).reshape([-1 if axis == dim else 1 for axis in range(len(shape))])
    return loudness


def gaussian(key, shape, scale, limit, pieces=(), kind=jnp.bfloat16):
    values = scale * jax.random.normal(key, shape, jnp.float32)
    if pieces:
        values = values * block_levels(key, shape, pieces, -0.22, 0.18)
    return jnp.clip(values, -limit, limit).astype(kind)


def setup_inputs(seed: int = 0, part: int = 0) -> dict:
    streams_of = jax.random.split(jax.random.key(seed), 5)
    part_keys = jax.random.split(jax.random.fold_in(streams_of[4], part), 5)
    green = gaussian(part_keys[0], (NPTS, 2 * NS), (NPTS ** -0.25), 0.52734375, ((0, 16),))
    log_strength = jnp.clip(jax.random.uniform(part_keys[1], (NPTS,), jnp.float32, -1.0, 1.0) * block_levels(part_keys[1], (NPTS,), ((0, 16),), -0.4, 0.0), -1.0, 1.0)
    observed = gaussian(part_keys[2], (TILES, 2 * B * B), 1.0, 6.0, (), jnp.float32)
    owner_map = jax.random.permutation(part_keys[3], TILES).astype(jnp.int32)
    return {"green": green, "log_strength": log_strength, "observed": observed, "owner_map": owner_map}


def upper_index(blocks):
    rows, cols = np.triu_indices(blocks)
    return jnp.asarray(rows * blocks + cols, dtype=jnp.int32)


def tile_spectra(green, strength, blocks):
    stations = green.shape[1] // 2
    width = stations // blocks
    weighted = (green.astype(jnp.float32) * strength[:, None]).astype(jnp.bfloat16)
    product = lax.dot_general(weighted, green, (((0,), (0,)), ((), ())), preferred_element_type=jnp.float32)
    real_part = product[:stations, :stations] + product[stations:, stations:]
    imag_part = product[stations:, :stations] - product[:stations, stations:]
    picked = upper_index(blocks)

    def to_tiles(matrix):
        return matrix.reshape(blocks, width, blocks, width).transpose(0, 2, 1, 3).reshape(blocks * blocks, width * width)

    return jnp.concatenate([to_tiles(real_part)[picked], to_tiles(imag_part)[picked]], axis=1)


def contraction(green, kernel_tiles, blocks):
    stations = green.shape[1] // 2
    width = stations // blocks
    full_tiles = jnp.zeros((blocks * blocks, 2 * width * width), jnp.bfloat16).at[upper_index(blocks)].set(kernel_tiles)

    def to_matrix(flat):
        return flat.reshape(blocks, blocks, width, width).transpose(0, 2, 1, 3).reshape(stations, stations)

    real_part = to_matrix(full_tiles[:, :width * width])
    imag_part = to_matrix(full_tiles[:, width * width:])
    kernel = jnp.concatenate([jnp.concatenate([real_part, -imag_part], axis=1), jnp.concatenate([imag_part, real_part], axis=1)], axis=0)
    mapped = jnp.dot(green, kernel, preferred_element_type=jnp.float32)
    return jnp.sum(green.astype(jnp.float32) * mapped, axis=1)


def reference(green, log_strength, observed, owner_map):
    log_now = log_strength
    tile_residual = observed
    for iteration in range(STEPS):
        strength = jnp.exp(log_now)
        spectra_tiles = tile_spectra(green, strength, NB)
        tile_residual = jnp.tanh(spectra_tiles - observed)
        kernel_tiles = tile_residual.astype(jnp.bfloat16)
        log_now = log_now - 0.5 * strength * contraction(green, kernel_tiles, NB)
    return log_now, tile_residual[owner_map]
```

```python
import math

import jax
import jax.numpy as jnp
import numpy as np
from jax import lax
from jax.experimental import pallas as pl
from jax.experimental.pallas import tpu as pltpu
from jax.sharding import PartitionSpec as P

STEPS = 2
LANES = 128
WIDE_BLOCK = 256
SUB = 16
TOP = 14.0
F32, BF16, F16 = jnp.float32, jnp.bfloat16, jnp.float16
VMEM = pl.BlockSpec(memory_space=pltpu.VMEM)
SMEM = pl.BlockSpec(memory_space=pltpu.SMEM)


class Plan:
    def __init__(self, mesh, green, observed, owner_map):
        self.points, columns = green.shape
        self.stations = columns // 2
        self.area = observed.shape[1] // 2
        self.width = math.isqrt(self.area)
        self.blocks = self.stations // self.width
        self.group = LANES // self.width
        self.wide = mesh.shape["wide"]
        self.narrow = mesh.shape["narrow"]
        side = self.stations // LANES
        self.pairs = [(i, j) for i in range(side) for j in range(i, side)]
        self.place = {pair: k for k, pair in enumerate(self.pairs)}
        rows = len(self.pairs) * LANES
        self.chunk = -(-rows // (self.wide * SUB)) * SUB
        self.piece = math.gcd(LANES, self.chunk)
        self.rows = self.wide * self.chunk
        self.slots = owner_map.shape[0] // self.wide

    def pieces(self):
        for k, (i, j) in enumerate(self.pairs):
            for r in range(0, LANES, self.piece):
                row = k * LANES + r
                yield i, j, r, row // self.chunk, row % self.chunk

    def strip_starts(self):
        starts = np.zeros(self.rows // self.width, np.int32)
        per = LANES // self.width
        for k, (i, j) in enumerate(self.pairs):
            for r in range(per):
                a, b = i * per + r, j * self.group
                starts[k * per + r] = a * self.blocks - a * (a - 1) // 2 + b - a
        return starts

    def tile_places(self):
        rows, cols = np.triu_indices(self.blocks)
        per = LANES // self.width
        table = [
            (self.place[(i // per, j // per)] * per + i % per) * self.group + j % per
            for i, j in zip(rows, cols)
        ]
        return np.asarray(table, np.int32)


def contract(a, b, over_a, over_b):
    return lax.dot_general(a, b, (((over_a,), (over_b,)), ((), ())), preferred_element_type=F32)


def swap_groups(x, width):
    n = LANES // width
    row = lax.broadcasted_iota(jnp.int32, (n, LANES), 0)
    run = lax.broadcasted_iota(jnp.int32, (n, LANES), 1) // width
    shift = (row - run + n) % n
    out = x
    for d in range(1, n):
        moved = pltpu.roll(pltpu.roll(x, d, 0), LANES - width * d, 1)
        out = jnp.where(shift == d, moved, out)
    return out


def to_column(rows):
    eye = lax.broadcasted_iota(jnp.int32, (LANES, LANES), 0) == lax.broadcasted_iota(
        jnp.int32, (LANES, LANES), 1
    )
    parts = []
    for i in range(rows.shape[0]):
        spread = jnp.broadcast_to(rows[i : i + 1, :], (LANES, LANES))
        parts.append(jnp.sum(jnp.where(eye, spread, 0.0), axis=1, keepdims=True))
    return jnp.concatenate(parts, axis=0)


def to_rows(column, out_ref):
    eye = lax.broadcasted_iota(jnp.int32, (LANES, LANES), 0) == lax.broadcasted_iota(
        jnp.int32, (LANES, LANES), 1
    )
    for i in range(column.shape[0] // LANES):
        spread = jnp.broadcast_to(column[i * LANES : (i + 1) * LANES], (LANES, LANES))
        out_ref[i : i + 1, :] = jnp.sum(jnp.where(eye, spread, 0.0), axis=0, keepdims=True)


def product(plan, green, strength, weighted, send, own):
    core, z = lax.axis_index("tile"), lax.axis_index("wide")
    ns = plan.stations
    for h in range(2):
        weighted[h] = (green[:, h * ns : (h + 1) * ns].astype(F32) * strength).astype(BF16)
    flip = (1 - 2 * core).astype(F32)
    most = jnp.zeros((8, LANES), F32)
    for out, first, sign in ((send, 1 - core, -flip), (own, core, flip)):
        for j in range(ns // WIDE_BLOCK):
            end = WIDE_BLOCK * (j + 1)
            a = green[:, end - WIDE_BLOCK : end]
            b = green[:, ns + end - WIDE_BLOCK : ns + end]
            part = contract(weighted[first, :, :end], a, 0, 0)
            part = part + sign * contract(weighted[1 - first, :, :end], b, 0, 0)
            for bi, bj, r, chunk, at in plan.pieces():
                if bj * LANES // WIDE_BLOCK != j:
                    continue
                left = bj * LANES % WIDE_BLOCK
                top = bi * LANES + r
                value = part[top : top + plan.piece, left : left + LANES]
                out[chunk ^ z, at : at + plan.piece, :] = value
                folded = jnp.max(jnp.abs(value).reshape(-1, 8, LANES), axis=0)
                most = jnp.maximum(most, folded)
    top = jnp.max(jnp.max(most, axis=0, keepdims=True), axis=1, keepdims=True)
    level = jnp.ceil(jnp.log2(jnp.maximum(top, 1e-30)))
    level = jnp.broadcast_to(level, (plan.wide, SUB, LANES))
    send[:, plan.chunk :, :] = level
    own[:, plan.chunk :, :] = level


def fill_kernel(plan, load, kernel):
    core, z = lax.axis_index("tile"), lax.axis_index("wide")
    row = lax.broadcasted_iota(jnp.int32, (plan.piece, LANES), 0)
    run = lax.broadcasted_iota(jnp.int32, (plan.piece, LANES), 1) // plan.width
    for q in range(2):
        half = q ^ core
        for bi, bj, r, chunk, at in plan.pieces():
            value = load(q, chunk ^ z, at)
            if bi == bj:
                value = jnp.where((row + r) // plan.width <= run, value, 0.0)
            top = bi * LANES + r
            kernel[half, top : top + plan.piece, bj * LANES : (bj + 1) * LANES] = value.astype(BF16)
        for k in range(plan.stations // WIDE_BLOCK):
            at = k * WIDE_BLOCK
            kernel[half, at + LANES : at + WIDE_BLOCK, at : at + LANES] = jnp.zeros(
                (WIDE_BLOCK - LANES, LANES), BF16
            )


def contraction(plan, green, kernel):
    ns = plan.stations
    total = jnp.zeros((plan.points, LANES), F32)
    for j in range(ns // WIDE_BLOCK):
        end = WIDE_BLOCK * (j + 1)
        real = kernel[0, :end, end - WIDE_BLOCK : end]
        imag = kernel[1, :end, end - WIDE_BLOCK : end]
        a, b = green[:, :end], green[:, ns : ns + end]
        u = contract(a, real, 1, 0) + contract(b, imag, 1, 0)
        v = contract(b, real, 1, 0) - contract(a, imag, 1, 0)
        x = green[:, end - WIDE_BLOCK : end].astype(F32)
        y = green[:, ns + end - WIDE_BLOCK : ns + end].astype(F32)
        part = u * x + v * y
        for left in range(0, WIDE_BLOCK, LANES):
            total = total + part[:, left : left + LANES]
    return jnp.sum(total, axis=1, keepdims=True)


def observed_kernel(plan, starts, observed, out):
    core, z = lax.axis_index("tile"), lax.axis_index("wide")
    strips = plan.chunk // plan.width
    left = pl.multiple_of(core * plan.area, LANES)

    n = plan.group
    row = lax.broadcasted_iota(jnp.int32, (n, LANES), 0)
    last = observed.shape[0] // n * n - n

    def strip(s, carry):
        start = starts[z * strips + s]
        low = pl.multiple_of(start // n * n, n)
        high = pl.multiple_of(jnp.minimum(low + n, last), n)
        skip = start - low
        for part in range(plan.area // LANES):
            at = pl.ds(pl.multiple_of(left + part * LANES, LANES), LANES)
            tiles = jnp.where(row >= skip, observed[pl.ds(low, n), at], observed[pl.ds(high, n), at])
            tiles = pltpu.roll(tiles, (n - skip) % n, 0)
            to = pl.multiple_of(s * plan.width + part * n, n)
            out[pl.ds(to, n), :] = swap_groups(tiles, plan.width)
        return carry

    lax.fori_loop(0, strips, strip, 0)


def first_kernel(plan, log_ref, green, send, own, weighted):
    product(plan, green, jnp.exp(to_column(log_ref[...])), weighted, send, own)


def middle_kernel(plan, log_ref, green, *refs):
    tiles = refs[: 2 * plan.wide]
    send, own, log_out, weighted, kernel, stack = refs[2 * plan.wide :]
    for k, ref in enumerate(tiles):
        stack[k] = ref[...]
    fill_kernel(
        plan,
        lambda q, slot, at: stack[q * plan.wide + slot, at : at + plan.piece, :],
        kernel,
    )
    log_now = to_column(log_ref[...])
    log_now = log_now - 0.5 * jnp.exp(log_now) * contraction(plan, green, kernel)
    to_rows(log_now, log_out)
    product(plan, green, jnp.exp(log_now), weighted, send, own)


def last_kernel(plan, log_ref, green, tiles, owners, places, log_out, residual, kernel):
    core, z = lax.axis_index("tile"), lax.axis_index("wide")
    fill_kernel(
        plan,
        lambda q, slot, at: tiles[q * plan.wide + slot, at : at + plan.piece, :],
        kernel,
    )
    log_now = to_column(log_ref[...])
    log_now = log_now - 0.5 * jnp.exp(log_now) * contraction(plan, green, kernel)
    to_rows(log_now, log_out)

    n = plan.group
    run = lax.broadcasted_iota(jnp.int32, (plan.width, LANES), 1) // plan.width

    def rows_of(first, count):
        found = [jnp.zeros((plan.width, LANES), F32) for _ in range(2)]
        for m in range(count):
            where = places[owners[z * plan.slots + first + m]]
            strip, col = where // n, where % n
            row = strip * plan.width
            slot = (row // plan.chunk) ^ z
            at = pl.multiple_of(row % plan.chunk, plan.width)
            shift = ((m - col + n) % n) * plan.width
            for h in range(2):
                value = tiles[(h ^ core) * plan.wide + slot, pl.ds(at, plan.width), :]
                found[h] = jnp.where(run == m, pltpu.roll(value, shift, 1), found[h])
        return [
            swap_groups(found[h][k * n : (k + 1) * n], plan.width)
            for h in range(2)
            for k in range(plan.width // n)
        ]

    def batch(i, carry):
        first = pl.multiple_of(i * n, n)
        for k, piece in enumerate(rows_of(first, n)):
            residual[pl.ds(first, n), k * LANES : (k + 1) * LANES] = piece
        return carry

    whole = plan.slots // n
    lax.fori_loop(0, whole, batch, 0)
    rest = plan.slots - whole * n
    if rest:
        for k, piece in enumerate(rows_of(whole * n, rest)):
            residual[whole * n :, k * LANES : (k + 1) * LANES] = piece[:rest]


def call(kernel, plan, out_shape, scratch, arguments, specs):
    def body(*refs):
        kernel(plan, *refs)

    return pl.pallas_call(
        body,
        in_specs=specs,
        out_specs=jax.tree.map(lambda _: VMEM, out_shape),
        out_shape=out_shape,
        scratch_shapes=scratch,
        compiler_params=pltpu.CompilerParams(vmem_limit_bytes=24 * 1024 * 1024),
    )(*arguments)


def exchange(x, axis, mask, size):
    return lax.ppermute(x, axis, [(i, i ^ mask) for i in range(size)])


def reduce_spectra(plan, send, own):
    recv = exchange(send, "tile", 1, 2)
    kept = own[0, : plan.chunk] + recv[0, : plan.chunk]
    body = lax.broadcasted_iota(jnp.int32, own.shape[1:], 0) < plan.chunk
    arrived = []
    for k in range(1, plan.wide):
        level = jnp.maximum(own[k, plan.chunk, 0], recv[k, plan.chunk, 0]) + (1.0 - TOP)
        message = jnp.where(body, (own[k] + recv[k]) * jnp.exp2(-level), level).astype(F16)
        arrived.append(exchange(message, "wide", k, plan.wide))
    total = kept
    for message in arrived:
        wider = message.astype(F32)
        total = total + wider[: plan.chunk] * jnp.exp2(wider[plan.chunk, 0])
    mask = 1
    while mask < plan.narrow:
        total = total + exchange(total, "narrow", mask, plan.narrow)
        mask *= 2
    return total


def spread(plan, chunk):
    mine = [chunk] + [exchange(chunk, "wide", k, plan.wide) for k in range(1, plan.wide)]
    return mine + [exchange(x, "tile", 1, 2) for x in mine]


def on_device(mesh, green, log_strength, observed, owner_map):
    plan = Plan(mesh, green, observed, owner_map)
    shape = jax.ShapeDtypeStruct
    log_now = log_strength.reshape(-1, LANES)
    log_shape = shape(log_now.shape, F32)
    message = shape((plan.wide, plan.chunk + SUB, LANES), F32)
    weighted = pltpu.VMEM((2, plan.points, plan.stations), BF16)
    kernel = pltpu.VMEM((2, plan.stations, plan.stations), BF16)

    target = call(
        observed_kernel, plan, shape((plan.chunk, LANES), F32), [],
        (jnp.asarray(plan.strip_starts()), observed), [SMEM, VMEM],
    )
    send, own = call(first_kernel, plan, (message, message), [weighted], (log_now, green), [VMEM] * 2)
    for _ in range(STEPS - 1):
        residual = jnp.tanh(reduce_spectra(plan, send, own) - target)
        tiles = spread(plan, residual.astype(BF16))
        stack = pltpu.VMEM((2 * plan.wide, plan.chunk, LANES), BF16)
        send, own, log_now = call(
            middle_kernel, plan, (message, message, log_shape), [weighted, kernel, stack],
            (log_now, green, *tiles), [VMEM] * (2 + len(tiles)),
        )
    residual = jnp.tanh(reduce_spectra(plan, send, own) - target)
    tiles = jnp.stack(spread(plan, residual.astype(F16))).astype(F32)
    log_now, owned = call(
        last_kernel, plan, (log_shape, shape((plan.slots, observed.shape[1]), F32)), [kernel],
        (log_now, green, tiles, owner_map, jnp.asarray(plan.tile_places())),
        [VMEM, VMEM, VMEM, SMEM, SMEM],
    )
    return log_now.reshape(-1), owned


def solution(mesh):
    points = P(("grp", "wide", "narrow", "tile"))
    in_specs = (P(("grp", "wide", "narrow", "tile"), None), points, P("grp", None), P("grp"))
    out_specs = (points, P(("grp", "wide"), None))

    def program(green, log_strength, observed, owner_map):
        return on_device(mesh, green, log_strength, observed, owner_map)

    return jax.shard_map(
        program, mesh=mesh, in_specs=in_specs, out_specs=out_specs, check_vma=False
    )
```

```python
import math

import jax
import jax.numpy as jnp
import numpy as np
from jax import lax
from jax.experimental import pallas as pl
from jax.experimental.pallas import tpu as pltpu
from jax.sharding import PartitionSpec as P

STEPS = 2
LANES = 128
WIDE_BLOCK = 256
SUB = 16
TOP = 14.0
LN2 = math.log(2.0)
F32, BF16, F16 = jnp.float32, jnp.bfloat16, jnp.float16
VMEM = pl.BlockSpec(memory_space=pltpu.VMEM)
SMEM = pl.BlockSpec(memory_space=pltpu.SMEM)


class Plan:
    def __init__(self, mesh, green, observed, owner_map):
        self.points, columns = green.shape
        self.stations = columns // 2
        self.area = observed.shape[1] // 2
        self.width = math.isqrt(self.area)
        self.blocks = self.stations // self.width
        self.group = LANES // self.width
        self.wide = mesh.shape["wide"]
        self.narrow = mesh.shape["narrow"]
        self.strips = self.list_strips()
        self.run = -(-len(self.strips) // self.wide)
        self.chunk = self.run * self.width
        self.slots = owner_map.shape[0] // self.wide

    def list_strips(self):
        side, per, w = self.stations // LANES, self.group, self.width
        strips = []
        for i in range(side):
            for j in range(i + 1, side):
                strips += [[(i * per + s, j, 0, LANES, 0)] for s in range(per)]
        for i in range(side):
            for s in range(per // 2):
                strip = [(i * per + s, i, s * w, LANES, 0)]
                if s:
                    strip.append((i * per + per - s, i, 0, s * w, s * w))
                strips.append(strip)
        half = LANES // 2
        for i in range(0, side, 2):
            strip = [(i * per + per // 2, i, half, LANES, 0)]
            if i + 1 < side:
                strip.append(((i + 1) * per + per // 2, i + 1, 0, half, half))
            strips.append(strip)
        return strips

    def tile(self, row, col):
        return row * self.blocks - row * (row - 1) // 2 + col - row

    def strip_table(self):
        table = np.zeros((3, self.run * self.wide), np.int32)
        for k, strip in enumerate(self.strips):
            row, j, first, _, _ = strip[0]
            table[0, k] = self.tile(row, j * self.group)
            if len(strip) > 1:
                row, j, _, last, shift = strip[1]
                table[1, k] = self.tile(row, (j + 1) * self.group - shift // self.width)
                table[2, k] = last // self.width
        return table.reshape(-1)

    def tile_places(self):
        places = np.zeros(self.tile(self.blocks - 1, self.blocks - 1) + 1, np.int32)
        for k, strip in enumerate(self.strips):
            for row, j, first, last, shift in strip:
                for m in range(first // self.width, last // self.width):
                    col = j * self.group + m - shift // self.width + (self.group if shift > m * self.width else 0)
                    at = (k % self.run) * self.width
                    places[self.tile(row, col)] = (k // self.run) * 65536 + at * 16 + m
        return places


def contract(a, b, over_a, over_b):
    return lax.dot_general(a, b, (((over_a,), (over_b,)), ((), ())), preferred_element_type=F32)


def swap_groups(x, width):
    n = LANES // width
    row = lax.broadcasted_iota(jnp.int32, (n, LANES), 0)
    run = lax.broadcasted_iota(jnp.int32, (n, LANES), 1) // width
    d = n // 2
    while d:
        up = pltpu.roll(pltpu.roll(x, n - d, 0), width * d, 1)
        down = up if 2 * d == n else pltpu.roll(pltpu.roll(x, d, 0), LANES - width * d, 1)
        low, high = (row & d) == 0, (run & d) == 0
        x = jnp.where(low == high, x, jnp.where(low, up, down))
        d //= 2
    return x


def to_column(rows):
    eye = lax.broadcasted_iota(jnp.int32, (LANES, LANES), 0) == lax.broadcasted_iota(
        jnp.int32, (LANES, LANES), 1
    )
    parts = []
    for i in range(rows.shape[0]):
        spread = jnp.broadcast_to(rows[i : i + 1, :], (LANES, LANES))
        parts.append(jnp.sum(jnp.where(eye, spread, 0.0), axis=1, keepdims=True))
    return jnp.concatenate(parts, axis=0)


def to_rows(column, out_ref):
    eye = lax.broadcasted_iota(jnp.int32, (LANES, LANES), 0) == lax.broadcasted_iota(
        jnp.int32, (LANES, LANES), 1
    )
    for i in range(column.shape[0] // LANES):
        spread = jnp.broadcast_to(column[i * LANES : (i + 1) * LANES], (LANES, LANES))
        out_ref[i : i + 1, :] = jnp.sum(jnp.where(eye, spread, 0.0), axis=0, keepdims=True)


def product(plan, green, strength, weighted, send, own):
    core, z = lax.axis_index("tile"), lax.axis_index("wide")
    ns, w = plan.stations, plan.width
    for h in range(2):
        weighted[h] = (green[:, h * ns : (h + 1) * ns].astype(F32) * strength).astype(BF16)
    flip = (1 - 2 * core).astype(F32)
    lane = lax.broadcasted_iota(jnp.int32, (w, LANES), 1)
    most = jnp.zeros((w, LANES), F32)
    for out, first, sign in ((send, 1 - core, -flip), (own, core, flip)):
        for j in range(ns // WIDE_BLOCK):
            end = WIDE_BLOCK * (j + 1)
            a = green[:, end - WIDE_BLOCK : end]
            b = green[:, ns + end - WIDE_BLOCK : ns + end]
            part = contract(weighted[first, :, :end], a, 0, 0)
            part = part + sign * contract(weighted[1 - first, :, :end], b, 0, 0)
            for k, strip in enumerate(plan.strips):
                if strip[0][1] * LANES // WIDE_BLOCK != j:
                    continue
                value = None
                for row, bj, _, last, shift in strip:
                    left = bj * LANES % WIDE_BLOCK
                    seen = part[row * w : (row + 1) * w, left : left + LANES]
                    seen = pltpu.roll(seen, shift, 1) if shift else seen
                    value = seen if value is None else jnp.where(lane < last, seen, value)
                at = k % plan.run * w
                out[(k // plan.run) ^ z, at : at + w, :] = value
                if send.shape[1] > plan.chunk:
                    most = jnp.maximum(most, jnp.abs(value))
        for k in range(len(plan.strips), plan.run * plan.wide):
            at = k % plan.run * w
            out[(k // plan.run) ^ z, at : at + w, :] = jnp.zeros((w, LANES), F32)
    if send.shape[1] > plan.chunk:
        top = jnp.max(jnp.max(most, axis=0, keepdims=True), axis=1, keepdims=True)
        level = jnp.ceil(jnp.log2(jnp.maximum(top, 1e-30)))
        level = jnp.broadcast_to(level, (plan.wide, SUB, LANES))
        send[:, plan.chunk :, :] = level
        own[:, plan.chunk :, :] = level


def fill_kernel(plan, load, kernel):
    core, z = lax.axis_index("tile"), lax.axis_index("wide")
    w = plan.width
    lane = lax.broadcasted_iota(jnp.int32, (w, LANES), 1)
    for q in range(2):
        half = q ^ core
        for k, strip in enumerate(plan.strips):
            value = load(q, (k // plan.run) ^ z, k % plan.run * w)
            for row, bj, first, _, shift in strip:
                seen = value
                if shift:
                    seen = pltpu.roll(value.astype(F32), LANES - shift, 1)
                start = first if not shift else LANES - shift
                if start:
                    seen = jnp.where(lane >= start, seen.astype(F32), 0.0)
                at = pl.ds(bj * LANES, LANES)
                kernel[half, row * w : (row + 1) * w, at] = seen.astype(BF16)
        for k in range(plan.stations // WIDE_BLOCK):
            at = k * WIDE_BLOCK
            kernel[half, at + LANES : at + WIDE_BLOCK, at : at + LANES] = jnp.zeros(
                (WIDE_BLOCK - LANES, LANES), BF16
            )


def contraction(plan, green, kernel):
    ns = plan.stations
    total = jnp.zeros((plan.points, LANES), F32)
    for j in range(ns // WIDE_BLOCK):
        end = WIDE_BLOCK * (j + 1)
        real = kernel[0, :end, end - WIDE_BLOCK : end]
        imag = kernel[1, :end, end - WIDE_BLOCK : end]
        a, b = green[:, :end], green[:, ns : ns + end]
        u = contract(a, real, 1, 0) + contract(b, imag, 1, 0)
        v = contract(b, real, 1, 0) - contract(a, imag, 1, 0)
        x = green[:, end - WIDE_BLOCK : end].astype(F32)
        y = green[:, ns + end - WIDE_BLOCK : ns + end].astype(F32)
        part = u * x + v * y
        for left in range(0, WIDE_BLOCK, LANES):
            total = total + part[:, left : left + LANES]
    return jnp.sum(total, axis=1, keepdims=True)


def observed_kernel(plan, table, observed, out):
    core, z = lax.axis_index("tile"), lax.axis_index("wide")
    left = pl.multiple_of(core * plan.area, LANES)
    n, count = plan.group, plan.run * plan.wide
    row = lax.broadcasted_iota(jnp.int32, (n, LANES), 0)
    last = observed.shape[0] // n * n - n

    def strip(s, carry):
        k = z * plan.run + s
        split = table[2 * count + k]
        for part in range(plan.area // LANES):
            at = pl.ds(pl.multiple_of(left + part * LANES, LANES), LANES)
            found = []
            for start in (table[k], table[count + k]):
                low = pl.multiple_of(start // n * n, n)
                high = pl.multiple_of(jnp.minimum(low + n, last), n)
                skip = start - low
                tiles = jnp.where(row >= skip, observed[pl.ds(low, n), at], observed[pl.ds(high, n), at])
                found.append(pltpu.roll(tiles, (n - skip) % n, 0))
            tiles = jnp.where(row < split, found[1], found[0])
            to = pl.multiple_of(s * plan.width + part * n, n)
            out[pl.ds(to, n), :] = swap_groups(tiles, plan.width)
        return carry

    lax.fori_loop(0, plan.run, strip, 0)


def place_kernel(plan, owners, places, where):
    z, n, total = lax.axis_index("wide"), plan.group, where.shape[0] // 2

    def place(k, carry):
        at = places[owners[z * plan.slots + jnp.minimum(k, plan.slots - 1)]]
        where[k] = (((at >> 16) ^ z) * plan.run * plan.width) + ((at >> 4) & 4095)
        where[total + k] = ((k - (at & 15)) & (n - 1)) * plan.width
        return carry

    lax.fori_loop(0, total, place, 0)


def first_kernel(plan, log_ref, green, send, own, weighted):
    product(plan, green, jnp.exp(to_column(log_ref[...])), weighted, send, own)


def new_log(plan, log_ref, green, kernel, log_out):
    log_now = to_column(log_ref[...])
    log_now = log_now - 0.5 * jnp.exp(log_now) * contraction(plan, green, kernel)
    to_rows(log_now, log_out)
    return log_now


def middle_kernel(plan, log_ref, green, *refs):
    tiles = refs[: 2 * plan.wide]
    send, own, log_out, weighted, kernel, stack = refs[2 * plan.wide :]
    for k, ref in enumerate(tiles):
        stack[k] = ref[...]
    fill_kernel(
        plan,
        lambda q, slot, at: stack[q * plan.wide + slot, at : at + plan.width, :],
        kernel,
    )
    log_now = new_log(plan, log_ref, green, kernel, log_out)
    product(plan, green, jnp.exp(log_now), weighted, send, own)


def last_kernel(plan, log_ref, green, tiles, where, log_out, residual, kernel):
    core = lax.axis_index("tile")
    half = plan.wide * plan.chunk
    fill_kernel(
        plan,
        lambda q, slot, at: tiles[pl.ds((q * plan.wide + slot) * plan.chunk + at, plan.width), :],
        kernel,
    )
    new_log(plan, log_ref, green, kernel, log_out)
    n, w = plan.group, plan.width
    run = lax.broadcasted_iota(jnp.int32, (w, LANES), 1) // w
    base = [pl.multiple_of((h ^ core) * half, w) for h in range(2)]

    def rows_of(first):
        found = [None, None]
        for m in range(n):
            at = where[first + m]
            shift = where[where.shape[0] // 2 + first + m]
            for h in range(2):
                value = tiles[pl.ds(pl.multiple_of(base[h] + at, w), w), :]
                value = pltpu.roll(value, shift, 1)
                found[h] = value if m == 0 else jnp.where(run == m, value, found[h])
        return [
            swap_groups(found[h][k * n : (k + 1) * n], w) for h in range(2) for k in range(w // n)
        ]

    def batch(i, carry):
        first = pl.multiple_of(i * n, n)
        for k, piece in enumerate(rows_of(first)):
            residual[pl.ds(first, n), k * LANES : (k + 1) * LANES] = piece
        return carry

    whole = plan.slots // n
    lax.fori_loop(0, whole, batch, 0)
    rest = plan.slots - whole * n
    if rest:
        for k, piece in enumerate(rows_of(whole * n)):
            residual[whole * n :, k * LANES : (k + 1) * LANES] = piece[:rest]


def join_kernel(plan, own, recv, *messages):
    c = plan.chunk
    level = jnp.maximum(own[0, c : c + 1, :], recv[0, c : c + 1, :]) + (1.0 - TOP)
    factor = jnp.exp(level * -LN2)
    for k, out in enumerate(messages):
        out[:c, :] = (own[k, :c, :] + recv[k, :c, :]) * factor
        out[c:, :] = jnp.broadcast_to(level, (SUB, LANES))


def sum_kernel(plan, *refs):
    c = plan.chunk
    *messages, out = refs
    levels = [x[c : c + 1, :] for x in messages]
    level = levels[0]
    for x in levels[1:]:
        level = jnp.maximum(level, x)
    level = level + float(math.ceil(math.log2(len(messages))))
    out[:c, :] = sum(x[:c, :] * jnp.exp((at - level) * LN2) for x, at in zip(messages, levels))
    out[c:, :] = jnp.broadcast_to(level, (SUB, LANES))


def tanh_kernel(plan, target, left, right, out):
    c = plan.chunk
    total = sum(x[:c, :] * jnp.exp(x[c : c + 1, :] * LN2) for x in (left, right))
    out[...] = jnp.tanh(total - target[...])


def call(kernel, plan, out_shape, scratch, arguments, specs, out_spec=VMEM):
    def body(*refs):
        kernel(plan, *refs)

    return pl.pallas_call(
        body,
        in_specs=specs,
        out_specs=jax.tree.map(lambda _: out_spec, out_shape),
        out_shape=out_shape,
        scratch_shapes=scratch,
        compiler_params=pltpu.CompilerParams(vmem_limit_bytes=24 * 1024 * 1024),
    )(*arguments)


def exchange(x, axis, mask, size):
    return lax.ppermute(x, axis, [(i, i ^ mask) for i in range(size)])


def to_half(x):
    return lax.reduce_precision(x, exponent_bits=5, mantissa_bits=10)


def bounded_residual(plan, send, own, target):
    recv = exchange(send, "tile", 1, 2)
    sums = [own[k] + recv[k] for k in range(plan.wide)]
    total = sums[0]
    for x in [exchange(sums[k].astype(F16), "wide", k, plan.wide) for k in range(1, plan.wide)]:
        total = total + x.astype(F32)
    mask = 1
    while mask < plan.narrow:
        total = to_half(total)
        total = total + exchange(total.astype(F16), "narrow", mask, plan.narrow).astype(F32)
        mask *= 2
    return jnp.tanh(total - target)


def scaled_residual(plan, send, own, target):
    message = jax.ShapeDtypeStruct((plan.chunk + SUB, LANES), F32)

    def join(*parts):
        return call(sum_kernel, plan, message, [], parts, [VMEM] * len(parts))

    recv = exchange(send, "tile", 1, 2)
    sums = call(join_kernel, plan, (message,) * plan.wide, [], (own, recv), [VMEM] * 2)
    parts = [sums[0]]
    for k in range(1, plan.wide):
        parts.append(exchange(sums[k].astype(F16), "wide", k, plan.wide).astype(F32))
    total = to_half(join(*parts))
    mask = 1
    while mask < plan.narrow:
        other = exchange(total.astype(F16), "narrow", mask, plan.narrow).astype(F32)
        mask *= 2
        if mask < plan.narrow:
            total = to_half(join(total, other))
    return call(
        tanh_kernel, plan, jax.ShapeDtypeStruct(target.shape, F32), [],
        (target, total, other), [VMEM] * 3,
    )


def spread(plan, chunk):
    mine = [chunk] + [exchange(chunk, "wide", k, plan.wide) for k in range(1, plan.wide)]
    return mine + [exchange(x, "tile", 1, 2) for x in mine]


def on_device(mesh, green, log_strength, observed, owner_map):
    plan = Plan(mesh, green, observed, owner_map)
    shape = jax.ShapeDtypeStruct
    log_now = log_strength.reshape(-1, LANES)
    log_shape = shape(log_now.shape, F32)
    plain = shape((plan.wide, plan.chunk, LANES), F32)
    levelled = shape((plan.wide, plan.chunk + SUB, LANES), F32)
    weighted = pltpu.VMEM((2, plan.points, plan.stations), BF16)
    kernel = pltpu.VMEM((2, plan.stations, plan.stations), BF16)

    target = call(
        observed_kernel, plan, shape((plan.chunk, LANES), F32), [],
        (jnp.asarray(plan.strip_table()), observed), [SMEM, VMEM],
    )
    where = call(
        place_kernel, plan, shape((2 * -(-plan.slots // plan.group) * plan.group,), jnp.int32), [],
        (owner_map, jnp.asarray(plan.tile_places())), [SMEM, SMEM], SMEM,
    )
    send, own = call(first_kernel, plan, (plain, plain), [weighted], (log_now, green), [VMEM] * 2)
    residual = bounded_residual(plan, send, own, target)
    for _ in range(STEPS - 1):
        tiles = spread(plan, residual.astype(BF16))
        stack = pltpu.VMEM((2 * plan.wide, plan.chunk, LANES), BF16)
        send, own, log_now = call(
            middle_kernel, plan, (levelled, levelled, log_shape), [weighted, kernel, stack],
            (log_now, green, *tiles), [VMEM] * (2 + len(tiles)),
        )
        residual = scaled_residual(plan, send, own, target)
    tiles = jnp.concatenate(spread(plan, to_half(residual).astype(F16))).astype(F32)
    log_now, owned = call(
        last_kernel, plan, (log_shape, shape((plan.slots, observed.shape[1]), F32)), [kernel],
        (log_now, green, tiles, where), [VMEM, VMEM, VMEM, SMEM],
    )
    return log_now.reshape(-1), owned


def solution(mesh):
    points = P(("grp", "wide", "narrow", "tile"))
    in_specs = (P(("grp", "wide", "narrow", "tile"), None), points, P("grp", None), P("grp"))
    out_specs = (points, P(("grp", "wide"), None))

    def program(green, log_strength, observed, owner_map):
        return on_device(mesh, green, log_strength, observed, owner_map)

    return jax.shard_map(
        program, mesh=mesh, in_specs=in_specs, out_specs=out_specs, check_vma=False
    )
```

```python
import math

import jax
import jax.numpy as jnp
import numpy as np
from jax import lax
from jax.experimental import pallas as pl
from jax.experimental.pallas import tpu as pltpu
from jax.sharding import PartitionSpec as P

STEPS = 2
LANES = 128
WIDE_BLOCK = 256
SUB = 16
TOP = 14.0
LN2 = math.log(2.0)
STRIPS, BATCHES = 17, 4
F32, BF16, F16 = jnp.float32, jnp.bfloat16, jnp.float16
VMEM = pl.BlockSpec(memory_space=pltpu.VMEM)
SMEM = pl.BlockSpec(memory_space=pltpu.SMEM)


class Plan:
    def __init__(self, mesh, green, observed, owner_map):
        self.points, columns = green.shape
        self.stations = columns // 2
        self.area = observed.shape[1] // 2
        self.width = math.isqrt(self.area)
        self.blocks = self.stations // self.width
        self.group = LANES // self.width
        self.wide = mesh.shape["wide"]
        self.narrow = mesh.shape["narrow"]
        self.strips = self.list_strips()
        self.run = -(-len(self.strips) // self.wide)
        self.chunk = self.run * self.width
        self.slots = owner_map.shape[0] // self.wide

    def list_strips(self):
        side, per, w = self.stations // LANES, self.group, self.width
        strips = []
        for i in range(side):
            for j in range(i + 1, side):
                strips += [[(i * per + s, j, 0, LANES, 0)] for s in range(per)]
        for i in range(side):
            for s in range(per // 2):
                strip = [(i * per + s, i, s * w, LANES, 0)]
                if s:
                    strip.append((i * per + per - s, i, 0, s * w, s * w))
                strips.append(strip)
        half = LANES // 2
        for i in range(0, side, 2):
            strip = [(i * per + per // 2, i, half, LANES, 0)]
            if i + 1 < side:
                strip.append(((i + 1) * per + per // 2, i + 1, 0, half, half))
            strips.append(strip)
        return strips

    def tile(self, row, col):
        return row * self.blocks - row * (row - 1) // 2 + col - row

    def strip_table(self):
        table = np.zeros((3, self.run * self.wide), np.int32)
        for k, strip in enumerate(self.strips):
            row, j, first, _, _ = strip[0]
            table[0, k] = self.tile(row, j * self.group)
            if len(strip) > 1:
                row, j, _, last, shift = strip[1]
                table[1, k] = self.tile(row, (j + 1) * self.group - shift // self.width)
                table[2, k] = last // self.width
        return table.reshape(-1)

    def tile_places(self):
        places = np.zeros(self.tile(self.blocks - 1, self.blocks - 1) + 1, np.int32)
        for k, strip in enumerate(self.strips):
            for row, j, first, last, shift in strip:
                for m in range(first // self.width, last // self.width):
                    col = j * self.group + m - shift // self.width + (self.group if shift > m * self.width else 0)
                    at = (k % self.run) * self.width
                    places[self.tile(row, col)] = (k // self.run) * 65536 + at * 16 + m
        return places


def contract(a, b, over_a, over_b):
    return lax.dot_general(a, b, (((over_a,), (over_b,)), ((), ())), preferred_element_type=F32)


def swap_groups(x, width):
    n = LANES // width
    row = lax.broadcasted_iota(jnp.int32, (n, LANES), 0)
    run = lax.broadcasted_iota(jnp.int32, (n, LANES), 1) // width
    d = n // 2
    while d:
        up = pltpu.roll(pltpu.roll(x, n - d, 0), width * d, 1)
        down = up if 2 * d == n else pltpu.roll(pltpu.roll(x, d, 0), LANES - width * d, 1)
        low, high = (row & d) == 0, (run & d) == 0
        x = jnp.where(low == high, x, jnp.where(low, up, down))
        d //= 2
    return x


def unrolled(count, step, body):
    def several(i, carry):
        for k in range(step):
            body(i * step + k)
        return carry

    whole = count // step
    if whole > 1:
        lax.fori_loop(0, whole, several, 0)
    elif whole:
        several(0, 0)
    for i in range(whole * step, count):
        body(i)


def to_column(rows):
    eye = lax.broadcasted_iota(jnp.int32, (LANES, LANES), 0) == lax.broadcasted_iota(
        jnp.int32, (LANES, LANES), 1
    )
    parts = []
    for i in range(rows.shape[0]):
        spread = jnp.broadcast_to(rows[i : i + 1, :], (LANES, LANES))
        parts.append(jnp.sum(jnp.where(eye, spread, 0.0), axis=1, keepdims=True))
    return jnp.concatenate(parts, axis=0)


def to_rows(column, out_ref):
    eye = lax.broadcasted_iota(jnp.int32, (LANES, LANES), 0) == lax.broadcasted_iota(
        jnp.int32, (LANES, LANES), 1
    )
    for i in range(column.shape[0] // LANES):
        spread = jnp.broadcast_to(column[i * LANES : (i + 1) * LANES], (LANES, LANES))
        out_ref[i : i + 1, :] = jnp.sum(jnp.where(eye, spread, 0.0), axis=0, keepdims=True)


def weigh(plan, green, strength, weighted):
    ns = plan.stations
    for h in range(2):
        weighted[h] = (green[:, h * ns : (h + 1) * ns].astype(F32) * strength).astype(BF16)


def product(plan, half, green, weighted, out):
    z = lax.axis_index("wide")
    ns, w = plan.stations, plan.width
    sign = (1 - 2 * half).astype(F32)
    lane = lax.broadcasted_iota(jnp.int32, (w, LANES), 1)
    most = jnp.zeros((w, LANES), F32)
    levelled = out.shape[1] > plan.chunk
    for j in range(ns // WIDE_BLOCK):
        end = WIDE_BLOCK * (j + 1)
        a = green[:, end - WIDE_BLOCK : end]
        b = green[:, ns + end - WIDE_BLOCK : ns + end]
        part = contract(weighted[half, :, :end], a, 0, 0)
        part = part + sign * contract(weighted[1 - half, :, :end], b, 0, 0)
        for k, strip in enumerate(plan.strips):
            if strip[0][1] * LANES // WIDE_BLOCK != j:
                continue
            value = None
            for row, bj, _, last, shift in strip:
                left = bj * LANES % WIDE_BLOCK
                seen = part[row * w : (row + 1) * w, left : left + LANES]
                seen = pltpu.roll(seen, shift, 1) if shift else seen
                value = seen if value is None else jnp.where(lane < last, seen, value)
            at = k % plan.run * w
            out[(k // plan.run) ^ z, at : at + w, :] = value
            if levelled:
                most = jnp.maximum(most, jnp.abs(value))
    for k in range(len(plan.strips), plan.run * plan.wide):
        at = k % plan.run * w
        out[(k // plan.run) ^ z, at : at + w, :] = jnp.zeros((w, LANES), F32)
    if levelled:
        top = jnp.max(jnp.max(most, axis=0, keepdims=True), axis=1, keepdims=True)
        level = jnp.ceil(jnp.log2(jnp.maximum(top, 1e-30)))
        out[:, plan.chunk :, :] = jnp.broadcast_to(level, (plan.wide, SUB, LANES))


def fill_half(plan, load, kernel):
    z = lax.axis_index("wide")
    w = plan.width
    lane = lax.broadcasted_iota(jnp.int32, (w, LANES), 1)
    for k, strip in enumerate(plan.strips):
        value = load((k // plan.run) ^ z, k % plan.run * w)
        for row, bj, first, _, shift in strip:
            seen = value
            if shift:
                seen = pltpu.roll(value.astype(F32), LANES - shift, 1)
            start = first if not shift else LANES - shift
            if start:
                seen = jnp.where(lane >= start, seen.astype(F32), 0.0)
            kernel[row * w : (row + 1) * w, bj * LANES : (bj + 1) * LANES] = seen.astype(BF16)
    for at in range(0, plan.stations, WIDE_BLOCK):
        kernel[at + LANES : at + WIDE_BLOCK, at : at + LANES] = jnp.zeros(
            (WIDE_BLOCK - LANES, LANES), BF16
        )


def contraction(plan, half, green, kernel):
    ns = plan.stations
    near = pl.multiple_of(half * ns, LANES)
    far = pl.multiple_of((1 - half) * ns, LANES)
    sign = (1 - 2 * half).astype(F32)
    total = None
    for j in range(ns // WIDE_BLOCK):
        end = WIDE_BLOCK * (j + 1)
        block = kernel[:end, end - WIDE_BLOCK : end]
        u = contract(green[:, pl.ds(near, end)], block, 1, 0)
        v = contract(green[:, pl.ds(far, end)], block, 1, 0) * sign
        x = green[:, end - WIDE_BLOCK : end].astype(F32)
        y = green[:, ns + end - WIDE_BLOCK : ns + end].astype(F32)
        part = u * x + v * y
        for left in range(0, WIDE_BLOCK, LANES):
            seen = part[:, left : left + LANES]
            total = seen if total is None else total + seen
    return total


def observed_kernel(plan, table, observed, out):
    core, z = lax.axis_index("tile"), lax.axis_index("wide")
    left = pl.multiple_of(core * plan.area, LANES)
    n, count = plan.group, plan.run * plan.wide
    row = lax.broadcasted_iota(jnp.int32, (n, LANES), 0)
    last = observed.shape[0] // n * n - n

    def strip(s):
        k = z * plan.run + s
        split = table[2 * count + k]
        for part in range(plan.area // LANES):
            at = pl.ds(pl.multiple_of(left + part * LANES, LANES), LANES)
            found = []
            for start in (table[k], table[count + k]):
                low = pl.multiple_of(start // n * n, n)
                high = pl.multiple_of(jnp.minimum(low + n, last), n)
                skip = start - low
                tiles = jnp.where(row >= skip, observed[pl.ds(low, n), at], observed[pl.ds(high, n), at])
                found.append(pltpu.roll(tiles, (n - skip) % n, 0))
            tiles = jnp.where(row < split, found[1], found[0])
            to = s * plan.width + part * n
            to = to if isinstance(to, int) else pl.multiple_of(to, n)
            out[pl.ds(to, n), :] = swap_groups(tiles, plan.width)

    unrolled(plan.run, STRIPS, strip)


def first_kernel(plan, log_ref, green, send, weighted):
    weigh(plan, green, jnp.exp(to_column(log_ref[...])), weighted)
    product(plan, 1 - lax.axis_index("tile"), green, weighted, send)


def own_product_kernel(plan, green, weighted, own):
    product(plan, lax.axis_index("tile"), green, weighted, own)


def own_contraction_kernel(plan, green, *refs):
    *tiles, total, kernel, stack = refs
    for k, ref in enumerate(tiles):
        stack[k] = ref[...].astype(BF16)
    fill_half(plan, lambda slot, at: stack[slot, at : at + plan.width, :], kernel)
    total[...] = contraction(plan, lax.axis_index("tile"), green, kernel)


def new_log(plan, log_ref, green, total, kernel, log_out):
    total = total[...] + contraction(plan, 1 - lax.axis_index("tile"), green, kernel)
    log_now = to_column(log_ref[...])
    log_now = log_now - 0.5 * jnp.exp(log_now) * jnp.sum(total, axis=1, keepdims=True)
    to_rows(log_now, log_out)
    return log_now


def middle_kernel(plan, log_ref, green, total, *refs):
    *tiles, send, weighted, log_out, kernel, stack = refs
    for k, ref in enumerate(tiles):
        stack[k] = ref[...]
    fill_half(plan, lambda slot, at: stack[slot, at : at + plan.width, :], kernel)
    log_now = new_log(plan, log_ref, green, total, kernel, log_out)
    weigh(plan, green, jnp.exp(log_now), weighted)
    product(plan, 1 - lax.axis_index("tile"), green, weighted, send)


def last_kernel(plan, log_ref, green, total, mine, others, owners, places, log_out, residual, kernel, tiles):
    core, z = lax.axis_index("tile"), lax.axis_index("wide")
    n, w, c = plan.group, plan.width, plan.chunk
    fill_half(
        plan,
        lambda slot, at: others[pl.ds(pl.multiple_of(slot * c + at, w), w), :],
        kernel,
    )
    new_log(plan, log_ref, green, total, kernel, log_out)
    tiles[core] = mine[...]
    tiles[1 - core] = others[...]
    run = lax.broadcasted_iota(jnp.int32, (w, LANES), 1) // w

    def rows_of(first, count):
        found = [None, None]
        for m in range(count):
            place = places[owners[z * plan.slots + first + m]]
            row = pl.multiple_of(((place >> 16) ^ z) * c + ((place >> 4) & 4095), w)
            shift = ((m - (place & 15)) & (n - 1)) * w
            for h in range(2):
                value = pltpu.roll(tiles[h, pl.ds(row, w), :], shift, 1)
                found[h] = value if m == 0 else jnp.where(run == m, value, found[h])
        return [
            swap_groups(found[h][k * n : (k + 1) * n], w) for h in range(2) for k in range(w // n)
        ]

    def batch(i):
        first = i * n if isinstance(i, int) else pl.multiple_of(i * n, n)
        for k, piece in enumerate(rows_of(first, n)):
            residual[pl.ds(first, n), k * LANES : (k + 1) * LANES] = piece

    whole = plan.slots // n
    unrolled(whole, BATCHES, batch)
    rest = plan.slots - whole * n
    if rest:
        for k, piece in enumerate(rows_of(whole * n, rest)):
            residual[whole * n :, k * LANES : (k + 1) * LANES] = piece[:rest]


def join_kernel(plan, own, recv, *messages):
    c = plan.chunk
    level = jnp.maximum(own[0, c : c + 1, :], recv[0, c : c + 1, :]) + (1.0 - TOP)
    factor = jnp.exp(level * -LN2)
    for k, out in enumerate(messages):
        out[:c, :] = (own[k, :c, :] + recv[k, :c, :]) * factor
        out[c:, :] = jnp.broadcast_to(level, (SUB, LANES))


def sum_kernel(plan, *refs):
    c = plan.chunk
    *messages, out = refs
    levels = [x[c : c + 1, :] for x in messages]
    level = levels[0]
    for x in levels[1:]:
        level = jnp.maximum(level, x)
    level = level + float(math.ceil(math.log2(len(messages))))
    out[:c, :] = sum(x[:c, :] * jnp.exp((at - level) * LN2) for x, at in zip(messages, levels))
    out[c:, :] = jnp.broadcast_to(level, (SUB, LANES))


def tanh_kernel(plan, target, left, right, out):
    c = plan.chunk
    total = sum(x[:c, :] * jnp.exp(x[c : c + 1, :] * LN2) for x in (left, right))
    out[...] = jnp.tanh(total - target[...])


def call(kernel, plan, out_shape, scratch, arguments, specs, out_spec=VMEM):
    def body(*refs):
        kernel(plan, *refs)

    return pl.pallas_call(
        body,
        in_specs=specs,
        out_specs=jax.tree.map(lambda _: out_spec, out_shape),
        out_shape=out_shape,
        scratch_shapes=scratch,
        compiler_params=pltpu.CompilerParams(vmem_limit_bytes=24 * 1024 * 1024),
    )(*arguments)


def exchange(x, axis, mask, size):
    return lax.ppermute(x, axis, [(i, i ^ mask) for i in range(size)])


def to_half(x):
    return lax.reduce_precision(x, exponent_bits=5, mantissa_bits=10)


def bounded_residual(plan, own, recv, target):
    sums = [own[k] + recv[k] for k in range(plan.wide)]
    total = sums[0]
    for x in [exchange(sums[k].astype(F16), "wide", k, plan.wide) for k in range(1, plan.wide)]:
        total = total + x.astype(F32)
    mask = 1
    while mask < plan.narrow:
        total = to_half(total)
        total = total + exchange(total.astype(F16), "narrow", mask, plan.narrow).astype(F32)
        mask *= 2
    return jnp.tanh(total - target)


def scaled_residual(plan, own, recv, target):
    message = jax.ShapeDtypeStruct((plan.chunk + SUB, LANES), F32)

    def join(*parts):
        return call(sum_kernel, plan, message, [], parts, [VMEM] * len(parts))

    sums = call(join_kernel, plan, (message,) * plan.wide, [], (own, recv), [VMEM] * 2)
    parts = [sums[0]]
    for k in range(1, plan.wide):
        parts.append(exchange(sums[k].astype(F16), "wide", k, plan.wide).astype(F32))
    total = to_half(join(*parts))
    mask = 1
    while mask < plan.narrow:
        other = exchange(total.astype(F16), "narrow", mask, plan.narrow).astype(F32)
        mask *= 2
        if mask < plan.narrow:
            total = to_half(join(total, other))
    return call(
        tanh_kernel, plan, jax.ShapeDtypeStruct(target.shape, F32), [],
        (target, total, other), [VMEM] * 3,
    )


def spread(plan, chunk):
    mine = [chunk] + [exchange(chunk, "wide", k, plan.wide) for k in range(1, plan.wide)]
    return mine, [exchange(x, "tile", 1, 2) for x in mine]


def on_device(mesh, green, log_strength, observed, owner_map):
    plan = Plan(mesh, green, observed, owner_map)
    shape = jax.ShapeDtypeStruct
    log_now = log_strength.reshape(-1, LANES)
    log_shape = shape(log_now.shape, F32)
    weighted_shape = shape((2, plan.points, plan.stations), BF16)
    total_shape = shape((plan.points, LANES), F32)
    kernel = pltpu.VMEM((plan.stations, plan.stations), BF16)
    stack = pltpu.VMEM((plan.wide, plan.chunk, LANES), BF16)

    def own_product(weighted, like):
        return call(own_product_kernel, plan, shape(like.shape, F32), [], (green, weighted), [VMEM] * 2)

    def own_contraction(tiles):
        return call(
            own_contraction_kernel, plan, total_shape, [kernel, stack], (green, *tiles),
            [VMEM] * (1 + len(tiles)),
        )

    target = call(
        observed_kernel, plan, shape((plan.chunk, LANES), F32), [],
        (jnp.asarray(plan.strip_table()), observed), [SMEM, VMEM],
    )
    send, weighted = call(
        first_kernel, plan, (shape((plan.wide, plan.chunk, LANES), F32), weighted_shape), [],
        (log_now, green), [VMEM] * 2,
    )
    residual = bounded_residual(
        plan, own_product(weighted, send), exchange(send, "tile", 1, 2), target
    )
    for _ in range(STEPS - 1):
        mine, others = spread(plan, residual.astype(BF16))
        levelled = shape((plan.wide, plan.chunk + SUB, LANES), F32)
        send, weighted, log_now = call(
            middle_kernel, plan, (levelled, weighted_shape, log_shape), [kernel, stack],
            (log_now, green, own_contraction(mine), *others), [VMEM] * (3 + len(others)),
        )
        residual = scaled_residual(
            plan, own_product(weighted, send), exchange(send, "tile", 1, 2), target
        )
    mine, others = spread(plan, to_half(residual).astype(F16))
    mine = [x.astype(F32) for x in mine]
    log_now, owned = call(
        last_kernel, plan, (log_shape, shape((plan.slots, observed.shape[1]), F32)),
        [kernel, pltpu.VMEM((2, plan.wide * plan.chunk, LANES), F32)],
        (
            log_now, green, own_contraction(mine), jnp.concatenate(mine),
            jnp.concatenate(others).astype(F32), owner_map, jnp.asarray(plan.tile_places()),
        ),
        [VMEM] * 5 + [SMEM] * 2,
    )
    return log_now.reshape(-1), owned


def solution(mesh):
    points = P(("grp", "wide", "narrow", "tile"))
    in_specs = (P(("grp", "wide", "narrow", "tile"), None), points, P("grp", None), P("grp"))
    out_specs = (points, P(("grp", "wide"), None))

    def program(green, log_strength, observed, owner_map):
        return on_device(mesh, green, log_strength, observed, owner_map)

    return jax.shard_map(
        program, mesh=mesh, in_specs=in_specs, out_specs=out_specs, check_vma=False
    )
```

```python
import math

import jax
import jax.numpy as jnp
import numpy as np
from jax import lax
from jax.experimental import pallas as pl
from jax.experimental.pallas import tpu as pltpu
from jax.sharding import PartitionSpec as P

STEPS = 2
LANES = 128
WIDE_BLOCK = 256
SUB = 16
TOP = 14.0
LN2 = math.log(2.0)
STRIPS, BATCHES, PIECES = 17, 4, 4
LIMIT = 48
F32, BF16, F16 = jnp.float32, jnp.bfloat16, jnp.float16
VMEM = pl.BlockSpec(memory_space=pltpu.VMEM)
SMEM = pl.BlockSpec(memory_space=pltpu.SMEM)
HBM = pl.BlockSpec(memory_space=pltpu.MemorySpace.HBM)


class Plan:
    def __init__(self, mesh, green, observed, owner_map):
        self.points, columns = green.shape
        self.stations = columns // 2
        self.area = observed.shape[1] // 2
        self.width = math.isqrt(self.area)
        self.blocks = self.stations // self.width
        self.group = LANES // self.width
        self.wide = mesh.shape["wide"]
        self.narrow = mesh.shape["narrow"]
        self.strips = self.list_strips()
        self.run = -(-len(self.strips) // self.wide)
        self.chunk = self.run * self.width
        self.slots = owner_map.shape[0] // self.wide

    def list_strips(self):
        side, per, w = self.stations // LANES, self.group, self.width
        strips = []
        for i in range(side):
            for j in range(i + 1, side):
                strips += [[(i * per + s, j, 0, LANES, 0)] for s in range(per)]
        for i in range(side):
            for s in range(per // 2):
                strip = [(i * per + s, i, s * w, LANES, 0)]
                if s:
                    strip.append((i * per + per - s, i, 0, s * w, s * w))
                strips.append(strip)
        half = LANES // 2
        for i in range(0, side, 2):
            strip = [(i * per + per // 2, i, half, LANES, 0)]
            if i + 1 < side:
                strip.append(((i + 1) * per + per // 2, i + 1, 0, half, half))
            strips.append(strip)
        return strips

    def tile(self, row, col):
        return row * self.blocks - row * (row - 1) // 2 + col - row

    def strip_table(self):
        table = np.zeros((3, self.run * self.wide), np.int32)
        for k, strip in enumerate(self.strips):
            row, j, first, _, _ = strip[0]
            table[0, k] = self.tile(row, j * self.group)
            if len(strip) > 1:
                row, j, _, last, shift = strip[1]
                table[1, k] = self.tile(row, (j + 1) * self.group - shift // self.width)
                table[2, k] = last // self.width
        return table.reshape(-1)

    def tile_places(self):
        places = np.zeros(self.tile(self.blocks - 1, self.blocks - 1) + 1, np.int32)
        for k, strip in enumerate(self.strips):
            for row, j, first, last, shift in strip:
                for m in range(first // self.width, last // self.width):
                    col = j * self.group + m - shift // self.width + (self.group if shift > m * self.width else 0)
                    at = (k % self.run) * self.width
                    places[self.tile(row, col)] = (k // self.run) * 65536 + at * 16 + m
        return places


def contract(a, b, over_a, over_b):
    return lax.dot_general(a, b, (((over_a,), (over_b,)), ((), ())), preferred_element_type=F32)


def lean(x, shift, width):
    return pltpu.roll(x, shift, 1, stride=width, stride_axis=0)


def settle(x, width):
    n = LANES // width
    row = lax.broadcasted_iota(jnp.int32, (n, LANES), 0)
    run = lax.broadcasted_iota(jnp.int32, (n, LANES), 1) // width
    x = jnp.take_along_axis(x, (run + row + 1) & (n - 1), axis=0)
    return lean(x, width, width)


def unrolled(count, step, body):
    def several(i, carry):
        for k in range(step):
            body(i * step + k)
        return carry

    whole = count // step
    if whole > 1:
        lax.fori_loop(0, whole, several, 0)
    elif whole:
        several(0, 0)
    for i in range(whole * step, count):
        body(i)


def row_sums(total):
    parts = []
    for at in range(0, total.shape[0], LANES):
        parts.append(jnp.sum(total[at : at + LANES].T, axis=0, keepdims=True))
    return jnp.concatenate(parts, axis=0)


def weigh_rows(plan, green, strength, weighted, i):
    column = jnp.broadcast_to(strength[i : i + 1, :], (LANES, LANES)).T
    at = slice(i * LANES, (i + 1) * LANES)
    for h in range(2):
        for left in range(0, plan.stations, LANES):
            part = green[at, h * plan.stations + left : h * plan.stations + left + LANES]
            weighted[h, at, left : left + LANES] = (part.astype(F32) * column).astype(BF16)


def product_part(plan, half, green, weighted, j, at=slice(None)):
    ns, end = plan.stations, WIDE_BLOCK * (j + 1)
    sign = (1 - 2 * half).astype(F32)
    a = green[at, end - WIDE_BLOCK : end]
    b = green[at, ns + end - WIDE_BLOCK : ns + end]
    part = contract(weighted[half, at, :end], a, 0, 0)
    return part + sign * contract(weighted[1 - half, at, :end], b, 0, 0)


def pack(plan, j, part, out, most=None):
    z = lax.axis_index("wide")
    w = plan.width
    lane = lax.broadcasted_iota(jnp.int32, (w, LANES), 1)
    for k, strip in enumerate(plan.strips):
        if strip[0][1] * LANES // WIDE_BLOCK != j:
            continue
        value = None
        for row, bj, _, last, shift in strip:
            left = bj * LANES % WIDE_BLOCK
            seen = part[row * w : (row + 1) * w, left : left + LANES]
            seen = pltpu.roll(seen, shift, 1) if shift else seen
            value = seen if value is None else jnp.where(lane < last, seen, value)
        at = k % plan.run * w
        out[(k // plan.run) ^ z, at : at + w, :] = value
        if most is not None:
            most = jnp.maximum(most, jnp.abs(value))
    return most


def pad(plan, out):
    z, w = lax.axis_index("wide"), plan.width
    for k in range(len(plan.strips), plan.run * plan.wide):
        at = k % plan.run * w
        out[(k // plan.run) ^ z, at : at + w, :] = jnp.zeros((w, LANES), F32)


def product(plan, half, green, weighted, out):
    most = jnp.zeros((plan.width, LANES), F32) if out.shape[1] > plan.chunk else None
    for j in range(plan.stations // WIDE_BLOCK):
        most = pack(plan, j, product_part(plan, half, green, weighted, j), out, most)
    pad(plan, out)
    if most is not None:
        top = jnp.max(jnp.max(most, axis=0, keepdims=True), axis=1, keepdims=True)
        level = jnp.ceil(jnp.log2(jnp.maximum(top, 1e-30))) + (1.0 - TOP)
        out[:, plan.chunk :, :] = jnp.broadcast_to(level, (plan.wide, SUB, LANES))


def fill_half(plan, load, kernel):
    z = lax.axis_index("wide")
    w = plan.width
    lane = lax.broadcasted_iota(jnp.int32, (w, LANES), 1)
    for k, strip in enumerate(plan.strips):
        value = load((k // plan.run) ^ z, k % plan.run * w)
        for row, bj, first, _, shift in strip:
            seen = value
            if shift:
                seen = pltpu.roll(value.astype(F32), LANES - shift, 1)
            start = first if not shift else LANES - shift
            if start:
                seen = jnp.where(lane >= start, seen.astype(F32), 0.0)
            kernel[row * w : (row + 1) * w, bj * LANES : (bj + 1) * LANES] = seen.astype(BF16)
    for at in range(0, plan.stations, WIDE_BLOCK):
        kernel[at + LANES : at + WIDE_BLOCK, at : at + LANES] = jnp.zeros(
            (WIDE_BLOCK - LANES, LANES), BF16
        )


def contraction(plan, half, green, kernel):
    ns = plan.stations
    near = pl.multiple_of(half * ns, LANES)
    far = pl.multiple_of((1 - half) * ns, LANES)
    sign = (1 - 2 * half).astype(F32)
    total = None
    for j in range(ns // WIDE_BLOCK):
        end = WIDE_BLOCK * (j + 1)
        block = kernel[:end, end - WIDE_BLOCK : end]
        u = contract(green[:, pl.ds(near, end)], block, 1, 0)
        v = contract(green[:, pl.ds(far, end)], block, 1, 0) * sign
        x = green[:, end - WIDE_BLOCK : end].astype(F32)
        y = green[:, ns + end - WIDE_BLOCK : ns + end].astype(F32)
        part = u * x + v * y
        for left in range(0, WIDE_BLOCK, LANES):
            seen = part[:, left : left + LANES]
            total = seen if total is None else total + seen
    return total


def observed_kernel(plan, table, observed, out):
    core, z = lax.axis_index("tile"), lax.axis_index("wide")
    left = pl.multiple_of(core * plan.area, LANES)
    n, count = plan.group, plan.run * plan.wide
    row = lax.broadcasted_iota(jnp.int32, (n, LANES), 0)
    last = observed.shape[0] // n * n - n

    def strip(s):
        k = z * plan.run + s
        split = table[2 * count + k]
        for part in range(plan.area // LANES):
            at = pl.ds(pl.multiple_of(left + part * LANES, LANES), LANES)
            found = []
            for start in (table[k], table[count + k]):
                low = pl.multiple_of(start // n * n, n)
                high = pl.multiple_of(jnp.minimum(low + n, last), n)
                skip = start - low
                tiles = jnp.where(row >= skip, observed[pl.ds(low, n), at], observed[pl.ds(high, n), at])
                found.append(pltpu.roll(tiles, (n - skip) % n, 0))
            tiles = jnp.where(row < split, found[1], found[0])
            to = s * plan.width + part * n
            to = to if isinstance(to, int) else pl.multiple_of(to, n)
            tiles = settle(lean(tiles, 0, plan.width), plan.width)
            out[pl.ds(to, n), :] = jnp.take_along_axis(tiles, n - 1 - row, axis=0)

    unrolled(plan.run, STRIPS, strip)


def first_kernel(plan, log_hbm, green_hbm, send, weighted, green, log_ref, sums, done):
    pieces = done.shape[0] - 1
    size = plan.points // pieces
    copies = [pltpu.make_async_copy(log_hbm, log_ref, done.at[pieces])]
    for k in range(pieces):
        at = pl.ds(k * size, size)
        copies.append(pltpu.make_async_copy(green_hbm.at[at, :], green.at[at, :], done.at[k]))
    for copy in copies:
        copy.start()
    copies[0].wait()
    strength = jnp.exp(log_ref[...])
    half = 1 - lax.axis_index("tile")
    for k in range(pieces):
        copies[1 + k].wait()
        for i in range(k * size // LANES, (k + 1) * size // LANES):
            weigh_rows(plan, green, strength, weighted, i)
        at = slice(k * size, (k + 1) * size)
        for j in range(plan.stations // WIDE_BLOCK):
            part = product_part(plan, half, green, weighted, j, at)
            part = part if k == 0 else part + sums[j, : part.shape[0], :]
            if k < pieces - 1:
                sums[j, : part.shape[0], :] = part
            else:
                pack(plan, j, part, send)
    pad(plan, send)


def own_product_kernel(plan, green, weighted, own):
    product(plan, lax.axis_index("tile"), green, weighted, own)


def own_contraction_kernel(plan, green, *refs):
    *tiles, total, kernel, stack = refs
    for k, ref in enumerate(tiles):
        stack[k] = ref[...].astype(BF16)
    fill_half(plan, lambda slot, at: stack[slot, at : at + plan.width, :], kernel)
    total[...] = contraction(plan, lax.axis_index("tile"), green, kernel)


def new_log(plan, log_ref, green, total, kernel, log_out):
    total = total[...] + contraction(plan, 1 - lax.axis_index("tile"), green, kernel)
    log_now = log_ref[...]
    log_now = log_now - 0.5 * jnp.exp(log_now) * row_sums(total)
    log_out[...] = log_now
    return log_now


def middle_kernel(plan, log_ref, green, total, *refs):
    *tiles, send, weighted, log_out, kernel, stack = refs
    for k, ref in enumerate(tiles):
        stack[k] = ref[...]
    fill_half(plan, lambda slot, at: stack[slot, at : at + plan.width, :], kernel)
    strength = jnp.exp(new_log(plan, log_ref, green, total, kernel, log_out))
    for i in range(plan.points // LANES):
        weigh_rows(plan, green, strength, weighted, i)
    product(plan, 1 - lax.axis_index("tile"), green, weighted, send)


def last_kernel(plan, log_ref, green, total, mine, others, owners, places, log_out, residual, kernel, tiles):
    core, z = lax.axis_index("tile"), lax.axis_index("wide")
    n, w, c = plan.group, plan.width, plan.chunk
    fill_half(
        plan,
        lambda slot, at: others[pl.ds(pl.multiple_of(slot * c + at, w), w), :],
        kernel,
    )
    new_log(plan, log_ref, green, total, kernel, log_out)
    tiles[core] = mine[...]
    tiles[1 - core] = others[...]
    run = lax.broadcasted_iota(jnp.int32, (w, LANES), 1) // w

    def rows_of(first, count):
        found = [None, None]
        for m in range(count):
            place = places[owners[z * plan.slots + first + m]]
            at = pl.multiple_of(((place >> 16) ^ z) * c + ((place >> 4) & 4095), w)
            shift = ((n - 1 - m - (place & 15)) & (n - 1)) * w
            for h in range(2):
                value = pltpu.roll(tiles[h, pl.ds(at, w), :], shift, 1)
                found[h] = value if m == 0 else jnp.where(run == n - 1 - m, value, found[h])
        parts = [found[h][k * n : (k + 1) * n] for h in range(2) for k in range(w // n)]
        return [settle(lean(x, 0, w), w) for x in parts]

    def batch(i):
        first = i * n if isinstance(i, int) else pl.multiple_of(i * n, n)
        for k, piece in enumerate(rows_of(first, n)):
            residual[pl.ds(first, n), k * LANES : (k + 1) * LANES] = piece

    whole = plan.slots // n
    unrolled(whole, BATCHES, batch)
    rest = plan.slots - whole * n
    if rest:
        for k, piece in enumerate(rows_of(whole * n, rest)):
            residual[whole * n :, k * LANES : (k + 1) * LANES] = piece[:rest]


def scale_kernel(plan, send, out):
    c = plan.chunk
    factor = jnp.exp(send[0, c : c + 1, :] * -LN2)
    for k in range(plan.wide):
        out[k, :c, :] = send[k, :c, :] * factor
        out[k, c:, :] = send[k, c:, :]


def join_kernel(plan, own, recv, *messages):
    c = plan.chunk
    mine, other = own[0, c : c + 1, :], recv[0, c : c + 1, :]
    level = jnp.maximum(mine, other) + 1.0
    factor, wider = jnp.exp(level * -LN2), jnp.exp((other - level) * LN2)
    for k, out in enumerate(messages):
        out[:c, :] = own[k, :c, :] * factor + recv[k, :c, :] * wider
        out[c:, :] = jnp.broadcast_to(level, (SUB, LANES))


def sum_kernel(plan, *refs):
    c = plan.chunk
    *messages, out = refs
    levels = [x[c : c + 1, :] for x in messages]
    level = levels[0]
    for x in levels[1:]:
        level = jnp.maximum(level, x)
    level = level + float(math.ceil(math.log2(len(messages))))
    out[:c, :] = sum(x[:c, :] * jnp.exp((at - level) * LN2) for x, at in zip(messages, levels))
    out[c:, :] = jnp.broadcast_to(level, (SUB, LANES))


def tanh_kernel(plan, target, left, right, out):
    c = plan.chunk
    total = sum(x[:c, :] * jnp.exp(x[c : c + 1, :] * LN2) for x in (left, right))
    out[...] = jnp.tanh(total - target[...])


def call(kernel, plan, out_shape, scratch, arguments, specs, limit=24):
    def body(*refs):
        kernel(plan, *refs)

    return pl.pallas_call(
        body,
        in_specs=specs,
        out_specs=jax.tree.map(lambda _: VMEM, out_shape),
        out_shape=out_shape,
        scratch_shapes=scratch,
        compiler_params=pltpu.CompilerParams(vmem_limit_bytes=limit * 1024 * 1024),
    )(*arguments)


def exchange(x, axis, mask, size):
    return lax.ppermute(x, axis, [(i, i ^ mask) for i in range(size)])


def to_half(x):
    return lax.reduce_precision(x, exponent_bits=5, mantissa_bits=10)


def bounded_residual(plan, own, recv, target):
    sums = [own[k] + recv[k] for k in range(plan.wide)]
    total = sums[0]
    for x in [exchange(sums[k].astype(F16), "wide", k, plan.wide) for k in range(1, plan.wide)]:
        total = total + x.astype(F32)
    mask = 1
    while mask < plan.narrow:
        total = to_half(total)
        total = total + exchange(total.astype(F16), "narrow", mask, plan.narrow).astype(F32)
        mask *= 2
    return jnp.tanh(total - target)


def scaled_residual(plan, own, recv, target):
    message = jax.ShapeDtypeStruct((plan.chunk + SUB, LANES), F32)

    def join(*parts):
        return call(sum_kernel, plan, message, [], parts, [VMEM] * len(parts))

    sums = call(join_kernel, plan, (message,) * plan.wide, [], (own, recv), [VMEM] * 2)
    parts = [sums[0]]
    for k in range(1, plan.wide):
        parts.append(exchange(sums[k].astype(F16), "wide", k, plan.wide).astype(F32))
    total = to_half(join(*parts))
    mask = 1
    while mask < plan.narrow:
        other = exchange(total.astype(F16), "narrow", mask, plan.narrow).astype(F32)
        mask *= 2
        if mask < plan.narrow:
            total = to_half(join(total, other))
    return call(
        tanh_kernel, plan, jax.ShapeDtypeStruct(target.shape, F32), [],
        (target, total, other), [VMEM] * 3,
    )


def spread(plan, chunk):
    mine = [chunk] + [exchange(chunk, "wide", k, plan.wide) for k in range(1, plan.wide)]
    return mine, [exchange(x, "tile", 1, 2) for x in mine]


def on_device(mesh, green, log_strength, observed, owner_map):
    plan = Plan(mesh, green, observed, owner_map)
    shape = jax.ShapeDtypeStruct
    log_now = log_strength.reshape(-1, LANES)
    log_shape = shape(log_now.shape, F32)
    weighted_shape = shape((2, plan.points, plan.stations), BF16)
    total_shape = shape((plan.points, LANES), F32)
    kernel = pltpu.VMEM((plan.stations, plan.stations), BF16)
    stack = pltpu.VMEM((plan.wide, plan.chunk, LANES), BF16)

    def own_product(weighted, like):
        return call(own_product_kernel, plan, shape(like.shape, F32), [], (green, weighted), [VMEM] * 2)

    def own_contraction(tiles):
        return call(
            own_contraction_kernel, plan, total_shape, [kernel, stack], (green, *tiles),
            [VMEM] * (1 + len(tiles)),
        )

    target = call(
        observed_kernel, plan, shape((plan.chunk, LANES), F32), [],
        (jnp.asarray(plan.strip_table()), observed), [SMEM, VMEM],
    )
    columns = plan.stations // WIDE_BLOCK
    send, weighted, green = call(
        first_kernel, plan,
        (shape((plan.wide, plan.chunk, LANES), F32), weighted_shape, shape(green.shape, BF16)),
        [
            pltpu.VMEM(log_now.shape, F32),
            pltpu.VMEM((columns, plan.stations, WIDE_BLOCK), F32),
            pltpu.SemaphoreType.DMA((PIECES + 1,)),
        ],
        (log_now, green), [HBM] * 2, LIMIT,
    )
    recv = exchange(send.astype(F16), "tile", 1, 2).astype(F32)
    residual = bounded_residual(plan, own_product(weighted, send), recv, target)
    for _ in range(STEPS - 1):
        mine, others = spread(plan, residual.astype(BF16))
        levelled = shape((plan.wide, plan.chunk + SUB, LANES), F32)
        send, weighted, log_now = call(
            middle_kernel, plan, (levelled, weighted_shape, log_shape), [kernel, stack],
            (log_now, green, own_contraction(mine), *others), [VMEM] * (3 + len(others)),
        )
        scaled = call(scale_kernel, plan, levelled, [], (send,), [VMEM])
        recv = exchange(scaled.astype(F16), "tile", 1, 2).astype(F32)
        residual = scaled_residual(plan, own_product(weighted, send), recv, target)
    mine, others = spread(plan, to_half(residual).astype(F16))
    mine = [x.astype(F32) for x in mine]
    log_now, owned = call(
        last_kernel, plan, (log_shape, shape((plan.slots, observed.shape[1]), F32)),
        [kernel, pltpu.VMEM((2, plan.wide * plan.chunk, LANES), F32)],
        (
            log_now, green, own_contraction(mine), jnp.concatenate(mine),
            jnp.concatenate(others).astype(F32), owner_map, jnp.asarray(plan.tile_places()),
        ),
        [VMEM] * 5 + [SMEM] * 2,
    )
    return log_now.reshape(-1), owned


def solution(mesh):
    points = P(("grp", "wide", "narrow", "tile"))
    in_specs = (P(("grp", "wide", "narrow", "tile"), None), points, P("grp", None), P("grp"))
    out_specs = (points, P(("grp", "wide"), None))

    def program(green, log_strength, observed, owner_map):
        return on_device(mesh, green, log_strength, observed, owner_map)

    return jax.shard_map(
        program, mesh=mesh, in_specs=in_specs, out_specs=out_specs, check_vma=False
    )
```

```python
import math

import jax
import jax.numpy as jnp
import numpy as np
from jax import lax
from jax.experimental import pallas as pl
from jax.experimental.pallas import tpu as pltpu
from jax.sharding import PartitionSpec as P

STEPS = 2
LANES = 128
WIDE_BLOCK = 256
SUB = 16
TOP = 14.0
LN2 = math.log(2.0)
STRIPS, BATCHES, PIECES = 17, 4, 4
F32, BF16, F16 = jnp.float32, jnp.bfloat16, jnp.float16
VMEM = pl.BlockSpec(memory_space=pltpu.VMEM)
SMEM = pl.BlockSpec(memory_space=pltpu.SMEM)
HBM = pl.BlockSpec(memory_space=pltpu.MemorySpace.HBM)


class Plan:
    def __init__(self, mesh, green, observed, owner_map):
        self.points, columns = green.shape
        self.stations = columns // 2
        self.area = observed.shape[1] // 2
        self.width = math.isqrt(self.area)
        self.blocks = self.stations // self.width
        self.group = LANES // self.width
        self.wide = mesh.shape["wide"]
        self.narrow = mesh.shape["narrow"]
        self.strips = self.list_strips()
        self.run = -(-len(self.strips) // self.wide)
        self.chunk = self.run * self.width
        self.slots = owner_map.shape[0] // self.wide
        self.order = [*range(min(2, self.wide)), *range(self.wide - 1, 1, -1)]

    def list_strips(self):
        side, per, w = self.stations // LANES, self.group, self.width
        strips = []
        for i in range(side):
            for j in range(i + 1, side):
                strips += [[(i * per + s, j, 0, LANES, 0)] for s in range(per)]
        for i in range(side):
            for s in range(per // 2):
                strip = [(i * per + s, i, s * w, LANES, 0)]
                if s:
                    strip.append((i * per + per - s, i, 0, s * w, s * w))
                strips.append(strip)
        half = LANES // 2
        for i in range(0, side, 2):
            strip = [(i * per + per // 2, i, half, LANES, 0)]
            if i + 1 < side:
                strip.append(((i + 1) * per + per // 2, i + 1, 0, half, half))
            strips.append(strip)
        return strips

    def tile(self, row, col):
        return row * self.blocks - row * (row - 1) // 2 + col - row

    def strip_table(self):
        table = np.zeros((3, self.run * self.wide), np.int32)
        for k, strip in enumerate(self.strips):
            row, j, first, _, _ = strip[0]
            table[0, k] = self.tile(row, j * self.group)
            if len(strip) > 1:
                row, j, _, last, shift = strip[1]
                table[1, k] = self.tile(row, (j + 1) * self.group - shift // self.width)
                table[2, k] = last // self.width
        return table.reshape(-1)

    def tile_places(self):
        places = np.zeros(self.tile(self.blocks - 1, self.blocks - 1) + 1, np.int32)
        for k, strip in enumerate(self.strips):
            for row, j, first, last, shift in strip:
                for m in range(first // self.width, last // self.width):
                    col = j * self.group + m - shift // self.width + (self.group if shift > m * self.width else 0)
                    at = (k % self.run) * self.width
                    places[self.tile(row, col)] = (k // self.run) * 65536 + at * 16 + m
        return places


def contract(a, b, over_a, over_b):
    return lax.dot_general(a, b, (((over_a,), (over_b,)), ((), ())), preferred_element_type=F32)


def lean(x, shift, width):
    return pltpu.roll(x, shift, 1, stride=width, stride_axis=0)


def settle(x, width):
    n = LANES // width
    row = lax.broadcasted_iota(jnp.int32, (n, LANES), 0)
    run = lax.broadcasted_iota(jnp.int32, (n, LANES), 1) // width
    x = jnp.take_along_axis(x, (run + row + 1) & (n - 1), axis=0)
    return lean(x, width, width)


def unrolled(count, step, body):
    def several(i, carry):
        for k in range(step):
            body(i * step + k)
        return carry

    whole = count // step
    if whole > 1:
        lax.fori_loop(0, whole, several, 0)
    elif whole:
        several(0, 0)
    for i in range(whole * step, count):
        body(i)


def row_sums(total):
    parts = []
    for at in range(0, total.shape[0], LANES):
        parts.append(jnp.sum(total[at : at + LANES].T, axis=0, keepdims=True))
    return jnp.concatenate(parts, axis=0)


def weigh_rows(plan, green, strength, weighted, i):
    column = jnp.broadcast_to(strength[i : i + 1, :], (LANES, LANES)).T
    at = slice(i * LANES, (i + 1) * LANES)
    for h in range(2):
        for left in range(0, plan.stations, LANES):
            part = green[at, h * plan.stations + left : h * plan.stations + left + LANES]
            weighted[h, at, left : left + LANES] = (part.astype(F32) * column).astype(BF16)


def product_part(plan, half, green, weighted, j):
    ns, end = plan.stations, WIDE_BLOCK * (j + 1)
    sign = (1 - 2 * half).astype(F32)
    a = green[:, end - WIDE_BLOCK : end]
    b = green[:, ns + end - WIDE_BLOCK : ns + end]
    part = contract(weighted[half, :, :end], a, 0, 0)
    return part + sign * contract(weighted[1 - half, :, :end], b, 0, 0)


def pack(plan, j, part, out, most=None):
    z = lax.axis_index("wide")
    w = plan.width
    lane = lax.broadcasted_iota(jnp.int32, (w, LANES), 1)
    for k, strip in enumerate(plan.strips):
        if strip[0][1] * LANES // WIDE_BLOCK != j:
            continue
        value = None
        for row, bj, _, last, shift in strip:
            left = bj * LANES % WIDE_BLOCK
            seen = part[row * w : (row + 1) * w, left : left + LANES]
            seen = pltpu.roll(seen, shift, 1) if shift else seen
            value = seen if value is None else jnp.where(lane < last, seen, value)
        at = k % plan.run * w
        out[(k // plan.run) ^ z, at : at + w, :] = value
        if most is not None:
            most = jnp.maximum(most, jnp.abs(value))
    return most


def pad(plan, out):
    z, w = lax.axis_index("wide"), plan.width
    for k in range(len(plan.strips), plan.run * plan.wide):
        at = k % plan.run * w
        out[(k // plan.run) ^ z, at : at + w, :] = jnp.zeros((w, LANES), F32)


def product(plan, half, green, weighted, out):
    most = jnp.zeros((plan.width, LANES), F32) if out.shape[1] > plan.chunk else None
    for j in range(plan.stations // WIDE_BLOCK):
        most = pack(plan, j, product_part(plan, half, green, weighted, j), out, most)
    pad(plan, out)
    if most is not None:
        top = jnp.max(jnp.max(most, axis=0, keepdims=True), axis=1, keepdims=True)
        level = jnp.ceil(jnp.log2(jnp.maximum(top, 1e-30))) + (1.0 - TOP)
        out[:, plan.chunk :, :] = jnp.broadcast_to(level, (plan.wide, SUB, LANES))


def fill_half(plan, load, kernel):
    z = lax.axis_index("wide")
    w = plan.width
    lane = lax.broadcasted_iota(jnp.int32, (w, LANES), 1)
    for k, strip in enumerate(plan.strips):
        value = load((k // plan.run) ^ z, k % plan.run * w)
        for row, bj, first, _, shift in strip:
            seen = value
            if shift:
                seen = pltpu.roll(value.astype(F32), LANES - shift, 1)
            start = first if not shift else LANES - shift
            if start:
                seen = jnp.where(lane >= start, seen.astype(F32), 0.0)
            kernel[row * w : (row + 1) * w, bj * LANES : (bj + 1) * LANES] = seen.astype(BF16)
    for at in range(0, plan.stations, WIDE_BLOCK):
        kernel[at + LANES : at + WIDE_BLOCK, at : at + LANES] = jnp.zeros(
            (WIDE_BLOCK - LANES, LANES), BF16
        )


def contraction(plan, half, green, kernel):
    ns = plan.stations
    near = pl.multiple_of(half * ns, LANES)
    far = pl.multiple_of((1 - half) * ns, LANES)
    sign = (1 - 2 * half).astype(F32)
    total = None
    for j in range(ns // WIDE_BLOCK):
        end = WIDE_BLOCK * (j + 1)
        block = kernel[:end, end - WIDE_BLOCK : end]
        u = contract(green[:, pl.ds(near, end)], block, 1, 0)
        v = contract(green[:, pl.ds(far, end)], block, 1, 0) * sign
        x = green[:, end - WIDE_BLOCK : end].astype(F32)
        y = green[:, ns + end - WIDE_BLOCK : ns + end].astype(F32)
        part = u * x + v * y
        for left in range(0, WIDE_BLOCK, LANES):
            seen = part[:, left : left + LANES]
            total = seen if total is None else total + seen
    return total


def observed_kernel(plan, table, observed, out):
    core, z = lax.axis_index("tile"), lax.axis_index("wide")
    left = pl.multiple_of(core * plan.area, LANES)
    n, count = plan.group, plan.run * plan.wide
    row = lax.broadcasted_iota(jnp.int32, (n, LANES), 0)
    last = observed.shape[0] // n * n - n

    def strip(s):
        k = z * plan.run + s
        split = table[2 * count + k]
        for part in range(plan.area // LANES):
            at = pl.ds(pl.multiple_of(left + part * LANES, LANES), LANES)
            found = []
            for start in (table[k], table[count + k]):
                low = pl.multiple_of(start // n * n, n)
                high = pl.multiple_of(jnp.minimum(low + n, last), n)
                skip = start - low
                tiles = jnp.where(row >= skip, observed[pl.ds(low, n), at], observed[pl.ds(high, n), at])
                found.append(pltpu.roll(tiles, (n - skip) % n, 0))
            tiles = jnp.where(row < split, found[1], found[0])
            to = s * plan.width + part * n
            to = to if isinstance(to, int) else pl.multiple_of(to, n)
            tiles = settle(lean(tiles, 0, plan.width), plan.width)
            out[pl.ds(to, n), :] = jnp.take_along_axis(tiles, n - 1 - row, axis=0)

    unrolled(plan.run, STRIPS, strip)


def first_kernel(plan, log_hbm, green_hbm, send, weighted, green, log_ref, done):
    pieces = done.shape[0] - 1
    size = plan.points // pieces
    copies = [pltpu.make_async_copy(log_hbm, log_ref, done.at[pieces])]
    for k in range(pieces):
        at = pl.ds(k * size, size)
        copies.append(pltpu.make_async_copy(green_hbm.at[at, :], green.at[at, :], done.at[k]))
    for copy in copies:
        copy.start()
    copies[0].wait()
    strength = jnp.exp(log_ref[...])
    for k in range(pieces):
        copies[1 + k].wait()
        for i in range(k * size // LANES, (k + 1) * size // LANES):
            weigh_rows(plan, green, strength, weighted, i)
    product(plan, 1 - lax.axis_index("tile"), green, weighted, send)


def own_product_kernel(plan, green, weighted, own):
    product(plan, lax.axis_index("tile"), green, weighted, own)


def own_contraction_kernel(plan, green, *refs):
    *tiles, total, kernel, stack = refs
    for k, ref in zip(plan.order, tiles):
        stack[k] = ref[...].astype(BF16)
    fill_half(plan, lambda slot, at: stack[slot, at : at + plan.width, :], kernel)
    total[...] = contraction(plan, lax.axis_index("tile"), green, kernel)


def new_log(plan, log_ref, green, total, kernel, log_out):
    total = total[...] + contraction(plan, 1 - lax.axis_index("tile"), green, kernel)
    log_now = log_ref[...]
    log_now = log_now - 0.5 * jnp.exp(log_now) * row_sums(total)
    log_out[...] = log_now
    return log_now


def middle_kernel(plan, log_ref, green, total, *refs):
    *tiles, send, weighted, log_out, kernel, stack = refs
    for k, ref in zip(plan.order, tiles):
        stack[k] = ref[...]
    fill_half(plan, lambda slot, at: stack[slot, at : at + plan.width, :], kernel)
    strength = jnp.exp(new_log(plan, log_ref, green, total, kernel, log_out))
    for i in range(plan.points // LANES):
        weigh_rows(plan, green, strength, weighted, i)
    product(plan, 1 - lax.axis_index("tile"), green, weighted, send)


def last_kernel(plan, log_ref, green, total, owners, places, *refs):
    *refs, log_out, residual, kernel, tiles = refs
    mine, others = refs[: plan.wide], refs[plan.wide :]
    core, z = lax.axis_index("tile"), lax.axis_index("wide")
    n, w, c = plan.group, plan.width, plan.chunk
    for k, left, right in zip(plan.order, mine, others):
        tiles[core, k * c : (k + 1) * c, :] = left[...]
        tiles[1 - core, k * c : (k + 1) * c, :] = right[...]
    fill_half(
        plan,
        lambda slot, at: tiles[1 - core, pl.ds(pl.multiple_of(slot * c + at, w), w), :],
        kernel,
    )
    new_log(plan, log_ref, green, total, kernel, log_out)
    run = lax.broadcasted_iota(jnp.int32, (w, LANES), 1) // w

    def rows_of(first, count):
        found = [None, None]
        for m in range(count):
            place = places[owners[z * plan.slots + first + m]]
            at = pl.multiple_of(((place >> 16) ^ z) * c + ((place >> 4) & 4095), w)
            shift = ((n - 1 - m - (place & 15)) & (n - 1)) * w
            for h in range(2):
                value = pltpu.roll(tiles[h, pl.ds(at, w), :], shift, 1)
                found[h] = value if m == 0 else jnp.where(run == n - 1 - m, value, found[h])
        parts = [found[h][k * n : (k + 1) * n] for h in range(2) for k in range(w // n)]
        return [settle(lean(x, 0, w), w) for x in parts]

    def batch(i):
        first = i * n if isinstance(i, int) else pl.multiple_of(i * n, n)
        for k, piece in enumerate(rows_of(first, n)):
            residual[pl.ds(first, n), k * LANES : (k + 1) * LANES] = piece

    whole = plan.slots // n
    unrolled(whole, BATCHES, batch)
    rest = plan.slots - whole * n
    if rest:
        for k, piece in enumerate(rows_of(whole * n, rest)):
            residual[whole * n :, k * LANES : (k + 1) * LANES] = piece[:rest]


def scale_kernel(plan, send, out):
    c = plan.chunk
    factor = jnp.exp(send[0, c : c + 1, :] * -LN2)
    for k in range(plan.wide):
        out[k, :c, :] = send[k, :c, :] * factor
        out[k, c:, :] = send[k, c:, :]


def join_kernel(plan, own, recv, *messages):
    c = plan.chunk
    mine, other = own[0, c : c + 1, :], recv[0, c : c + 1, :]
    level = jnp.maximum(mine, other) + 1.0
    factor, wider = jnp.exp(level * -LN2), jnp.exp((other - level) * LN2)
    for k, out in enumerate(messages):
        out[:c, :] = own[k, :c, :] * factor + recv[k, :c, :] * wider
        out[c:, :] = jnp.broadcast_to(level, (SUB, LANES))


def sum_kernel(plan, *refs):
    c = plan.chunk
    *messages, out = refs
    levels = [x[c : c + 1, :] for x in messages]
    level = levels[0]
    for x in levels[1:]:
        level = jnp.maximum(level, x)
    level = level + float(math.ceil(math.log2(len(messages))))
    out[:c, :] = sum(x[:c, :] * jnp.exp((at - level) * LN2) for x, at in zip(messages, levels))
    out[c:, :] = jnp.broadcast_to(level, (SUB, LANES))


def tanh_kernel(plan, target, left, right, out):
    c = plan.chunk
    total = sum(x[:c, :] * jnp.exp(x[c : c + 1, :] * LN2) for x in (left, right))
    out[...] = jnp.tanh(total - target[...])


def call(kernel, plan, out_shape, scratch, arguments, specs):
    def body(*refs):
        kernel(plan, *refs)

    return pl.pallas_call(
        body,
        in_specs=specs,
        out_specs=jax.tree.map(lambda _: VMEM, out_shape),
        out_shape=out_shape,
        scratch_shapes=scratch,
        compiler_params=pltpu.CompilerParams(vmem_limit_bytes=24 * 1024 * 1024),
    )(*arguments)


def exchange(x, axis, mask, size):
    return lax.ppermute(x, axis, [(i, i ^ mask) for i in range(size)])


def to_half(x):
    return lax.reduce_precision(x, exponent_bits=5, mantissa_bits=10)


def bounded_residual(plan, own, recv, target):
    sums = [own[k] + recv[k] for k in range(plan.wide)]
    total = sums[0]
    for x in [exchange(sums[k].astype(F16), "wide", k, plan.wide) for k in range(plan.wide - 1, 0, -1)]:
        total = total + x.astype(F32)
    mask = 1
    while mask < plan.narrow:
        total = to_half(total)
        total = total + exchange(total.astype(F16), "narrow", mask, plan.narrow).astype(F32)
        mask *= 2
    return jnp.tanh(total - target)


def scaled_residual(plan, own, recv, target):
    message = jax.ShapeDtypeStruct((plan.chunk + SUB, LANES), F32)

    def join(*parts):
        return call(sum_kernel, plan, message, [], parts, [VMEM] * len(parts))

    sums = call(join_kernel, plan, (message,) * plan.wide, [], (own, recv), [VMEM] * 2)
    parts = [sums[0]]
    for k in [*range(plan.wide - 1, 2, -1), *range(1, min(3, plan.wide))]:
        parts.append(exchange(sums[k].astype(F16), "wide", k, plan.wide).astype(F32))
    total = to_half(join(*parts))
    mask = 1
    while mask < plan.narrow:
        other = exchange(total.astype(F16), "narrow", mask, plan.narrow).astype(F32)
        mask *= 2
        if mask < plan.narrow:
            total = to_half(join(total, other))
    return call(
        tanh_kernel, plan, jax.ShapeDtypeStruct(target.shape, F32), [],
        (target, total, other), [VMEM] * 3,
    )


def spread(plan, chunk):
    mine = [chunk] + [exchange(chunk, "wide", k, plan.wide) for k in plan.order[1:]]
    return mine, [exchange(x, "tile", 1, 2) for x in mine]


def on_device(mesh, green, log_strength, observed, owner_map):
    plan = Plan(mesh, green, observed, owner_map)
    shape = jax.ShapeDtypeStruct
    log_now = log_strength.reshape(-1, LANES)
    log_shape = shape(log_now.shape, F32)
    weighted_shape = shape((2, plan.points, plan.stations), BF16)
    total_shape = shape((plan.points, LANES), F32)
    kernel = pltpu.VMEM((plan.stations, plan.stations), BF16)
    stack = pltpu.VMEM((plan.wide, plan.chunk, LANES), BF16)

    def own_product(weighted, like):
        return call(own_product_kernel, plan, shape(like.shape, F32), [], (green, weighted), [VMEM] * 2)

    def own_contraction(tiles):
        return call(
            own_contraction_kernel, plan, total_shape, [kernel, stack], (green, *tiles),
            [VMEM] * (1 + len(tiles)),
        )

    target = call(
        observed_kernel, plan, shape((plan.chunk, LANES), F32), [],
        (jnp.asarray(plan.strip_table()), observed), [SMEM, VMEM],
    )
    send, weighted, green = call(
        first_kernel, plan,
        (shape((plan.wide, plan.chunk, LANES), F32), weighted_shape, shape(green.shape, BF16)),
        [
            pltpu.VMEM(log_now.shape, F32),
            pltpu.SemaphoreType.DMA((PIECES + 1,)),
        ],
        [pltpu.with_memory_space_constraint(x, pltpu.MemorySpace.HBM) for x in (log_now, green)],
        [HBM] * 2,
    )
    recv = exchange(send.astype(F16), "tile", 1, 2).astype(F32)
    residual = bounded_residual(plan, own_product(weighted, send), recv, target)
    for _ in range(STEPS - 1):
        mine, others = spread(plan, residual.astype(BF16))
        levelled = shape((plan.wide, plan.chunk + SUB, LANES), F32)
        send, weighted, log_now = call(
            middle_kernel, plan, (levelled, weighted_shape, log_shape), [kernel, stack],
            (log_now, green, own_contraction(mine), *others), [VMEM] * (3 + len(others)),
        )
        scaled = call(scale_kernel, plan, levelled, [], (send,), [VMEM])
        recv = exchange(scaled.astype(F16), "tile", 1, 2).astype(F32)
        residual = scaled_residual(plan, own_product(weighted, send), recv, target)
    mine, others = spread(plan, to_half(residual).astype(F16))
    mine = [x.astype(F32) for x in mine]
    log_now, owned = call(
        last_kernel, plan, (log_shape, shape((plan.slots, observed.shape[1]), F32)),
        [kernel, pltpu.VMEM((2, plan.wide * plan.chunk, LANES), F32)],
        (
            log_now, green, own_contraction(mine), owner_map, jnp.asarray(plan.tile_places()),
            *mine, *[x.astype(F32) for x in others],
        ),
        [VMEM] * 3 + [SMEM] * 2 + [VMEM] * (2 * plan.wide),
    )
    return log_now.reshape(-1), owned


def solution(mesh):
    points = P(("grp", "wide", "narrow", "tile"))
    in_specs = (P(("grp", "wide", "narrow", "tile"), None), points, P("grp", None), P("grp"))
    out_specs = (points, P(("grp", "wide"), None))

    def program(green, log_strength, observed, owner_map):
        return on_device(mesh, green, log_strength, observed, owner_map)

    return jax.shard_map(
        program, mesh=mesh, in_specs=in_specs, out_specs=out_specs, check_vma=False
    )
```

```python
import math

import jax
import jax.numpy as jnp
import numpy as np
from jax import lax
from jax.experimental import pallas as pl
from jax.experimental.pallas import tpu as pltpu
from jax.sharding import PartitionSpec as P

STEPS = 2
LANES = 128
WIDE_BLOCK = 256
SUB = 16
TOP = 14.0
LN2 = math.log(2.0)
STRIPS, PIECES, BLOCK = 17, 4, 256
F32, BF16, F16 = jnp.float32, jnp.bfloat16, jnp.float16
VMEM = pl.BlockSpec(memory_space=pltpu.VMEM)
SMEM = pl.BlockSpec(memory_space=pltpu.SMEM)
HBM = pl.BlockSpec(memory_space=pltpu.MemorySpace.HBM)


def doubling(first, size):
    return [1 << k for k in range(first.bit_length() - 1, (size - 1).bit_length())]


class Plan:
    def __init__(self, mesh, green, observed, owner_map):
        self.points, columns = green.shape
        self.stations = columns // 2
        self.area = observed.shape[1] // 2
        self.width = math.isqrt(self.area)
        self.blocks = self.stations // self.width
        self.group = LANES // self.width
        self.wide = mesh.shape["wide"]
        self.narrow = mesh.shape["narrow"]
        self.ways, self.near, self.far = self.list_masks()
        self.strips = self.list_strips()
        self.run = -(-len(self.strips) // self.ways)
        self.chunk = self.run * self.width
        self.slots = owner_map.shape[0] // self.wide
        self.order = [k for k in (0, 2, 1, 3) if k < self.ways]
        self.sums1 = [k for k in (3, 2, 1) if k < self.ways]
        self.sums2 = [k for k in (2, 1, 3) if k < self.ways]

    def list_masks(self):
        bits = [step for step, size in ((1, self.narrow), (self.narrow, self.wide)) if size > 1]
        near = [0]
        for bit in bits:
            near += [mask ^ bit for mask in near]
        far = [self.narrow * (3 if k == 2 else k) for k in doubling(2, self.wide)]
        return len(near), near, far + doubling(2, self.narrow)

    def corner(self):
        x, z = lax.axis_index("narrow"), lax.axis_index("wide")
        return (x & 1) + ((z ^ (z >> 1)) & 1) * min(2, self.narrow)

    def list_strips(self):
        side, per, w = self.stations // LANES, self.group, self.width
        strips = []
        for i in range(side):
            for j in range(i + 1, side):
                strips += [[(i * per + s, j, 0, LANES, 0)] for s in range(per)]
        for i in range(side):
            for s in range(per // 2):
                strip = [(i * per + s, i, s * w, LANES, 0)]
                if s:
                    strip.append((i * per + per - s, i, 0, s * w, s * w))
                strips.append(strip)
        half = LANES // 2
        for i in range(0, side, 2):
            strip = [(i * per + per // 2, i, half, LANES, 0)]
            if i + 1 < side:
                strip.append(((i + 1) * per + per // 2, i + 1, 0, half, half))
            strips.append(strip)
        return strips

    def tile(self, row, col):
        return row * self.blocks - row * (row - 1) // 2 + col - row

    def strip_table(self):
        table = np.zeros((3, self.run * self.ways), np.int32)
        for k, strip in enumerate(self.strips):
            row, j, first, _, _ = strip[0]
            table[0, k] = self.tile(row, j * self.group)
            if len(strip) > 1:
                row, j, _, last, shift = strip[1]
                table[1, k] = self.tile(row, (j + 1) * self.group - shift // self.width)
                table[2, k] = last // self.width
        return table.reshape(-1)

    def tile_places(self):
        places = np.zeros(self.tile(self.blocks - 1, self.blocks - 1) + 1, np.int32)
        for k, strip in enumerate(self.strips):
            for row, j, first, last, shift in strip:
                for m in range(first // self.width, last // self.width):
                    col = j * self.group + m - shift // self.width + (self.group if shift > m * self.width else 0)
                    at = (k % self.run) * self.width
                    places[self.tile(row, col)] = (k // self.run) * 65536 + at * 16 + m
        return places


def contract(a, b, over_a, over_b):
    return lax.dot_general(a, b, (((over_a,), (over_b,)), ((), ())), preferred_element_type=F32)


def lean(x, shift, width):
    return pltpu.roll(x, shift, 1, stride=width, stride_axis=0)


def settle(x, width):
    n = LANES // width
    row = lax.broadcasted_iota(jnp.int32, (n, LANES), 0)
    run = lax.broadcasted_iota(jnp.int32, (n, LANES), 1) // width
    x = jnp.take_along_axis(x, (run + row + 1) & (n - 1), axis=0)
    return lean(x, width, width)


def unrolled(count, step, body):
    def several(i, carry):
        for k in range(step):
            body(i * step + k)
        return carry

    whole = count // step
    if whole > 1:
        lax.fori_loop(0, whole, several, 0)
    elif whole:
        several(0, 0)
    for i in range(whole * step, count):
        body(i)


def row_sums(total):
    parts = []
    for at in range(0, total.shape[0], LANES):
        parts.append(jnp.sum(total[at : at + LANES].T, axis=0, keepdims=True))
    return jnp.concatenate(parts, axis=0)


def weigh_rows(plan, green, strength, weighted, i):
    column = jnp.broadcast_to(strength[i : i + 1, :], (LANES, LANES)).T
    at = slice(i * LANES, (i + 1) * LANES)
    for h in range(2):
        for left in range(0, plan.stations, LANES):
            part = green[at, h * plan.stations + left : h * plan.stations + left + LANES]
            weighted[h, at, left : left + LANES] = (part.astype(F32) * column).astype(BF16)


def product_part(plan, half, green, weighted, j):
    ns, end = plan.stations, WIDE_BLOCK * (j + 1)
    sign = (1 - 2 * half).astype(F32)
    a = green[:, end - WIDE_BLOCK : end]
    b = green[:, ns + end - WIDE_BLOCK : ns + end]
    part = contract(weighted[half, :, :end], a, 0, 0)
    return part + sign * contract(weighted[1 - half, :, :end], b, 0, 0)


def pack(plan, j, part, out, most=None):
    z = plan.corner()
    w = plan.width
    lane = lax.broadcasted_iota(jnp.int32, (w, LANES), 1)
    for k, strip in enumerate(plan.strips):
        if strip[0][1] * LANES // WIDE_BLOCK != j:
            continue
        value = None
        for row, bj, _, last, shift in strip:
            left = bj * LANES % WIDE_BLOCK
            seen = part[row * w : (row + 1) * w, left : left + LANES]
            seen = pltpu.roll(seen, shift, 1) if shift else seen
            value = seen if value is None else jnp.where(lane < last, seen, value)
        at = k % plan.run * w
        out[(k // plan.run) ^ z, at : at + w, :] = value
        if most is not None:
            most = jnp.maximum(most, jnp.abs(value))
    return most


def pad(plan, out):
    z, w = plan.corner(), plan.width
    for k in range(len(plan.strips), plan.run * plan.ways):
        at = k % plan.run * w
        out[(k // plan.run) ^ z, at : at + w, :] = jnp.zeros((w, LANES), F32)


def product(plan, half, green, weighted, out):
    most = jnp.zeros((plan.width, LANES), F32) if out.shape[1] > plan.chunk else None
    for j in range(plan.stations // WIDE_BLOCK):
        most = pack(plan, j, product_part(plan, half, green, weighted, j), out, most)
    pad(plan, out)
    if most is not None:
        top = jnp.max(jnp.max(most, axis=0, keepdims=True), axis=1, keepdims=True)
        level = jnp.ceil(jnp.log2(jnp.maximum(top, 1e-30))) + (1.0 - TOP)
        out[:, plan.chunk :, :] = jnp.broadcast_to(level, (plan.ways, SUB, LANES))


def fill_half(plan, load, kernel):
    z = plan.corner()
    w = plan.width
    lane = lax.broadcasted_iota(jnp.int32, (w, LANES), 1)
    for k, strip in enumerate(plan.strips):
        value = load((k // plan.run) ^ z, k % plan.run * w)
        for row, bj, first, _, shift in strip:
            seen = value
            if shift:
                seen = pltpu.roll(value.astype(F32), LANES - shift, 1)
            start = first if not shift else LANES - shift
            if start:
                seen = jnp.where(lane >= start, seen.astype(F32), 0.0)
            kernel[row * w : (row + 1) * w, bj * LANES : (bj + 1) * LANES] = seen.astype(BF16)
    for at in range(0, plan.stations, WIDE_BLOCK):
        kernel[at + LANES : at + WIDE_BLOCK, at : at + LANES] = jnp.zeros(
            (WIDE_BLOCK - LANES, LANES), BF16
        )


def contraction(plan, half, green, kernel, at=slice(None)):
    ns = plan.stations
    near = pl.multiple_of(half * ns, LANES)
    far = pl.multiple_of((1 - half) * ns, LANES)
    sign = (1 - 2 * half).astype(F32)
    total = None
    for j in range(ns // WIDE_BLOCK):
        end = WIDE_BLOCK * (j + 1)
        block = kernel[:end, end - WIDE_BLOCK : end]
        u = contract(green[at, pl.ds(near, end)], block, 1, 0)
        v = contract(green[at, pl.ds(far, end)], block, 1, 0) * sign
        x = green[at, end - WIDE_BLOCK : end].astype(F32)
        y = green[at, ns + end - WIDE_BLOCK : ns + end].astype(F32)
        part = u * x + v * y
        for left in range(0, WIDE_BLOCK, LANES):
            seen = part[:, left : left + LANES]
            total = seen if total is None else total + seen
    return total


def observed_kernel(plan, table, observed, out):
    core, z = lax.axis_index("tile"), plan.corner()
    left = pl.multiple_of(core * plan.area, LANES)
    n, count = plan.group, plan.run * plan.ways
    row = lax.broadcasted_iota(jnp.int32, (n, LANES), 0)
    last = observed.shape[0] // n * n - n

    def strip(s):
        k = z * plan.run + s
        split = table[2 * count + k]
        for part in range(plan.area // LANES):
            at = pl.ds(pl.multiple_of(left + part * LANES, LANES), LANES)
            found = []
            for start in (table[k], table[count + k]):
                low = pl.multiple_of(start // n * n, n)
                high = pl.multiple_of(jnp.minimum(low + n, last), n)
                skip = start - low
                tiles = jnp.where(row >= skip, observed[pl.ds(low, n), at], observed[pl.ds(high, n), at])
                found.append(pltpu.roll(tiles, (n - skip) % n, 0))
            tiles = jnp.where(row < split, found[1], found[0])
            to = s * plan.width + part * n
            to = to if isinstance(to, int) else pl.multiple_of(to, n)
            tiles = settle(lean(tiles, 0, plan.width), plan.width)
            out[pl.ds(to, n), :] = jnp.take_along_axis(tiles, n - 1 - row, axis=0)

    unrolled(plan.run, STRIPS, strip)


def first_kernel(plan, log_hbm, green_hbm, send, weighted, green, log_ref, done):
    pieces = done.shape[0] - 1
    size = plan.points // pieces
    copies = [pltpu.make_async_copy(log_hbm, log_ref, done.at[pieces])]
    for k in range(pieces):
        at = pl.ds(k * size, size)
        copies.append(pltpu.make_async_copy(green_hbm.at[at, :], green.at[at, :], done.at[k]))
    for copy in copies:
        copy.start()
    copies[0].wait()
    strength = jnp.exp(log_ref[...])
    for k in range(pieces):
        copies[1 + k].wait()
        for i in range(k * size // LANES, (k + 1) * size // LANES):
            weigh_rows(plan, green, strength, weighted, i)
    product(plan, 1 - lax.axis_index("tile"), green, weighted, send)


def own_product_kernel(plan, green, weighted, own):
    product(plan, lax.axis_index("tile"), green, weighted, own)


def own_contraction_kernel(plan, green, *refs):
    *tiles, total, kernel, stack = refs
    for k, ref in zip(plan.order, tiles):
        stack[k] = ref[...].astype(BF16)
    fill_half(plan, lambda slot, at: stack[slot, at : at + plan.width, :], kernel)
    total[...] = contraction(plan, lax.axis_index("tile"), green, kernel)


def new_log(plan, log_ref, green, total, kernel, log_out):
    total = total[...] + contraction(plan, 1 - lax.axis_index("tile"), green, kernel)
    log_now = log_ref[...]
    log_now = log_now - 0.5 * jnp.exp(log_now) * row_sums(total)
    log_out[...] = log_now
    return log_now


def middle_kernel(plan, log_ref, green, total, *refs):
    *tiles, send, weighted, log_out, kernel, stack = refs
    for k, ref in zip(plan.order, tiles):
        stack[k] = ref[...]
    fill_half(plan, lambda slot, at: stack[slot, at : at + plan.width, :], kernel)
    strength = jnp.exp(new_log(plan, log_ref, green, total, kernel, log_out))
    for i in range(plan.points // LANES):
        weigh_rows(plan, green, strength, weighted, i)
    product(plan, 1 - lax.axis_index("tile"), green, weighted, send)


def last_kernel(plan, log_ref, green, total, owners, places, *refs):
    *refs, log_out, residual, kernel, tiles, sums = refs
    mine, others = refs[: plan.ways], refs[plan.ways :]
    core, z, owned = lax.axis_index("tile"), plan.corner(), lax.axis_index("wide") * plan.slots
    n, w, c = plan.group, plan.width, plan.chunk
    for k, left, right in zip(plan.order, mine, others):
        tiles[core, k * c : (k + 1) * c, :] = left[...]
        tiles[1 - core, k * c : (k + 1) * c, :] = right[...]
    fill_half(
        plan,
        lambda slot, at: tiles[1 - core, pl.ds(pl.multiple_of(slot * c + at, w), w), :],
        kernel,
    )
    run = lax.broadcasted_iota(jnp.int32, (w, LANES), 1) // w

    def rows_of(first, count):
        found = [None, None]
        for m in range(count):
            place = places[owners[owned + first + m]]
            at = pl.multiple_of(((place >> 16) ^ z) * c + ((place >> 4) & 4095), w)
            shift = ((n - 1 - m - (place & 15)) & (n - 1)) * w
            for h in range(2):
                value = pltpu.roll(tiles[h, pl.ds(at, w), :], shift, 1)
                found[h] = value if m == 0 else jnp.where(run == n - 1 - m, value, found[h])
        parts = [found[h][k * n : (k + 1) * n] for h in range(2) for k in range(w // n)]
        return [settle(lean(x, 0, w), w) for x in parts]

    def batch(i):
        first = i * n if isinstance(i, int) else pl.multiple_of(i * n, n)
        for k, piece in enumerate(rows_of(first, n)):
            residual[pl.ds(first, n), k * LANES : (k + 1) * LANES] = piece

    whole = plan.slots // n
    steps = plan.points // BLOCK
    batches, rows = whole // steps, BLOCK // LANES

    def step(p, carry):
        at = pl.ds(pl.multiple_of(p * BLOCK, BLOCK), BLOCK)
        part = row_sums(total[at, :] + contraction(plan, 1 - core, green, kernel, at))
        for i in range(rows):
            sums[pl.ds(p * rows + i, 1), :] = part[i : i + 1, :]
        for k in range(batches):
            batch(p * batches + k)
        return carry

    lax.fori_loop(0, steps, step, 0)
    for i in range(batches * steps, whole):
        batch(i)
    log_now = log_ref[...]
    log_out[...] = log_now - 0.5 * jnp.exp(log_now) * sums[...]
    rest = plan.slots - whole * n
    if rest:
        for k, piece in enumerate(rows_of(whole * n, rest)):
            residual[whole * n :, k * LANES : (k + 1) * LANES] = piece[:rest]


def scale_kernel(plan, send, out):
    c = plan.chunk
    factor = jnp.exp(send[0, c : c + 1, :] * -LN2)
    for k in range(plan.ways):
        out[k, :c, :] = send[k, :c, :] * factor
        out[k, c:, :] = send[k, c:, :]


def join_kernel(plan, own, recv, *messages):
    c = plan.chunk
    mine, other = own[0, c : c + 1, :], recv[0, c : c + 1, :]
    level = jnp.maximum(mine, other) + 1.0
    factor, wider = jnp.exp(level * -LN2), jnp.exp((other - level) * LN2)
    for k, out in enumerate(messages):
        out[:c, :] = own[k, :c, :] * factor + recv[k, :c, :] * wider
        out[c:, :] = jnp.broadcast_to(level, (SUB, LANES))


def sum_kernel(plan, *refs):
    c = plan.chunk
    *messages, out = refs
    levels = [x[c : c + 1, :] for x in messages]
    level = levels[0]
    for x in levels[1:]:
        level = jnp.maximum(level, x)
    level = level + float(math.ceil(math.log2(len(messages))))
    out[:c, :] = sum(x[:c, :] * jnp.exp((at - level) * LN2) for x, at in zip(messages, levels))
    out[c:, :] = jnp.broadcast_to(level, (SUB, LANES))


def tanh_kernel(plan, target, *refs):
    *parts, out = refs
    c = plan.chunk
    total = sum(x[:c, :] * jnp.exp(x[c : c + 1, :] * LN2) for x in parts)
    out[...] = jnp.tanh(total - target[...])


def call(kernel, plan, out_shape, scratch, arguments, specs):
    def body(*refs):
        kernel(plan, *refs)

    return pl.pallas_call(
        body,
        in_specs=specs,
        out_specs=jax.tree.map(lambda _: VMEM, out_shape),
        out_shape=out_shape,
        scratch_shapes=scratch,
        compiler_params=pltpu.CompilerParams(vmem_limit_bytes=24 * 1024 * 1024),
    )(*arguments)


def swap_cores(x):
    return lax.ppermute(x, "tile", [(0, 1), (1, 0)])


def exchange(plan, x, mask):
    pairs = [(i, i ^ mask) for i in range(plan.wide * plan.narrow)]
    return lax.ppermute(x, ("wide", "narrow"), pairs)


def to_half(x):
    return lax.reduce_precision(x, exponent_bits=5, mantissa_bits=10)


def bounded_residual(plan, own, recv, target):
    sums = [own[k] + recv[k] for k in range(plan.ways)]
    total = sums[0]
    for x in [exchange(plan, sums[k].astype(F16), plan.near[k]) for k in plan.sums1]:
        total = total + x.astype(F32)
    for mask in plan.far:
        total = to_half(total)
        total = total + exchange(plan, total.astype(F16), mask).astype(F32)
    return jnp.tanh(total - target)


def scaled_residual(plan, own, recv, target):
    message = jax.ShapeDtypeStruct((plan.chunk + SUB, LANES), F32)

    def join(*parts):
        return call(sum_kernel, plan, message, [], parts, [VMEM] * len(parts))

    sums = call(join_kernel, plan, (message,) * plan.ways, [], (own, recv), [VMEM] * 2)
    parts = [sums[0]]
    for k in plan.sums2:
        parts.append(exchange(plan, sums[k].astype(F16), plan.near[k]).astype(F32))
    parts = [join(*parts)]
    for mask in plan.far:
        total = to_half(join(*parts) if len(parts) > 1 else parts[0])
        parts = [total, exchange(plan, total.astype(F16), mask).astype(F32)]
    return call(
        tanh_kernel, plan, jax.ShapeDtypeStruct(target.shape, F32), [],
        (target, *parts), [VMEM] * (1 + len(parts)),
    )


def spread(plan, chunk):
    mine = [chunk] + [exchange(plan, chunk, plan.near[k]) for k in plan.order[1:]]
    return mine, [swap_cores(x) for x in mine]


def on_device(mesh, green, log_strength, observed, owner_map):
    plan = Plan(mesh, green, observed, owner_map)
    shape = jax.ShapeDtypeStruct
    log_now = log_strength.reshape(-1, LANES)
    log_shape = shape(log_now.shape, F32)
    weighted_shape = shape((2, plan.points, plan.stations), BF16)
    total_shape = shape((plan.points, LANES), F32)
    kernel = pltpu.VMEM((plan.stations, plan.stations), BF16)
    stack = pltpu.VMEM((plan.ways, plan.chunk, LANES), BF16)

    def own_product(weighted, like):
        return call(own_product_kernel, plan, shape(like.shape, F32), [], (green, weighted), [VMEM] * 2)

    def own_contraction(tiles):
        return call(
            own_contraction_kernel, plan, total_shape, [kernel, stack], (green, *tiles),
            [VMEM] * (1 + len(tiles)),
        )

    target = call(
        observed_kernel, plan, shape((plan.chunk, LANES), F32), [],
        (jnp.asarray(plan.strip_table()), observed), [SMEM, VMEM],
    )
    send, weighted, green = call(
        first_kernel, plan,
        (shape((plan.ways, plan.chunk, LANES), F32), weighted_shape, shape(green.shape, BF16)),
        [
            pltpu.VMEM(log_now.shape, F32),
            pltpu.SemaphoreType.DMA((PIECES + 1,)),
        ],
        [pltpu.with_memory_space_constraint(x, pltpu.MemorySpace.HBM) for x in (log_now, green)],
        [HBM] * 2,
    )
    recv = swap_cores(send.astype(F16)).astype(F32)
    residual = bounded_residual(plan, own_product(weighted, send), recv, target)
    for _ in range(STEPS - 1):
        mine, others = spread(plan, residual.astype(BF16))
        levelled = shape((plan.ways, plan.chunk + SUB, LANES), F32)
        send, weighted, log_now = call(
            middle_kernel, plan, (levelled, weighted_shape, log_shape), [kernel, stack],
            (log_now, green, own_contraction(mine), *others), [VMEM] * (3 + len(others)),
        )
        scaled = call(scale_kernel, plan, levelled, [], (send,), [VMEM])
        recv = swap_cores(scaled.astype(F16)).astype(F32)
        residual = scaled_residual(plan, own_product(weighted, send), recv, target)
    mine, others = spread(plan, to_half(residual).astype(F16))
    mine = [x.astype(F32) for x in mine]
    log_now, owned = call(
        last_kernel, plan, (log_shape, shape((plan.slots, observed.shape[1]), F32)),
        [
            kernel, pltpu.VMEM((2, plan.ways * plan.chunk, LANES), F32),
            pltpu.VMEM(log_now.shape, F32),
        ],
        (
            log_now, green, own_contraction(mine), owner_map, jnp.asarray(plan.tile_places()),
            *mine, *[x.astype(F32) for x in others],
        ),
        [VMEM] * 3 + [SMEM] * 2 + [VMEM] * (2 * plan.ways),
    )
    return log_now.reshape(-1), owned


def solution(mesh):
    points = P(("grp", "wide", "narrow", "tile"))
    in_specs = (P(("grp", "wide", "narrow", "tile"), None), points, P("grp", None), P("grp"))
    out_specs = (points, P(("grp", "wide"), None))

    def program(green, log_strength, observed, owner_map):
        return on_device(mesh, green, log_strength, observed, owner_map)

    return jax.shard_map(
        program, mesh=mesh, in_specs=in_specs, out_specs=out_specs, check_vma=False
    )
```

```python
import math

import jax
import jax.numpy as jnp
import numpy as np
from jax import lax
from jax.experimental import pallas as pl
from jax.experimental.pallas import tpu as pltpu
from jax.sharding import PartitionSpec as P

STEPS = 2
LANES = 128
WIDE_BLOCK = 256
SUB = 16
TOP = 14.0
LN2 = math.log(2.0)
STRIPS, PIECES, BLOCK = 17, 4, 256
F32, BF16, F16 = jnp.float32, jnp.bfloat16, jnp.float16
VMEM = pl.BlockSpec(memory_space=pltpu.VMEM)
SMEM = pl.BlockSpec(memory_space=pltpu.SMEM)
HBM = pl.BlockSpec(memory_space=pltpu.MemorySpace.HBM)


def doubling(first, size):
    return [1 << k for k in range(first.bit_length() - 1, (size - 1).bit_length())]


class Plan:
    def __init__(self, mesh, green, observed, owner_map):
        self.points, columns = green.shape
        self.stations = columns // 2
        self.area = observed.shape[1] // 2
        self.width = math.isqrt(self.area)
        self.blocks = self.stations // self.width
        self.group = LANES // self.width
        self.wide = mesh.shape["wide"]
        self.narrow = mesh.shape["narrow"]
        self.ways, self.near, self.far = self.list_masks()
        self.strips = self.list_strips()
        self.run = -(-len(self.strips) // self.ways)
        self.chunk = self.run * self.width
        self.slots = owner_map.shape[0] // self.wide
        self.order = [k for k in (0, 2, 1, 3) if k < self.ways]
        self.sums1 = [k for k in (3, 2, 1) if k < self.ways]
        self.sums2 = [k for k in (2, 1, 3) if k < self.ways]

    def list_masks(self):
        bits = [step for step, size in ((1, self.narrow), (self.narrow, self.wide)) if size > 1]
        near = [0]
        for bit in bits:
            near += [mask ^ bit for mask in near]
        far = [self.narrow * (3 if k == 2 else k) for k in doubling(2, self.wide)]
        return len(near), near, far + doubling(2, self.narrow)

    def corner(self):
        x, z = lax.axis_index("narrow"), lax.axis_index("wide")
        return (x & 1) + ((z ^ (z >> 1)) & 1) * min(2, self.narrow)

    def half(self):
        x, z = lax.axis_index("narrow"), lax.axis_index("wide")
        return lax.axis_index("tile") ^ ((x ^ z ^ (z >> 1)) & 1)

    def list_strips(self):
        side, per, w = self.stations // LANES, self.group, self.width
        strips = []
        for i in range(side):
            for j in range(i + 1, side):
                strips += [[(i * per + s, j, 0, LANES, 0)] for s in range(per)]
        for i in range(side):
            for s in range(per // 2):
                strip = [(i * per + s, i, s * w, LANES, 0)]
                if s:
                    strip.append((i * per + per - s, i, 0, s * w, s * w))
                strips.append(strip)
        half = LANES // 2
        for i in range(0, side, 2):
            strip = [(i * per + per // 2, i, half, LANES, 0)]
            if i + 1 < side:
                strip.append(((i + 1) * per + per // 2, i + 1, 0, half, half))
            strips.append(strip)
        return strips

    def tile(self, row, col):
        return row * self.blocks - row * (row - 1) // 2 + col - row

    def strip_table(self):
        table = np.zeros((3, self.run * self.ways), np.int32)
        for k, strip in enumerate(self.strips):
            row, j, first, _, _ = strip[0]
            table[0, k] = self.tile(row, j * self.group)
            if len(strip) > 1:
                row, j, _, last, shift = strip[1]
                table[1, k] = self.tile(row, (j + 1) * self.group - shift // self.width)
                table[2, k] = last // self.width
        return table.reshape(-1)

    def tile_places(self):
        places = np.zeros(self.tile(self.blocks - 1, self.blocks - 1) + 1, np.int32)
        for k, strip in enumerate(self.strips):
            for row, j, first, last, shift in strip:
                for m in range(first // self.width, last // self.width):
                    col = j * self.group + m - shift // self.width + (self.group if shift > m * self.width else 0)
                    at = (k % self.run) * self.width
                    places[self.tile(row, col)] = (k // self.run) * 65536 + at * 16 + m
        return places


def contract(a, b, over_a, over_b):
    return lax.dot_general(a, b, (((over_a,), (over_b,)), ((), ())), preferred_element_type=F32)


def lean(x, shift, width):
    return pltpu.roll(x, shift, 1, stride=width, stride_axis=0)


def settle(x, width):
    n = LANES // width
    row = lax.broadcasted_iota(jnp.int32, (n, LANES), 0)
    run = lax.broadcasted_iota(jnp.int32, (n, LANES), 1) // width
    x = jnp.take_along_axis(x, (run + row + 1) & (n - 1), axis=0)
    return lean(x, width, width)


def unrolled(count, step, body):
    def several(i, carry):
        for k in range(step):
            body(i * step + k)
        return carry

    whole = count // step
    if whole > 1:
        lax.fori_loop(0, whole, several, 0)
    elif whole:
        several(0, 0)
    for i in range(whole * step, count):
        body(i)


def row_sums(total):
    parts = []
    for at in range(0, total.shape[0], LANES):
        parts.append(jnp.sum(total[at : at + LANES].T, axis=0, keepdims=True))
    return jnp.concatenate(parts, axis=0)


def weigh_rows(plan, green, strength, weighted, i):
    column = jnp.broadcast_to(strength[i : i + 1, :], (LANES, LANES)).T
    at = slice(i * LANES, (i + 1) * LANES)
    for h in range(2):
        for left in range(0, plan.stations, LANES):
            part = green[at, h * plan.stations + left : h * plan.stations + left + LANES]
            weighted[h, at, left : left + LANES] = (part.astype(F32) * column).astype(BF16)


def product_part(plan, half, green, weighted, j):
    ns, end = plan.stations, WIDE_BLOCK * (j + 1)
    sign = (1 - 2 * half).astype(F32)
    a = green[:, end - WIDE_BLOCK : end]
    b = green[:, ns + end - WIDE_BLOCK : ns + end]
    part = contract(weighted[half, :, :end], a, 0, 0)
    return part + sign * contract(weighted[1 - half, :, :end], b, 0, 0)


def pack(plan, j, part, out, most=None):
    z = plan.corner()
    w = plan.width
    lane = lax.broadcasted_iota(jnp.int32, (w, LANES), 1)
    for k, strip in enumerate(plan.strips):
        if strip[0][1] * LANES // WIDE_BLOCK != j:
            continue
        value = None
        for row, bj, _, last, shift in strip:
            left = bj * LANES % WIDE_BLOCK
            seen = part[row * w : (row + 1) * w, left : left + LANES]
            seen = pltpu.roll(seen, shift, 1) if shift else seen
            value = seen if value is None else jnp.where(lane < last, seen, value)
        at = k % plan.run * w
        out[(k // plan.run) ^ z, at : at + w, :] = value
        if most is not None:
            most = jnp.maximum(most, jnp.abs(value))
    return most


def pad(plan, out):
    z, w = plan.corner(), plan.width
    for k in range(len(plan.strips), plan.run * plan.ways):
        at = k % plan.run * w
        out[(k // plan.run) ^ z, at : at + w, :] = jnp.zeros((w, LANES), F32)


def product(plan, half, green, weighted, out):
    most = jnp.zeros((plan.width, LANES), F32) if out.shape[1] > plan.chunk else None
    for j in range(plan.stations // WIDE_BLOCK):
        most = pack(plan, j, product_part(plan, half, green, weighted, j), out, most)
    pad(plan, out)
    if most is not None:
        top = jnp.max(jnp.max(most, axis=0, keepdims=True), axis=1, keepdims=True)
        level = jnp.ceil(jnp.log2(jnp.maximum(top, 1e-30))) + (1.0 - TOP)
        out[:, plan.chunk :, :] = jnp.broadcast_to(level, (plan.ways, SUB, LANES))


def fill_half(plan, load, kernel):
    z = plan.corner()
    w = plan.width
    lane = lax.broadcasted_iota(jnp.int32, (w, LANES), 1)
    for k, strip in enumerate(plan.strips):
        value = load((k // plan.run) ^ z, k % plan.run * w)
        for row, bj, first, _, shift in strip:
            seen = value
            if shift:
                seen = pltpu.roll(value.astype(F32), LANES - shift, 1)
            start = first if not shift else LANES - shift
            if start:
                seen = jnp.where(lane >= start, seen.astype(F32), 0.0)
            kernel[row * w : (row + 1) * w, bj * LANES : (bj + 1) * LANES] = seen.astype(BF16)
    for at in range(0, plan.stations, WIDE_BLOCK):
        kernel[at + LANES : at + WIDE_BLOCK, at : at + LANES] = jnp.zeros(
            (WIDE_BLOCK - LANES, LANES), BF16
        )


def contraction(plan, half, green, kernel, at=slice(None)):
    ns = plan.stations
    near = pl.multiple_of(half * ns, LANES)
    far = pl.multiple_of((1 - half) * ns, LANES)
    sign = (1 - 2 * half).astype(F32)
    total = None
    for j in range(ns // WIDE_BLOCK):
        end = WIDE_BLOCK * (j + 1)
        block = kernel[:end, end - WIDE_BLOCK : end]
        u = contract(green[at, pl.ds(near, end)], block, 1, 0)
        v = contract(green[at, pl.ds(far, end)], block, 1, 0) * sign
        x = green[at, end - WIDE_BLOCK : end].astype(F32)
        y = green[at, ns + end - WIDE_BLOCK : ns + end].astype(F32)
        part = u * x + v * y
        for left in range(0, WIDE_BLOCK, LANES):
            seen = part[:, left : left + LANES]
            total = seen if total is None else total + seen
    return total


def observed_kernel(plan, table, observed, owners, places, out, owners_out, places_out, done):
    copies = [
        pltpu.make_async_copy(owners, owners_out, done.at[0]),
        pltpu.make_async_copy(places, places_out, done.at[1]),
    ]
    for copy in copies:
        copy.start()
    z = plan.corner()
    left = pl.multiple_of(plan.half() * plan.area, LANES)
    n, count = plan.group, plan.run * plan.ways
    row = lax.broadcasted_iota(jnp.int32, (n, LANES), 0)
    last = observed.shape[0] // n * n - n

    def strip(s):
        k = z * plan.run + s
        split = table[2 * count + k]
        for part in range(plan.area // LANES):
            at = pl.ds(pl.multiple_of(left + part * LANES, LANES), LANES)
            found = []
            for start in (table[k], table[count + k]):
                low = pl.multiple_of(start // n * n, n)
                high = pl.multiple_of(jnp.minimum(low + n, last), n)
                skip = start - low
                tiles = jnp.where(row >= skip, observed[pl.ds(low, n), at], observed[pl.ds(high, n), at])
                found.append(pltpu.roll(tiles, (n - skip) % n, 0))
            tiles = jnp.where(row < split, found[1], found[0])
            to = s * plan.width + part * n
            to = to if isinstance(to, int) else pl.multiple_of(to, n)
            tiles = settle(lean(tiles, 0, plan.width), plan.width)
            out[pl.ds(to, n), :] = jnp.take_along_axis(tiles, n - 1 - row, axis=0)

    unrolled(plan.run, STRIPS, strip)
    for copy in copies:
        copy.wait()


def first_kernel(plan, log_hbm, green_hbm, send, weighted, green, log_ref, done):
    pieces = done.shape[0] - 1
    size = plan.points // pieces
    copies = [pltpu.make_async_copy(log_hbm, log_ref, done.at[pieces])]
    for k in range(pieces):
        at = pl.ds(k * size, size)
        copies.append(pltpu.make_async_copy(green_hbm.at[at, :], green.at[at, :], done.at[k]))
    for copy in copies:
        copy.start()
    copies[0].wait()
    strength = jnp.exp(log_ref[...])
    for k in range(pieces):
        copies[1 + k].wait()
        for i in range(k * size // LANES, (k + 1) * size // LANES):
            weigh_rows(plan, green, strength, weighted, i)
    product(plan, 1 - plan.half(), green, weighted, send)


def own_product_kernel(plan, green, weighted, own):
    product(plan, plan.half(), green, weighted, own)


def own_contraction_kernel(plan, green, *refs):
    *tiles, total, kernel, stack = refs
    for k, ref in zip(plan.order, tiles):
        stack[k] = ref[...].astype(BF16)
    fill_half(plan, lambda slot, at: stack[slot, at : at + plan.width, :], kernel)
    total[...] = contraction(plan, plan.half(), green, kernel)


def new_log(plan, log_ref, green, total, kernel, log_out):
    total = total[...] + contraction(plan, 1 - plan.half(), green, kernel)
    log_now = log_ref[...]
    log_now = log_now - 0.5 * jnp.exp(log_now) * row_sums(total)
    log_out[...] = log_now
    return log_now


def middle_kernel(plan, log_ref, green, total, *refs):
    *tiles, send, weighted, log_out, kernel, stack = refs
    for k, ref in zip(plan.order, tiles):
        stack[k] = ref[...]
    fill_half(plan, lambda slot, at: stack[slot, at : at + plan.width, :], kernel)
    strength = jnp.exp(new_log(plan, log_ref, green, total, kernel, log_out))
    for i in range(plan.points // LANES):
        weigh_rows(plan, green, strength, weighted, i)
    product(plan, 1 - plan.half(), green, weighted, send)


def last_kernel(plan, log_ref, green, total, owners, places, *refs):
    *refs, log_out, residual, kernel, tiles, sums = refs
    mine, others = refs[: plan.ways], refs[plan.ways :]
    half, z, owned = plan.half(), plan.corner(), lax.axis_index("wide") * plan.slots
    n, w, c = plan.group, plan.width, plan.chunk
    for k, left, right in zip(plan.order, mine, others):
        tiles[half, k * c : (k + 1) * c, :] = left[...]
        tiles[1 - half, k * c : (k + 1) * c, :] = right[...]
    fill_half(
        plan,
        lambda slot, at: tiles[1 - half, pl.ds(pl.multiple_of(slot * c + at, w), w), :],
        kernel,
    )
    run = lax.broadcasted_iota(jnp.int32, (w, LANES), 1) // w

    def rows_of(first, count):
        found = [None, None]
        for m in range(count):
            place = places[owners[owned + first + m]]
            at = pl.multiple_of(((place >> 16) ^ z) * c + ((place >> 4) & 4095), w)
            shift = ((n - 1 - m - (place & 15)) & (n - 1)) * w
            for h in range(2):
                value = pltpu.roll(tiles[h, pl.ds(at, w), :], shift, 1)
                found[h] = value if m == 0 else jnp.where(run == n - 1 - m, value, found[h])
        parts = [found[h][k * n : (k + 1) * n] for h in range(2) for k in range(w // n)]
        return [settle(lean(x, 0, w), w) for x in parts]

    def batch(i):
        first = i * n if isinstance(i, int) else pl.multiple_of(i * n, n)
        for k, piece in enumerate(rows_of(first, n)):
            residual[pl.ds(first, n), k * LANES : (k + 1) * LANES] = piece

    whole = plan.slots // n
    steps = plan.points // BLOCK
    batches, rows = whole // steps, BLOCK // LANES

    def step(p, carry):
        at = pl.ds(pl.multiple_of(p * BLOCK, BLOCK), BLOCK)
        part = row_sums(total[at, :] + contraction(plan, 1 - half, green, kernel, at))
        for i in range(rows):
            sums[pl.ds(p * rows + i, 1), :] = part[i : i + 1, :]
        for k in range(batches):
            batch(p * batches + k)
        return carry

    lax.fori_loop(0, steps, step, 0)
    for i in range(batches * steps, whole):
        batch(i)
    log_now = log_ref[...]
    log_out[...] = log_now - 0.5 * jnp.exp(log_now) * sums[...]
    rest = plan.slots - whole * n
    if rest:
        for k, piece in enumerate(rows_of(whole * n, rest)):
            residual[whole * n :, k * LANES : (k + 1) * LANES] = piece[:rest]


def scale_kernel(plan, send, out):
    c = plan.chunk
    factor = jnp.exp(send[0, c : c + 1, :] * -LN2)
    for k in range(plan.ways):
        out[k, :c, :] = send[k, :c, :] * factor
        out[k, c:, :] = send[k, c:, :]


def join_kernel(plan, own, recv, *messages):
    c = plan.chunk
    mine, other = own[0, c : c + 1, :], recv[0, c : c + 1, :]
    level = jnp.maximum(mine, other) + 1.0
    factor, wider = jnp.exp(level * -LN2), jnp.exp((other - level) * LN2)
    for k, out in enumerate(messages):
        out[:c, :] = own[k, :c, :] * factor + recv[k, :c, :] * wider
        out[c:, :] = jnp.broadcast_to(level, (SUB, LANES))


def sum_kernel(plan, *refs):
    c = plan.chunk
    *messages, out = refs
    levels = [x[c : c + 1, :] for x in messages]
    level = levels[0]
    for x in levels[1:]:
        level = jnp.maximum(level, x)
    level = level + float(math.ceil(math.log2(len(messages))))
    out[:c, :] = sum(x[:c, :] * jnp.exp((at - level) * LN2) for x, at in zip(messages, levels))
    out[c:, :] = jnp.broadcast_to(level, (SUB, LANES))


def tanh_kernel(plan, target, *refs):
    *parts, out = refs
    c = plan.chunk
    total = sum(x[:c, :] * jnp.exp(x[c : c + 1, :] * LN2) for x in parts)
    out[...] = jnp.tanh(total - target[...])


def call(kernel, plan, out_shape, scratch, arguments, specs, out_specs=None):
    def body(*refs):
        kernel(plan, *refs)

    return pl.pallas_call(
        body,
        in_specs=specs,
        out_specs=out_specs or jax.tree.map(lambda _: VMEM, out_shape),
        out_shape=out_shape,
        scratch_shapes=scratch,
        compiler_params=pltpu.CompilerParams(vmem_limit_bytes=24 * 1024 * 1024),
    )(*arguments)


def swap_cores(x):
    return lax.ppermute(x, "tile", [(0, 1), (1, 0)])


def exchange(plan, x, mask):
    dz, dx = divmod(mask, plan.narrow)
    mask = 2 * mask + ((dx ^ dz ^ (dz >> 1)) & 1)
    pairs = [(i, i ^ mask) for i in range(2 * plan.wide * plan.narrow)]
    return lax.ppermute(x, ("wide", "narrow", "tile"), pairs)


def to_half(x):
    return lax.reduce_precision(x, exponent_bits=5, mantissa_bits=10)


def bounded_residual(plan, own, recv, target):
    sums = [own[k] + recv[k] for k in range(plan.ways)]
    total = sums[0]
    for x in [exchange(plan, sums[k].astype(F16), plan.near[k]) for k in plan.sums1]:
        total = total + x.astype(F32)
    for mask in plan.far:
        total = to_half(total)
        total = total + exchange(plan, total.astype(F16), mask).astype(F32)
    return jnp.tanh(total - target)


def scaled_residual(plan, own, recv, target):
    message = jax.ShapeDtypeStruct((plan.chunk + SUB, LANES), F32)

    def join(*parts):
        return call(sum_kernel, plan, message, [], parts, [VMEM] * len(parts))

    sums = call(join_kernel, plan, (message,) * plan.ways, [], (own, recv), [VMEM] * 2)
    parts = [sums[0]]
    for k in plan.sums2:
        parts.append(exchange(plan, sums[k].astype(F16), plan.near[k]).astype(F32))
    parts = [join(*parts)]
    for mask in plan.far:
        total = to_half(join(*parts) if len(parts) > 1 else parts[0])
        parts = [total, exchange(plan, total.astype(F16), mask).astype(F32)]
    return call(
        tanh_kernel, plan, jax.ShapeDtypeStruct(target.shape, F32), [],
        (target, *parts), [VMEM] * (1 + len(parts)),
    )


def spread(plan, chunk):
    mine = [chunk] + [exchange(plan, chunk, plan.near[k]) for k in plan.order[1:]]
    return mine, [swap_cores(x) for x in mine]


def on_device(mesh, green, log_strength, observed, owner_map):
    plan = Plan(mesh, green, observed, owner_map)
    shape = jax.ShapeDtypeStruct
    log_now = log_strength.reshape(-1, LANES)
    log_shape = shape(log_now.shape, F32)
    weighted_shape = shape((2, plan.points, plan.stations), BF16)
    total_shape = shape((plan.points, LANES), F32)
    kernel = pltpu.VMEM((plan.stations, plan.stations), BF16)
    stack = pltpu.VMEM((plan.ways, plan.chunk, LANES), BF16)

    def own_product(weighted, like):
        return call(own_product_kernel, plan, shape(like.shape, F32), [], (green, weighted), [VMEM] * 2)

    def own_contraction(tiles):
        return call(
            own_contraction_kernel, plan, total_shape, [kernel, stack], (green, *tiles),
            [VMEM] * (1 + len(tiles)),
        )

    places = jnp.asarray(plan.tile_places())
    tables = [pltpu.SMEM(x.shape, jnp.int32) for x in (owner_map, places)]
    target, *tables = call(
        observed_kernel, plan, (shape((plan.chunk, LANES), F32), *tables),
        [pltpu.SemaphoreType.DMA((2,))],
        (jnp.asarray(plan.strip_table()), observed, owner_map, places), [SMEM, VMEM, HBM, HBM],
        (VMEM, SMEM, SMEM),
    )
    send, weighted, green = call(
        first_kernel, plan,
        (shape((plan.ways, plan.chunk, LANES), F32), weighted_shape, shape(green.shape, BF16)),
        [
            pltpu.VMEM(log_now.shape, F32),
            pltpu.SemaphoreType.DMA((PIECES + 1,)),
        ],
        [pltpu.with_memory_space_constraint(x, pltpu.MemorySpace.HBM) for x in (log_now, green)],
        [HBM] * 2,
    )
    recv = swap_cores(send.astype(F16)).astype(F32)
    residual = bounded_residual(plan, own_product(weighted, send), recv, target)
    for _ in range(STEPS - 1):
        mine, others = spread(plan, residual.astype(BF16))
        levelled = shape((plan.ways, plan.chunk + SUB, LANES), F32)
        send, weighted, log_now = call(
            middle_kernel, plan, (levelled, weighted_shape, log_shape), [kernel, stack],
            (log_now, green, own_contraction(mine), *others), [VMEM] * (3 + len(others)),
        )
        scaled = call(scale_kernel, plan, levelled, [], (send,), [VMEM])
        recv = swap_cores(scaled.astype(F16)).astype(F32)
        residual = scaled_residual(plan, own_product(weighted, send), recv, target)
    mine, others = spread(plan, to_half(residual).astype(F16))
    mine = [x.astype(F32) for x in mine]
    log_now, owned = call(
        last_kernel, plan, (log_shape, shape((plan.slots, observed.shape[1]), F32)),
        [
            kernel, pltpu.VMEM((2, plan.ways * plan.chunk, LANES), F32),
            pltpu.VMEM(log_now.shape, F32),
        ],
        (
            log_now, green, own_contraction(mine), *tables,
            *mine, *[x.astype(F32) for x in others],
        ),
        [VMEM] * 3 + [SMEM] * 2 + [VMEM] * (2 * plan.ways),
    )
    return log_now.reshape(-1), owned


def solution(mesh):
    points = P(("grp", "wide", "narrow", "tile"))
    in_specs = (P(("grp", "wide", "narrow", "tile"), None), points, P("grp", None), P("grp"))
    out_specs = (points, P(("grp", "wide"), None))

    def program(green, log_strength, observed, owner_map):
        return on_device(mesh, green, log_strength, observed, owner_map)

    return jax.shard_map(
        program, mesh=mesh, in_specs=in_specs, out_specs=out_specs, check_vma=False
    )
```

```python
import math

import jax
import jax.numpy as jnp
import numpy as np
from jax import lax
from jax.experimental import pallas as pl
from jax.experimental.pallas import tpu as pltpu
from jax.sharding import PartitionSpec as P

STEPS = 2
LANES = 128
WIDE_BLOCK = 256
SUB = 8
TOP = 14.0
LN2 = math.log(2.0)
STRIPS, PIECES, BLOCK = 17, 4, 256
F32, BF16, F16 = jnp.float32, jnp.bfloat16, jnp.float16
VMEM = pl.BlockSpec(memory_space=pltpu.VMEM)
SMEM = pl.BlockSpec(memory_space=pltpu.SMEM)
HBM = pl.BlockSpec(memory_space=pltpu.MemorySpace.HBM)


def doubling(first, size):
    return [1 << k for k in range(first.bit_length() - 1, (size - 1).bit_length())]


class Plan:
    def __init__(self, mesh, green, observed, owner_map):
        self.points, columns = green.shape
        self.stations = columns // 2
        self.area = observed.shape[1] // 2
        self.width = math.isqrt(self.area)
        self.blocks = self.stations // self.width
        self.group = LANES // self.width
        self.wide = mesh.shape["wide"]
        self.narrow = mesh.shape["narrow"]
        self.ways, self.near, self.far = self.list_masks()
        self.strips = self.list_strips()
        self.run = -(-len(self.strips) // self.ways)
        self.chunk = self.run * self.width
        self.slots = owner_map.shape[0] // self.wide
        self.order = [k for k in (0, 2, 1, 3) if k < self.ways]
        self.sums1 = [k for k in (3, 2, 1) if k < self.ways]
        self.sums2 = [k for k in (2, 1, 3) if k < self.ways]

    def list_masks(self):
        bits = [step for step, size in ((1, self.narrow), (self.narrow, self.wide)) if size > 1]
        near = [0]
        for bit in bits:
            near += [mask ^ bit for mask in near]
        far = [self.narrow * (3 if k == 2 else k) for k in doubling(2, self.wide)]
        return len(near), near, far + doubling(2, self.narrow)

    def corner(self):
        x, z = lax.axis_index("narrow"), lax.axis_index("wide")
        return (x & 1) + ((z ^ (z >> 1)) & 1) * min(2, self.narrow)

    def half(self):
        x, z = lax.axis_index("narrow"), lax.axis_index("wide")
        return lax.axis_index("tile") ^ ((x ^ z) & 1)

    def list_strips(self):
        side, per, w = self.stations // LANES, self.group, self.width
        strips = []
        for i in range(side):
            for j in range(i + 1, side):
                strips += [[(i * per + s, j, 0, LANES, 0)] for s in range(per)]
        for i in range(side):
            for s in range(per // 2):
                strip = [(i * per + s, i, s * w, LANES, 0)]
                if s:
                    strip.append((i * per + per - s, i, 0, s * w, s * w))
                strips.append(strip)
        half = LANES // 2
        for i in range(0, side, 2):
            strip = [(i * per + per // 2, i, half, LANES, 0)]
            if i + 1 < side:
                strip.append(((i + 1) * per + per // 2, i + 1, 0, half, half))
            strips.append(strip)
        return strips

    def tile(self, row, col):
        return row * self.blocks - row * (row - 1) // 2 + col - row

    def strip_table(self):
        table = np.zeros((3, self.run * self.ways), np.int32)
        for k, strip in enumerate(self.strips):
            row, j, first, _, _ = strip[0]
            table[0, k] = self.tile(row, j * self.group)
            if len(strip) > 1:
                row, j, _, last, shift = strip[1]
                table[1, k] = self.tile(row, (j + 1) * self.group - shift // self.width)
                table[2, k] = last // self.width
        return table.reshape(-1)

    def tile_places(self):
        places = np.zeros(self.tile(self.blocks - 1, self.blocks - 1) + 1, np.int32)
        for k, strip in enumerate(self.strips):
            for row, j, first, last, shift in strip:
                for m in range(first // self.width, last // self.width):
                    col = j * self.group + m - shift // self.width + (self.group if shift > m * self.width else 0)
                    at = (k % self.run) * self.width
                    places[self.tile(row, col)] = (k // self.run) * 65536 + at * 16 + m
        return places


def contract(a, b, over_a, over_b):
    return lax.dot_general(a, b, (((over_a,), (over_b,)), ((), ())), preferred_element_type=F32)


def lean(x, shift, width):
    return pltpu.roll(x, shift, 1, stride=width, stride_axis=0)


def settle(x, width):
    n = LANES // width
    row = lax.broadcasted_iota(jnp.int32, (n, LANES), 0)
    run = lax.broadcasted_iota(jnp.int32, (n, LANES), 1) // width
    x = jnp.take_along_axis(x, (run + row + 1) & (n - 1), axis=0)
    return lean(x, width, width)


def unrolled(count, step, body):
    def several(i, carry):
        for k in range(step):
            body(i * step + k)
        return carry

    whole = count // step
    if whole > 1:
        lax.fori_loop(0, whole, several, 0)
    elif whole:
        several(0, 0)
    for i in range(whole * step, count):
        body(i)


def row_sums(total):
    parts = []
    for at in range(0, total.shape[0], LANES):
        parts.append(jnp.sum(total[at : at + LANES].T, axis=0, keepdims=True))
    return jnp.concatenate(parts, axis=0)


def weigh_rows(plan, green, strength, weighted, i):
    column = jnp.broadcast_to(strength[i : i + 1, :], (LANES, LANES)).T
    at = slice(i * LANES, (i + 1) * LANES)
    for h in range(2):
        for left in range(0, plan.stations, LANES):
            part = green[at, h * plan.stations + left : h * plan.stations + left + LANES]
            weighted[h, at, left : left + LANES] = (part.astype(F32) * column).astype(BF16)


def product_part(plan, half, green, weighted, j):
    ns, end = plan.stations, WIDE_BLOCK * (j + 1)
    sign = (1 - 2 * half).astype(F32)
    a = green[:, end - WIDE_BLOCK : end]
    b = green[:, ns + end - WIDE_BLOCK : ns + end]
    part = contract(weighted[half, :, :end], a, 0, 0)
    return part + sign * contract(weighted[1 - half, :, :end], b, 0, 0)


def pack(plan, j, part, out, most=None):
    z = plan.corner()
    w = plan.width
    lane = lax.broadcasted_iota(jnp.int32, (w, LANES), 1)
    for k, strip in enumerate(plan.strips):
        if strip[0][1] * LANES // WIDE_BLOCK != j:
            continue
        value = None
        for row, bj, _, last, shift in strip:
            left = bj * LANES % WIDE_BLOCK
            seen = part[row * w : (row + 1) * w, left : left + LANES]
            seen = pltpu.roll(seen, shift, 1) if shift else seen
            value = seen if value is None else jnp.where(lane < last, seen, value)
        at = k % plan.run * w
        out[(k // plan.run) ^ z, at : at + w, :] = value
        if most is not None:
            most = jnp.maximum(most, jnp.abs(value))
    return most


def pad(plan, out):
    z, w = plan.corner(), plan.width
    for k in range(len(plan.strips), plan.run * plan.ways):
        at = k % plan.run * w
        out[(k // plan.run) ^ z, at : at + w, :] = jnp.zeros((w, LANES), F32)


def product(plan, half, green, weighted, out):
    most = jnp.zeros((plan.width, LANES), F32) if out.shape[1] > plan.chunk else None
    for j in range(plan.stations // WIDE_BLOCK):
        most = pack(plan, j, product_part(plan, half, green, weighted, j), out, most)
    pad(plan, out)
    if most is not None:
        top = jnp.max(jnp.max(most, axis=0, keepdims=True), axis=1, keepdims=True)
        level = jnp.ceil(jnp.log2(jnp.maximum(top, 1e-30))) + (1.0 - TOP)
        out[:, plan.chunk :, :] = jnp.broadcast_to(level, (plan.ways, SUB, LANES))


def fill_half(plan, load, kernel):
    z = plan.corner()
    w = plan.width
    lane = lax.broadcasted_iota(jnp.int32, (w, LANES), 1)
    for k, strip in enumerate(plan.strips):
        value = load((k // plan.run) ^ z, k % plan.run * w)
        for row, bj, first, _, shift in strip:
            seen = value
            if shift:
                seen = pltpu.roll(value.astype(F32), LANES - shift, 1)
            start = first if not shift else LANES - shift
            if start:
                seen = jnp.where(lane >= start, seen.astype(F32), 0.0)
            kernel[row * w : (row + 1) * w, bj * LANES : (bj + 1) * LANES] = seen.astype(BF16)
    for at in range(0, plan.stations, WIDE_BLOCK):
        kernel[at + LANES : at + WIDE_BLOCK, at : at + LANES] = jnp.zeros(
            (WIDE_BLOCK - LANES, LANES), BF16
        )


def contraction(plan, half, green, kernel, at=slice(None)):
    ns = plan.stations
    near = pl.multiple_of(half * ns, LANES)
    far = pl.multiple_of((1 - half) * ns, LANES)
    sign = (1 - 2 * half).astype(F32)
    total = None
    for j in range(ns // WIDE_BLOCK):
        end = WIDE_BLOCK * (j + 1)
        block = kernel[:end, end - WIDE_BLOCK : end]
        u = contract(green[at, pl.ds(near, end)], block, 1, 0)
        v = contract(green[at, pl.ds(far, end)], block, 1, 0) * sign
        x = green[at, end - WIDE_BLOCK : end].astype(F32)
        y = green[at, ns + end - WIDE_BLOCK : ns + end].astype(F32)
        part = u * x + v * y
        for left in range(0, WIDE_BLOCK, LANES):
            seen = part[:, left : left + LANES]
            total = seen if total is None else total + seen
    return total


def observed_kernel(plan, table, observed, owners, places, out, owners_out, places_out, done):
    copies = [
        pltpu.make_async_copy(owners, owners_out, done.at[0]),
        pltpu.make_async_copy(places, places_out, done.at[1]),
    ]
    for copy in copies:
        copy.start()
    z = plan.corner()
    left = pl.multiple_of(plan.half() * plan.area, LANES)
    n, count = plan.group, plan.run * plan.ways
    row = lax.broadcasted_iota(jnp.int32, (n, LANES), 0)
    last = observed.shape[0] // n * n - n

    def strip(s):
        k = z * plan.run + s
        split = table[2 * count + k]
        for part in range(plan.area // LANES):
            at = pl.ds(pl.multiple_of(left + part * LANES, LANES), LANES)
            found = []
            for start in (table[k], table[count + k]):
                low = pl.multiple_of(start // n * n, n)
                high = pl.multiple_of(jnp.minimum(low + n, last), n)
                skip = start - low
                tiles = jnp.where(row >= skip, observed[pl.ds(low, n), at], observed[pl.ds(high, n), at])
                found.append(pltpu.roll(tiles, (n - skip) % n, 0))
            tiles = jnp.where(row < split, found[1], found[0])
            to = s * plan.width + part * n
            to = to if isinstance(to, int) else pl.multiple_of(to, n)
            tiles = settle(lean(tiles, 0, plan.width), plan.width)
            out[pl.ds(to, n), :] = jnp.take_along_axis(tiles, n - 1 - row, axis=0)

    unrolled(plan.run, STRIPS, strip)
    for copy in copies:
        copy.wait()


def first_kernel(plan, log_hbm, green_hbm, send, weighted, green, log_ref, done):
    pieces = done.shape[0] - 1
    size = plan.points // pieces
    copies = [pltpu.make_async_copy(log_hbm, log_ref, done.at[pieces])]
    for k in range(pieces):
        at = pl.ds(k * size, size)
        copies.append(pltpu.make_async_copy(green_hbm.at[at, :], green.at[at, :], done.at[k]))
    for copy in copies:
        copy.start()
    copies[0].wait()
    strength = jnp.exp(log_ref[...])
    for k in range(pieces):
        copies[1 + k].wait()
        for i in range(k * size // LANES, (k + 1) * size // LANES):
            weigh_rows(plan, green, strength, weighted, i)
    product(plan, 1 - plan.half(), green, weighted, send)


def own_product_kernel(plan, green, weighted, own):
    product(plan, plan.half(), green, weighted, own)


def own_contraction_kernel(plan, green, *refs):
    *tiles, total, kernel, stack = refs
    for k, ref in zip(plan.order, tiles):
        stack[k] = ref[...].astype(BF16)
    fill_half(plan, lambda slot, at: stack[slot, at : at + plan.width, :], kernel)
    total[...] = contraction(plan, plan.half(), green, kernel)


def new_log(plan, log_ref, green, total, kernel, log_out):
    total = total[...] + contraction(plan, 1 - plan.half(), green, kernel)
    log_now = log_ref[...]
    log_now = log_now - 0.5 * jnp.exp(log_now) * row_sums(total)
    log_out[...] = log_now
    return log_now


def middle_kernel(plan, log_ref, green, total, *refs):
    *tiles, send, weighted, log_out, kernel, stack = refs
    for k, ref in zip(plan.order, tiles):
        stack[k] = ref[...]
    fill_half(plan, lambda slot, at: stack[slot, at : at + plan.width, :], kernel)
    strength = jnp.exp(new_log(plan, log_ref, green, total, kernel, log_out))
    for i in range(plan.points // LANES):
        weigh_rows(plan, green, strength, weighted, i)
    product(plan, 1 - plan.half(), green, weighted, send)


def last_kernel(plan, log_ref, green, total, owners, places, *refs):
    *refs, log_out, residual, kernel, tiles, sums = refs
    mine, others = refs[: plan.ways], refs[plan.ways :]
    half, z, owned = plan.half(), plan.corner(), lax.axis_index("wide") * plan.slots
    n, w, c = plan.group, plan.width, plan.chunk
    for k, left, right in zip(plan.order, mine, others):
        tiles[half, k * c : (k + 1) * c, :] = left[...]
        tiles[1 - half, k * c : (k + 1) * c, :] = right[...]
    fill_half(
        plan,
        lambda slot, at: tiles[1 - half, pl.ds(pl.multiple_of(slot * c + at, w), w), :],
        kernel,
    )
    run = lax.broadcasted_iota(jnp.int32, (w, LANES), 1) // w

    def rows_of(first, count):
        found = [None, None]
        for m in range(count):
            place = places[owners[owned + first + m]]
            at = pl.multiple_of(((place >> 16) ^ z) * c + ((place >> 4) & 4095), w)
            shift = ((n - 1 - m - (place & 15)) & (n - 1)) * w
            for h in range(2):
                value = pltpu.roll(tiles[h, pl.ds(at, w), :], shift, 1)
                found[h] = value if m == 0 else jnp.where(run == n - 1 - m, value, found[h])
        parts = [found[h][k * n : (k + 1) * n] for h in range(2) for k in range(w // n)]
        return [settle(lean(x, 0, w), w) for x in parts]

    def batch(i):
        first = i * n if isinstance(i, int) else pl.multiple_of(i * n, n)
        for k, piece in enumerate(rows_of(first, n)):
            residual[pl.ds(first, n), k * LANES : (k + 1) * LANES] = piece

    whole = plan.slots // n
    steps = plan.points // BLOCK
    batches, rows = whole // steps, BLOCK // LANES

    def step(p, carry):
        at = pl.ds(pl.multiple_of(p * BLOCK, BLOCK), BLOCK)
        part = row_sums(total[at, :] + contraction(plan, 1 - half, green, kernel, at))
        for i in range(rows):
            sums[pl.ds(p * rows + i, 1), :] = part[i : i + 1, :]
        for k in range(batches):
            batch(p * batches + k)
        return carry

    lax.fori_loop(0, steps, step, 0)
    for i in range(batches * steps, whole):
        batch(i)
    log_now = log_ref[...]
    log_out[...] = log_now - 0.5 * jnp.exp(log_now) * sums[...]
    rest = plan.slots - whole * n
    if rest:
        for k, piece in enumerate(rows_of(whole * n, rest)):
            residual[whole * n :, k * LANES : (k + 1) * LANES] = piece[:rest]


def scale_kernel(plan, send, out):
    c = plan.chunk
    factor = jnp.exp(send[0, c : c + 1, :] * -LN2)
    for k in range(plan.ways):
        out[k, :c, :] = send[k, :c, :] * factor
        out[k, c:, :] = send[k, c:, :]


def join_kernel(plan, own, recv, *messages):
    c = plan.chunk
    mine, other = own[0, c : c + 1, :], recv[0, c : c + 1, :]
    level = jnp.maximum(mine, other) + 1.0
    factor, wider = jnp.exp(level * -LN2), jnp.exp((other - level) * LN2)
    for k, out in enumerate(messages):
        out[:c, :] = own[k, :c, :] * factor + recv[k, :c, :] * wider
        out[c:, :] = jnp.broadcast_to(level, (SUB, LANES))


def sum_kernel(plan, *refs):
    c = plan.chunk
    *messages, out = refs
    levels = [x[c : c + 1, :] for x in messages]
    level = levels[0]
    for x in levels[1:]:
        level = jnp.maximum(level, x)
    level = level + float(math.ceil(math.log2(len(messages))))
    out[:c, :] = sum(x[:c, :] * jnp.exp((at - level) * LN2) for x, at in zip(messages, levels))
    out[c:, :] = jnp.broadcast_to(level, (SUB, LANES))


def tanh_kernel(plan, target, *refs):
    *parts, out = refs
    c = plan.chunk
    total = sum(x[:c, :] * jnp.exp(x[c : c + 1, :] * LN2) for x in parts)
    out[...] = jnp.tanh(total - target[...])


def call(kernel, plan, out_shape, scratch, arguments, specs, out_specs=None):
    def body(*refs):
        kernel(plan, *refs)

    return pl.pallas_call(
        body,
        in_specs=specs,
        out_specs=out_specs or jax.tree.map(lambda _: VMEM, out_shape),
        out_shape=out_shape,
        scratch_shapes=scratch,
        compiler_params=pltpu.CompilerParams(vmem_limit_bytes=24 * 1024 * 1024),
    )(*arguments)


def swap_cores(x):
    return lax.ppermute(x, "tile", [(0, 1), (1, 0)])


def exchange(plan, x, mask):
    dz, dx = divmod(mask, plan.narrow)
    mask = 2 * mask + ((dx ^ dz) & 1)
    pairs = [(i, i ^ mask) for i in range(2 * plan.wide * plan.narrow)]
    return lax.ppermute(x, ("wide", "narrow", "tile"), pairs)


def to_half(x):
    return lax.reduce_precision(x, exponent_bits=5, mantissa_bits=10)


def bounded_residual(plan, own, recv, target):
    sums = [own[k] + recv[k] for k in range(plan.ways)]
    total = sums[0]
    for x in [exchange(plan, sums[k].astype(F16), plan.near[k]) for k in plan.sums1]:
        total = total + x.astype(F32)
    for mask in plan.far:
        total = to_half(total)
        total = total + exchange(plan, total.astype(F16), mask).astype(F32)
    return jnp.tanh(total - target)


def scaled_residual(plan, own, recv, target):
    message = jax.ShapeDtypeStruct((plan.chunk + SUB, LANES), F32)

    def join(*parts):
        return call(sum_kernel, plan, message, [], parts, [VMEM] * len(parts))

    sums = call(join_kernel, plan, (message,) * plan.ways, [], (own, recv), [VMEM] * 2)
    parts = [sums[0]]
    for k in plan.sums2:
        parts.append(exchange(plan, sums[k].astype(F16), plan.near[k]).astype(F32))
    parts = [join(*parts)]
    for mask in plan.far:
        total = to_half(join(*parts) if len(parts) > 1 else parts[0])
        parts = [total, exchange(plan, total.astype(F16), mask).astype(F32)]
    return call(
        tanh_kernel, plan, jax.ShapeDtypeStruct(target.shape, F32), [],
        (target, *parts), [VMEM] * (1 + len(parts)),
    )


def spread(plan, chunk):
    mine = [chunk] + [exchange(plan, chunk, plan.near[k]) for k in plan.order[1:]]
    return mine, [swap_cores(x) for x in mine]


def on_device(mesh, green, log_strength, observed, owner_map):
    plan = Plan(mesh, green, observed, owner_map)
    shape = jax.ShapeDtypeStruct
    log_now = log_strength.reshape(-1, LANES)
    log_shape = shape(log_now.shape, F32)
    weighted_shape = shape((2, plan.points, plan.stations), BF16)
    total_shape = shape((plan.points, LANES), F32)
    kernel = pltpu.VMEM((plan.stations, plan.stations), BF16)
    stack = pltpu.VMEM((plan.ways, plan.chunk, LANES), BF16)

    def own_product(weighted, like):
        return call(own_product_kernel, plan, shape(like.shape, F32), [], (green, weighted), [VMEM] * 2)

    def own_contraction(tiles):
        return call(
            own_contraction_kernel, plan, total_shape, [kernel, stack], (green, *tiles),
            [VMEM] * (1 + len(tiles)),
        )

    places = jnp.asarray(plan.tile_places())
    tables = [pltpu.SMEM(x.shape, jnp.int32) for x in (owner_map, places)]
    target, *tables = call(
        observed_kernel, plan, (shape((plan.chunk, LANES), F32), *tables),
        [pltpu.SemaphoreType.DMA((2,))],
        (jnp.asarray(plan.strip_table()), observed, owner_map, places), [SMEM, VMEM, HBM, HBM],
        (VMEM, SMEM, SMEM),
    )
    send, weighted, green = call(
        first_kernel, plan,
        (shape((plan.ways, plan.chunk, LANES), F32), weighted_shape, shape(green.shape, BF16)),
        [
            pltpu.VMEM(log_now.shape, F32),
            pltpu.SemaphoreType.DMA((PIECES + 1,)),
        ],
        [pltpu.with_memory_space_constraint(x, pltpu.MemorySpace.HBM) for x in (log_now, green)],
        [HBM] * 2,
    )
    recv = swap_cores(send.astype(F16)).astype(F32)
    residual = bounded_residual(plan, own_product(weighted, send), recv, target)
    for _ in range(STEPS - 1):
        mine, others = spread(plan, residual.astype(BF16))
        levelled = shape((plan.ways, plan.chunk + SUB, LANES), F32)
        send, weighted, log_now = call(
            middle_kernel, plan, (levelled, weighted_shape, log_shape), [kernel, stack],
            (log_now, green, own_contraction(mine), *others), [VMEM] * (3 + len(others)),
        )
        scaled = call(scale_kernel, plan, levelled, [], (send,), [VMEM])
        recv = swap_cores(scaled.astype(F16)).astype(F32)
        residual = scaled_residual(plan, own_product(weighted, send), recv, target)
    mine, others = spread(plan, to_half(residual).astype(F16))
    mine = [x.astype(F32) for x in mine]
    log_now, owned = call(
        last_kernel, plan, (log_shape, shape((plan.slots, observed.shape[1]), F32)),
        [
            kernel, pltpu.VMEM((2, plan.ways * plan.chunk, LANES), F32),
            pltpu.VMEM(log_now.shape, F32),
        ],
        (
            log_now, green, own_contraction(mine), *tables,
            *mine, *[x.astype(F32) for x in others],
        ),
        [VMEM] * 3 + [SMEM] * 2 + [VMEM] * (2 * plan.ways),
    )
    return log_now.reshape(-1), owned


def solution(mesh):
    points = P(("grp", "wide", "narrow", "tile"))
    in_specs = (P(("grp", "wide", "narrow", "tile"), None), points, P("grp", None), P("grp"))
    out_specs = (points, P(("grp", "wide"), None))

    def program(green, log_strength, observed, owner_map):
        return on_device(mesh, green, log_strength, observed, owner_map)

    return jax.shard_map(
        program, mesh=mesh, in_specs=in_specs, out_specs=out_specs, check_vma=False
    )
```

```python
import math

import jax
import jax.numpy as jnp
import numpy as np
from jax import lax
from jax.experimental import pallas as pl
from jax.experimental.pallas import tpu as pltpu
from jax.sharding import PartitionSpec as P

STEPS = 2
LANES = 128
WIDE_BLOCK = 256
SUB = 8
TOP = 14.0
LN2 = math.log(2.0)
STRIPS, PIECES, BLOCK = 17, 4, 256
F32, BF16, F16 = jnp.float32, jnp.bfloat16, jnp.float16
VMEM = pl.BlockSpec(memory_space=pltpu.VMEM)
SMEM = pl.BlockSpec(memory_space=pltpu.SMEM)
HBM = pl.BlockSpec(memory_space=pltpu.MemorySpace.HBM)


def doubling(first, size):
    return [1 << k for k in range(first.bit_length() - 1, (size - 1).bit_length())]


class Plan:
    def __init__(self, mesh, green, observed, owner_map):
        self.points, columns = green.shape
        self.stations = columns // 2
        self.area = observed.shape[1] // 2
        self.width = math.isqrt(self.area)
        self.blocks = self.stations // self.width
        self.group = LANES // self.width
        self.wide = mesh.shape["wide"]
        self.narrow = mesh.shape["narrow"]
        self.ways, self.near, self.far = self.list_masks()
        self.strips = self.list_strips()
        self.run = -(-len(self.strips) // self.ways)
        self.chunk = self.run * self.width
        self.slots = owner_map.shape[0] // self.wide
        self.order = [k for k in (0, 2, 1, 3) if k < self.ways]
        self.sums1 = [k for k in (3, 2, 1) if k < self.ways]
        self.sums2 = [k for k in (2, 1, 3) if k < self.ways]

    def list_masks(self):
        bits = [step for step, size in ((1, self.narrow), (self.narrow, self.wide)) if size > 1]
        near = [0]
        for bit in bits:
            near += [mask ^ bit for mask in near]
        far = [self.narrow * (3 if k == 2 else k) for k in doubling(2, self.wide)]
        return len(near), near, far + doubling(2, self.narrow)

    def corner(self):
        x, z = lax.axis_index("narrow"), lax.axis_index("wide")
        return (x & 1) + ((z ^ (z >> 1)) & 1) * min(2, self.narrow)

    def half(self):
        x, z = lax.axis_index("narrow"), lax.axis_index("wide")
        return lax.axis_index("tile") ^ ((x ^ z) & 1)

    def list_strips(self):
        side, per, w = self.stations // LANES, self.group, self.width
        strips = []
        for i in range(side):
            for j in range(i + 1, side):
                strips += [[(i * per + s, j, 0, LANES, 0)] for s in range(per)]
        for i in range(side):
            for s in range(per // 2):
                strip = [(i * per + s, i, s * w, LANES, 0)]
                if s:
                    strip.append((i * per + per - s, i, 0, s * w, s * w))
                strips.append(strip)
        half = LANES // 2
        for i in range(0, side, 2):
            strip = [(i * per + per // 2, i, half, LANES, 0)]
            if i + 1 < side:
                strip.append(((i + 1) * per + per // 2, i + 1, 0, half, half))
            strips.append(strip)
        return strips

    def tile(self, row, col):
        return row * self.blocks - row * (row - 1) // 2 + col - row

    def strip_table(self):
        table = np.zeros((3, self.run * self.ways), np.int32)
        for k, strip in enumerate(self.strips):
            row, j, first, _, _ = strip[0]
            table[0, k] = self.tile(row, j * self.group)
            if len(strip) > 1:
                row, j, _, last, shift = strip[1]
                table[1, k] = self.tile(row, (j + 1) * self.group - shift // self.width)
                table[2, k] = last // self.width
        return table.reshape(-1)

    def tile_places(self):
        places = np.zeros(self.tile(self.blocks - 1, self.blocks - 1) + 1, np.int32)
        for k, strip in enumerate(self.strips):
            for row, j, first, last, shift in strip:
                for m in range(first // self.width, last // self.width):
                    col = j * self.group + m - shift // self.width + (self.group if shift > m * self.width else 0)
                    at = (k % self.run) * self.width
                    places[self.tile(row, col)] = (k // self.run) * 65536 + at * 16 + m
        return places


def contract(a, b, over_a, over_b):
    return lax.dot_general(a, b, (((over_a,), (over_b,)), ((), ())), preferred_element_type=F32)


def lean(x, shift, width):
    return pltpu.roll(x, shift, 1, stride=width, stride_axis=0)


def settle(x, width):
    n = LANES // width
    row = lax.broadcasted_iota(jnp.int32, (n, LANES), 0)
    run = lax.broadcasted_iota(jnp.int32, (n, LANES), 1) // width
    x = jnp.take_along_axis(x, (run + row + 1) & (n - 1), axis=0)
    return lean(x, width, width)


def unrolled(count, step, body):
    def several(i, carry):
        for k in range(step):
            body(i * step + k)
        return carry

    whole = count // step
    if whole > 1:
        lax.fori_loop(0, whole, several, 0)
    elif whole:
        several(0, 0)
    for i in range(whole * step, count):
        body(i)


def row_sums(total):
    parts = []
    for at in range(0, total.shape[0], LANES):
        parts.append(jnp.sum(total[at : at + LANES].T, axis=0, keepdims=True))
    return jnp.concatenate(parts, axis=0)


def columns_of(rows):
    blank = jnp.zeros((LANES - rows.shape[0], LANES), F32)
    return jnp.concatenate([rows, blank], axis=0).T


def weigh_rows(plan, green, strength, weighted, i):
    column = jnp.broadcast_to(strength[:, i : i + 1], (LANES, LANES))
    at = slice(i * LANES, (i + 1) * LANES)
    for h in range(2):
        for left in range(0, plan.stations, LANES):
            part = green[at, h * plan.stations + left : h * plan.stations + left + LANES]
            weighted[h, at, left : left + LANES] = (part.astype(F32) * column).astype(BF16)


def product_part(plan, half, green, weighted, j):
    ns, end = plan.stations, WIDE_BLOCK * (j + 1)
    sign = (1 - 2 * half).astype(F32)
    a = green[:, end - WIDE_BLOCK : end]
    b = green[:, ns + end - WIDE_BLOCK : ns + end]
    part = contract(weighted[half, :, :end], a, 0, 0)
    return part + sign * contract(weighted[1 - half, :, :end], b, 0, 0)


def pack(plan, j, part, out, most=None):
    z = plan.corner()
    w = plan.width
    lane = lax.broadcasted_iota(jnp.int32, (w, LANES), 1)
    for k, strip in enumerate(plan.strips):
        if strip[0][1] * LANES // WIDE_BLOCK != j:
            continue
        value = None
        for row, bj, _, last, shift in strip:
            left = bj * LANES % WIDE_BLOCK
            seen = part[row * w : (row + 1) * w, left : left + LANES]
            seen = pltpu.roll(seen, shift, 1) if shift else seen
            value = seen if value is None else jnp.where(lane < last, seen, value)
        at = k % plan.run * w
        out[(k // plan.run) ^ z, at : at + w, :] = value
        if most is not None:
            most = jnp.maximum(most, jnp.abs(value))
    return most


def pad(plan, out):
    z, w = plan.corner(), plan.width
    for k in range(len(plan.strips), plan.run * plan.ways):
        at = k % plan.run * w
        out[(k // plan.run) ^ z, at : at + w, :] = jnp.zeros((w, LANES), F32)


def product(plan, half, green, weighted, out):
    most = jnp.zeros((plan.width, LANES), F32) if out.shape[1] > plan.chunk else None
    for j in range(plan.stations // WIDE_BLOCK):
        most = pack(plan, j, product_part(plan, half, green, weighted, j), out, most)
    pad(plan, out)
    if most is not None:
        top = jnp.max(jnp.max(most, axis=0, keepdims=True), axis=1, keepdims=True)
        level = jnp.ceil(jnp.log2(jnp.maximum(top, 1e-30))) + (1.0 - TOP)
        out[:, plan.chunk :, :] = jnp.broadcast_to(level, (plan.ways, SUB, LANES))


def fill_half(plan, load, kernel):
    z = plan.corner()
    w = plan.width
    lane = lax.broadcasted_iota(jnp.int32, (w, LANES), 1)
    for k, strip in enumerate(plan.strips):
        value = load((k // plan.run) ^ z, k % plan.run * w)
        for row, bj, first, _, shift in strip:
            seen = value
            if shift:
                seen = pltpu.roll(value.astype(F32), LANES - shift, 1)
            start = first if not shift else LANES - shift
            if start:
                seen = jnp.where(lane >= start, seen.astype(F32), 0.0)
            kernel[row * w : (row + 1) * w, bj * LANES : (bj + 1) * LANES] = seen.astype(BF16)
    for at in range(0, plan.stations, WIDE_BLOCK):
        kernel[at + LANES : at + WIDE_BLOCK, at : at + LANES] = jnp.zeros(
            (WIDE_BLOCK - LANES, LANES), BF16
        )


def contraction(plan, half, green, kernel, at=slice(None)):
    ns = plan.stations
    near = pl.multiple_of(half * ns, LANES)
    far = pl.multiple_of((1 - half) * ns, LANES)
    sign = (1 - 2 * half).astype(F32)
    total = None
    for j in range(ns // WIDE_BLOCK):
        end = WIDE_BLOCK * (j + 1)
        block = kernel[:end, end - WIDE_BLOCK : end]
        u = contract(green[at, pl.ds(near, end)], block, 1, 0)
        v = contract(green[at, pl.ds(far, end)], block, 1, 0) * sign
        x = green[at, end - WIDE_BLOCK : end].astype(F32)
        y = green[at, ns + end - WIDE_BLOCK : ns + end].astype(F32)
        part = u * x + v * y
        for left in range(0, WIDE_BLOCK, LANES):
            seen = part[:, left : left + LANES]
            total = seen if total is None else total + seen
    return total


def observed_kernel(plan, table, observed, owners, places, out, owners_out, places_out, done):
    copies = [
        pltpu.make_async_copy(owners, owners_out, done.at[0]),
        pltpu.make_async_copy(places, places_out, done.at[1]),
    ]
    for copy in copies:
        copy.start()
    z = plan.corner()
    left = pl.multiple_of(plan.half() * plan.area, LANES)
    n, count = plan.group, plan.run * plan.ways
    row = lax.broadcasted_iota(jnp.int32, (n, LANES), 0)
    last = observed.shape[0] // n * n - n

    def strip(s):
        k = z * plan.run + s
        split = table[2 * count + k]
        for part in range(plan.area // LANES):
            at = pl.ds(pl.multiple_of(left + part * LANES, LANES), LANES)
            found = []
            for start in (table[k], table[count + k]):
                low = pl.multiple_of(start // n * n, n)
                high = pl.multiple_of(jnp.minimum(low + n, last), n)
                skip = start - low
                tiles = jnp.where(row >= skip, observed[pl.ds(low, n), at], observed[pl.ds(high, n), at])
                found.append(pltpu.roll(tiles, (n - skip) % n, 0))
            tiles = jnp.where(row < split, found[1], found[0])
            to = s * plan.width + part * n
            to = to if isinstance(to, int) else pl.multiple_of(to, n)
            tiles = settle(lean(tiles, 0, plan.width), plan.width)
            out[pl.ds(to, n), :] = jnp.take_along_axis(tiles, n - 1 - row, axis=0)

    unrolled(plan.run, STRIPS, strip)
    for copy in copies:
        copy.wait()


def first_kernel(plan, log_hbm, green_hbm, send, weighted, green, log_ref, done):
    pieces = done.shape[0] - 1
    size = plan.points // pieces
    copies = [pltpu.make_async_copy(log_hbm, log_ref, done.at[pieces])]
    for k in range(pieces):
        at = pl.ds(k * size, size)
        copies.append(pltpu.make_async_copy(green_hbm.at[at, :], green.at[at, :], done.at[k]))
    for copy in copies:
        copy.start()
    copies[0].wait()
    strength = columns_of(jnp.exp(log_ref[...]))
    for k in range(pieces):
        copies[1 + k].wait()
        for i in range(k * size // LANES, (k + 1) * size // LANES):
            weigh_rows(plan, green, strength, weighted, i)
    product(plan, 1 - plan.half(), green, weighted, send)


def own_product_kernel(plan, green, weighted, own):
    product(plan, plan.half(), green, weighted, own)


def own_contraction_kernel(plan, green, *refs):
    *tiles, total, kernel, stack = refs
    for k, ref in zip(plan.order, tiles):
        stack[k] = ref[...].astype(BF16)
    fill_half(plan, lambda slot, at: stack[slot, at : at + plan.width, :], kernel)
    total[...] = contraction(plan, plan.half(), green, kernel)


def new_log(plan, log_ref, green, total, kernel, log_out):
    total = total[...] + contraction(plan, 1 - plan.half(), green, kernel)
    log_now = log_ref[...]
    log_now = log_now - 0.5 * jnp.exp(log_now) * row_sums(total)
    log_out[...] = log_now
    return log_now


def middle_kernel(plan, log_ref, green, total, *refs):
    *tiles, send, weighted, log_out, kernel, stack = refs
    for k, ref in zip(plan.order, tiles):
        stack[k] = ref[...]
    fill_half(plan, lambda slot, at: stack[slot, at : at + plan.width, :], kernel)
    strength = columns_of(jnp.exp(new_log(plan, log_ref, green, total, kernel, log_out)))
    for i in range(plan.points // LANES):
        weigh_rows(plan, green, strength, weighted, i)
    product(plan, 1 - plan.half(), green, weighted, send)


def last_kernel(plan, log_ref, green, total, owners, places, *refs):
    *refs, log_out, residual, kernel, tiles, sums = refs
    mine, others = refs[: plan.ways], refs[plan.ways :]
    half, z, owned = plan.half(), plan.corner(), lax.axis_index("wide") * plan.slots
    n, w, c = plan.group, plan.width, plan.chunk
    for k, left, right in zip(plan.order, mine, others):
        tiles[half, k * c : (k + 1) * c, :] = left[...]
        tiles[1 - half, k * c : (k + 1) * c, :] = right[...]
    fill_half(
        plan,
        lambda slot, at: tiles[1 - half, pl.ds(pl.multiple_of(slot * c + at, w), w), :],
        kernel,
    )
    run = lax.broadcasted_iota(jnp.int32, (w, LANES), 1) // w

    def rows_of(first, count):
        found = [None, None]
        for m in range(count):
            place = places[owners[owned + first + m]]
            at = pl.multiple_of(((place >> 16) ^ z) * c + ((place >> 4) & 4095), w)
            shift = ((n - 1 - m - (place & 15)) & (n - 1)) * w
            for h in range(2):
                value = pltpu.roll(tiles[h, pl.ds(at, w), :], shift, 1)
                found[h] = value if m == 0 else jnp.where(run == n - 1 - m, value, found[h])
        parts = [found[h][k * n : (k + 1) * n] for h in range(2) for k in range(w // n)]
        return [settle(lean(x, 0, w), w) for x in parts]

    def batch(i):
        first = i * n if isinstance(i, int) else pl.multiple_of(i * n, n)
        for k, piece in enumerate(rows_of(first, n)):
            residual[pl.ds(first, n), k * LANES : (k + 1) * LANES] = piece

    whole = plan.slots // n
    steps = plan.points // BLOCK
    batches, rows = whole // steps, BLOCK // LANES

    def step(p, carry):
        at = pl.ds(pl.multiple_of(p * BLOCK, BLOCK), BLOCK)
        part = row_sums(total[at, :] + contraction(plan, 1 - half, green, kernel, at))
        for i in range(rows):
            sums[pl.ds(p * rows + i, 1), :] = part[i : i + 1, :]
        for k in range(batches):
            batch(p * batches + k)
        return carry

    rest = plan.slots - whole * n
    if rest:
        for k, piece in enumerate(rows_of(whole * n, rest)):
            residual[whole * n :, k * LANES : (k + 1) * LANES] = piece[:rest]
    lax.fori_loop(0, steps, step, 0)
    for i in range(batches * steps, whole):
        batch(i)
    log_now = log_ref[...]
    log_out[...] = log_now - 0.5 * jnp.exp(log_now) * sums[...]


def scale_kernel(plan, send, out):
    c = plan.chunk
    factor = jnp.exp(send[0, c : c + 1, :] * -LN2)
    for k in range(plan.ways):
        out[k, :c, :] = send[k, :c, :] * factor
        out[k, c:, :] = send[k, c:, :]


def join_kernel(plan, own, recv, *messages):
    c = plan.chunk
    mine, other = own[0, c : c + 1, :], recv[0, c : c + 1, :]
    level = jnp.maximum(mine, other) + 1.0
    factor, wider = jnp.exp(level * -LN2), jnp.exp((other - level) * LN2)
    for k, out in enumerate(messages):
        out[:c, :] = own[k, :c, :] * factor + recv[k, :c, :] * wider
        out[c:, :] = jnp.broadcast_to(level, (SUB, LANES))


def sum_kernel(plan, *refs):
    c = plan.chunk
    *messages, out = refs
    levels = [x[c : c + 1, :] for x in messages]
    level = levels[0]
    for x in levels[1:]:
        level = jnp.maximum(level, x)
    level = level + float(math.ceil(math.log2(len(messages))))
    out[:c, :] = sum(x[:c, :] * jnp.exp((at - level) * LN2) for x, at in zip(messages, levels))
    out[c:, :] = jnp.broadcast_to(level, (SUB, LANES))


def tanh_kernel(plan, target, *refs):
    *parts, out = refs
    c = plan.chunk
    total = sum(x[:c, :] * jnp.exp(x[c : c + 1, :] * LN2) for x in parts)
    out[...] = jnp.tanh(total - target[...])


def call(kernel, plan, out_shape, scratch, arguments, specs, out_specs=None):
    def body(*refs):
        kernel(plan, *refs)

    return pl.pallas_call(
        body,
        in_specs=specs,
        out_specs=out_specs or jax.tree.map(lambda _: VMEM, out_shape),
        out_shape=out_shape,
        scratch_shapes=scratch,
        compiler_params=pltpu.CompilerParams(vmem_limit_bytes=24 * 1024 * 1024),
    )(*arguments)


def swap_cores(x):
    return lax.ppermute(x, "tile", [(0, 1), (1, 0)])


def exchange(plan, x, mask):
    dz, dx = divmod(mask, plan.narrow)
    mask = 2 * mask + ((dx ^ dz) & 1)
    pairs = [(i, i ^ mask) for i in range(2 * plan.wide * plan.narrow)]
    return lax.ppermute(x, ("wide", "narrow", "tile"), pairs)


def to_half(x):
    return lax.reduce_precision(x, exponent_bits=5, mantissa_bits=10)


def bounded_residual(plan, own, recv, target):
    sums = [own[k] + recv[k] for k in range(plan.ways)]
    total = sums[0]
    for x in [exchange(plan, sums[k].astype(F16), plan.near[k]) for k in plan.sums1]:
        total = total + x.astype(F32)
    for mask in plan.far:
        total = to_half(total)
        total = total + exchange(plan, total.astype(F16), mask).astype(F32)
    return jnp.tanh(total - target)


def scaled_residual(plan, own, recv, target):
    message = jax.ShapeDtypeStruct((plan.chunk + SUB, LANES), F32)

    def join(*parts):
        return call(sum_kernel, plan, message, [], parts, [VMEM] * len(parts))

    sums = call(join_kernel, plan, (message,) * plan.ways, [], (own, recv), [VMEM] * 2)
    parts = [sums[0]]
    for k in plan.sums2:
        parts.append(exchange(plan, sums[k].astype(F16), plan.near[k]).astype(F32))
    parts = [join(*parts)]
    for mask in plan.far:
        total = to_half(join(*parts) if len(parts) > 1 else parts[0])
        parts = [total, exchange(plan, total.astype(F16), mask).astype(F32)]
    return call(
        tanh_kernel, plan, jax.ShapeDtypeStruct(target.shape, F32), [],
        (target, *parts), [VMEM] * (1 + len(parts)),
    )


def spread(plan, chunk):
    mine = [chunk] + [exchange(plan, chunk, plan.near[k]) for k in plan.order[1:]]
    return mine, [swap_cores(x) for x in mine]


def on_device(mesh, green, log_strength, observed, owner_map):
    plan = Plan(mesh, green, observed, owner_map)
    shape = jax.ShapeDtypeStruct
    log_now = log_strength.reshape(-1, LANES)
    log_shape = shape(log_now.shape, F32)
    weighted_shape = shape((2, plan.points, plan.stations), BF16)
    total_shape = shape((plan.points, LANES), F32)
    kernel = pltpu.VMEM((plan.stations, plan.stations), BF16)
    stack = pltpu.VMEM((plan.ways, plan.chunk, LANES), BF16)

    def own_product(weighted, like):
        return call(own_product_kernel, plan, shape(like.shape, F32), [], (green, weighted), [VMEM] * 2)

    def own_contraction(tiles):
        return call(
            own_contraction_kernel, plan, total_shape, [kernel, stack], (green, *tiles),
            [VMEM] * (1 + len(tiles)),
        )

    places = jnp.asarray(plan.tile_places())
    tables = [pltpu.SMEM(x.shape, jnp.int32) for x in (owner_map, places)]
    target, *tables = call(
        observed_kernel, plan, (shape((plan.chunk, LANES), F32), *tables),
        [pltpu.SemaphoreType.DMA((2,))],
        (jnp.asarray(plan.strip_table()), observed, owner_map, places), [SMEM, VMEM, HBM, HBM],
        (VMEM, SMEM, SMEM),
    )
    send, weighted, green = call(
        first_kernel, plan,
        (shape((plan.ways, plan.chunk, LANES), F32), weighted_shape, shape(green.shape, BF16)),
        [
            pltpu.VMEM(log_now.shape, F32),
            pltpu.SemaphoreType.DMA((PIECES + 1,)),
        ],
        [pltpu.with_memory_space_constraint(x, pltpu.MemorySpace.HBM) for x in (log_now, green)],
        [HBM] * 2,
    )
    recv = swap_cores(send.astype(F16)).astype(F32)
    residual = bounded_residual(plan, own_product(weighted, send), recv, target)
    for _ in range(STEPS - 1):
        mine, others = spread(plan, residual.astype(BF16))
        levelled = shape((plan.ways, plan.chunk + SUB, LANES), F32)
        send, weighted, log_now = call(
            middle_kernel, plan, (levelled, weighted_shape, log_shape), [kernel, stack],
            (log_now, green, own_contraction(mine), *others), [VMEM] * (3 + len(others)),
        )
        scaled = call(scale_kernel, plan, levelled, [], (send,), [VMEM])
        recv = swap_cores(scaled.astype(F16)).astype(F32)
        residual = scaled_residual(plan, own_product(weighted, send), recv, target)
    mine, others = spread(plan, to_half(residual).astype(F16))
    mine = [x.astype(F32) for x in mine]
    log_now, owned = call(
        last_kernel, plan, (log_shape, shape((plan.slots, observed.shape[1]), F32)),
        [
            kernel, pltpu.VMEM((2, plan.ways * plan.chunk, LANES), F32),
            pltpu.VMEM(log_now.shape, F32),
        ],
        (
            log_now, green, own_contraction(mine), *tables,
            *mine, *[x.astype(F32) for x in others],
        ),
        [VMEM] * 3 + [SMEM] * 2 + [VMEM] * (2 * plan.ways),
    )
    return log_now.reshape(-1), owned


def solution(mesh):
    points = P(("grp", "wide", "narrow", "tile"))
    in_specs = (P(("grp", "wide", "narrow", "tile"), None), points, P("grp", None), P("grp"))
    out_specs = (points, P(("grp", "wide"), None))

    def program(green, log_strength, observed, owner_map):
        return on_device(mesh, green, log_strength, observed, owner_map)

    return jax.shard_map(
        program, mesh=mesh, in_specs=in_specs, out_specs=out_specs, check_vma=False
    )
```

```python
import math

import jax
import jax.numpy as jnp
import numpy as np
from jax import lax
from jax.experimental import pallas as pl
from jax.experimental.pallas import tpu as pltpu
from jax.sharding import PartitionSpec as P

STEPS = 2
LANES = 128
WIDE_BLOCK = 256
SUB = 8
TOP = 14.0
LN2 = math.log(2.0)
STRIPS, PIECES, BLOCK = 17, 4, 256
F32, BF16, F16 = jnp.float32, jnp.bfloat16, jnp.float16
VMEM = pl.BlockSpec(memory_space=pltpu.VMEM)
SMEM = pl.BlockSpec(memory_space=pltpu.SMEM)
HBM = pl.BlockSpec(memory_space=pltpu.MemorySpace.HBM)


def doubling(first, size):
    return [1 << k for k in range(first.bit_length() - 1, (size - 1).bit_length())]


class Plan:
    def __init__(self, mesh, green, observed, owner_map):
        self.points, columns = green.shape
        self.stations = columns // 2
        self.area = observed.shape[1] // 2
        self.width = math.isqrt(self.area)
        self.blocks = self.stations // self.width
        self.group = LANES // self.width
        self.wide = mesh.shape["wide"]
        self.narrow = mesh.shape["narrow"]
        self.ways, self.near, self.far = self.list_masks()
        self.strips = self.list_strips()
        self.run = -(-len(self.strips) // self.ways)
        self.chunk = self.run * self.width
        self.slots = owner_map.shape[0] // self.wide
        self.order = [k for k in (0, 2, 1, 3) if k < self.ways]
        self.sums1 = [k for k in (3, 2, 1) if k < self.ways]
        self.sums2 = [k for k in (2, 1, 3) if k < self.ways]

    def list_masks(self):
        bits = [step for step, size in ((1, self.narrow), (self.narrow, self.wide)) if size > 1]
        near = [0]
        for bit in bits:
            near += [mask ^ bit for mask in near]
        far = [self.narrow * (3 if k == 2 else k) for k in doubling(2, self.wide)]
        return len(near), near, far + doubling(2, self.narrow)

    def corner(self):
        x, z = lax.axis_index("narrow"), lax.axis_index("wide")
        return (x & 1) + ((z ^ (z >> 1)) & 1) * min(2, self.narrow)

    def half(self):
        x, z = lax.axis_index("narrow"), lax.axis_index("wide")
        return lax.axis_index("tile") ^ ((x ^ z) & 1)

    def list_strips(self):
        side, per, w = self.stations // LANES, self.group, self.width
        strips = []
        for i in range(side):
            for j in range(i + 1, side):
                strips += [[(i * per + s, j, 0, LANES, 0)] for s in range(per)]
        for i in range(side):
            for s in range(per // 2):
                strip = [(i * per + s, i, s * w, LANES, 0)]
                if s:
                    strip.append((i * per + per - s, i, 0, s * w, s * w))
                strips.append(strip)
        half = LANES // 2
        for i in range(0, side, 2):
            strip = [(i * per + per // 2, i, half, LANES, 0)]
            if i + 1 < side:
                strip.append(((i + 1) * per + per // 2, i + 1, 0, half, half))
            strips.append(strip)
        return strips

    def tile(self, row, col):
        return row * self.blocks - row * (row - 1) // 2 + col - row

    def strip_table(self):
        table = np.zeros((3, self.run * self.ways), np.int32)
        for k, strip in enumerate(self.strips):
            row, j, first, _, _ = strip[0]
            table[0, k] = self.tile(row, j * self.group)
            if len(strip) > 1:
                row, j, _, last, shift = strip[1]
                table[1, k] = self.tile(row, (j + 1) * self.group - shift // self.width)
                table[2, k] = last // self.width
        return table.reshape(-1)

    def tile_places(self):
        places = np.zeros(self.tile(self.blocks - 1, self.blocks - 1) + 1, np.int32)
        for k, strip in enumerate(self.strips):
            for row, j, first, last, shift in strip:
                for m in range(first // self.width, last // self.width):
                    col = j * self.group + m - shift // self.width + (self.group if shift > m * self.width else 0)
                    at = (k % self.run) * self.width
                    places[self.tile(row, col)] = (k // self.run) * 65536 + at * 16 + m
        return places


def contract(a, b, over_a, over_b):
    return lax.dot_general(a, b, (((over_a,), (over_b,)), ((), ())), preferred_element_type=F32)


def lean(x, shift, width):
    return pltpu.roll(x, shift, 1, stride=width, stride_axis=0)


def settle(x, width):
    n = LANES // width
    row = lax.broadcasted_iota(jnp.int32, (n, LANES), 0)
    run = lax.broadcasted_iota(jnp.int32, (n, LANES), 1) // width
    x = jnp.take_along_axis(x, (run + row + 1) & (n - 1), axis=0)
    return lean(x, width, width)


def unrolled(count, step, body):
    def several(i, carry):
        for k in range(step):
            body(i * step + k)
        return carry

    whole = count // step
    if whole > 1:
        lax.fori_loop(0, whole, several, 0)
    elif whole:
        several(0, 0)
    for i in range(whole * step, count):
        body(i)


def row_sums(total):
    parts = []
    for at in range(0, total.shape[0], LANES):
        parts.append(jnp.sum(total[at : at + LANES].T, axis=0, keepdims=True))
    return jnp.concatenate(parts, axis=0)


def columns_of(rows):
    blank = jnp.zeros((LANES - rows.shape[0], LANES), F32)
    return jnp.concatenate([rows, blank], axis=0).T


def weigh_rows(plan, green, strength, weighted, i):
    column = jnp.broadcast_to(strength[:, i : i + 1], (LANES, LANES))
    at = slice(i * LANES, (i + 1) * LANES)
    for h in range(2):
        for left in range(0, plan.stations, LANES):
            part = green[at, h * plan.stations + left : h * plan.stations + left + LANES]
            weighted[h, at, left : left + LANES] = (part.astype(F32) * column).astype(BF16)


def product_part(plan, half, green, weighted, j):
    ns, end = plan.stations, WIDE_BLOCK * (j + 1)
    sign = (1 - 2 * half).astype(F32)
    a = green[:, end - WIDE_BLOCK : end]
    b = green[:, ns + end - WIDE_BLOCK : ns + end]
    part = contract(weighted[half, :, :end], a, 0, 0)
    return part + sign * contract(weighted[1 - half, :, :end], b, 0, 0)


def pack(plan, j, part, out, most=None):
    z = plan.corner()
    w = plan.width
    lane = lax.broadcasted_iota(jnp.int32, (w, LANES), 1)
    for k, strip in enumerate(plan.strips):
        if strip[0][1] * LANES // WIDE_BLOCK != j:
            continue
        value = None
        for row, bj, _, last, shift in strip:
            left = bj * LANES % WIDE_BLOCK
            seen = part[row * w : (row + 1) * w, left : left + LANES]
            seen = pltpu.roll(seen, shift, 1) if shift else seen
            value = seen if value is None else jnp.where(lane < last, seen, value)
        at = k % plan.run * w
        out[(k // plan.run) ^ z, at : at + w, :] = value
        if most is not None:
            most = jnp.maximum(most, jnp.abs(value))
    return most


def pad(plan, out):
    z, w = plan.corner(), plan.width
    for k in range(len(plan.strips), plan.run * plan.ways):
        at = k % plan.run * w
        out[(k // plan.run) ^ z, at : at + w, :] = jnp.zeros((w, LANES), F32)


def product(plan, half, green, weighted, out):
    most = jnp.zeros((plan.width, LANES), F32) if out.shape[1] > plan.chunk else None
    for j in range(plan.stations // WIDE_BLOCK):
        most = pack(plan, j, product_part(plan, half, green, weighted, j), out, most)
    pad(plan, out)
    if most is not None:
        top = jnp.max(jnp.max(most, axis=0, keepdims=True), axis=1, keepdims=True)
        level = jnp.ceil(jnp.log2(jnp.maximum(top, 1e-30))) + (1.0 - TOP)
        out[:, plan.chunk :, :] = jnp.broadcast_to(level, (plan.ways, SUB, LANES))


def fill_half(plan, load, kernel):
    z = plan.corner()
    w = plan.width
    lane = lax.broadcasted_iota(jnp.int32, (w, LANES), 1)
    for k, strip in enumerate(plan.strips):
        value = load((k // plan.run) ^ z, k % plan.run * w)
        for row, bj, first, _, shift in strip:
            seen = value
            if shift:
                seen = pltpu.roll(value.astype(F32), LANES - shift, 1)
            start = first if not shift else LANES - shift
            if start:
                seen = jnp.where(lane >= start, seen.astype(F32), 0.0)
            kernel[row * w : (row + 1) * w, bj * LANES : (bj + 1) * LANES] = seen.astype(BF16)
    for at in range(0, plan.stations, WIDE_BLOCK):
        kernel[at + LANES : at + WIDE_BLOCK, at : at + LANES] = jnp.zeros(
            (WIDE_BLOCK - LANES, LANES), BF16
        )


def contraction(plan, half, green, kernel, at=slice(None)):
    ns = plan.stations
    near = pl.multiple_of(half * ns, LANES)
    far = pl.multiple_of((1 - half) * ns, LANES)
    sign = (1 - 2 * half).astype(F32)
    total = None
    for j in range(ns // WIDE_BLOCK):
        end = WIDE_BLOCK * (j + 1)
        block = kernel[:end, end - WIDE_BLOCK : end]
        u = contract(green[at, pl.ds(near, end)], block, 1, 0)
        v = contract(green[at, pl.ds(far, end)], block, 1, 0) * sign
        x = green[at, end - WIDE_BLOCK : end].astype(F32)
        y = green[at, ns + end - WIDE_BLOCK : ns + end].astype(F32)
        part = u * x + v * y
        for left in range(0, WIDE_BLOCK, LANES):
            seen = part[:, left : left + LANES]
            total = seen if total is None else total + seen
    return total


def observed_kernel(plan, table, observed, owners, places, out, owners_out, places_out, done):
    copies = [
        pltpu.make_async_copy(owners, owners_out, done.at[0]),
        pltpu.make_async_copy(places, places_out, done.at[1]),
    ]
    for copy in copies:
        copy.start()
    z = plan.corner()
    left = pl.multiple_of(plan.half() * plan.area, LANES)
    n, count = plan.group, plan.run * plan.ways
    row = lax.broadcasted_iota(jnp.int32, (n, LANES), 0)
    last = observed.shape[0] // n * n - n

    def strip(s):
        k = z * plan.run + s
        split = table[2 * count + k]
        for part in range(plan.area // LANES):
            at = pl.ds(pl.multiple_of(left + part * LANES, LANES), LANES)
            found = []
            for start in (table[k], table[count + k]):
                low = pl.multiple_of(start // n * n, n)
                high = pl.multiple_of(jnp.minimum(low + n, last), n)
                skip = start - low
                tiles = jnp.where(row >= skip, observed[pl.ds(low, n), at], observed[pl.ds(high, n), at])
                found.append(pltpu.roll(tiles, (n - skip) % n, 0))
            tiles = jnp.where(row < split, found[1], found[0])
            to = s * plan.width + part * n
            to = to if isinstance(to, int) else pl.multiple_of(to, n)
            tiles = settle(lean(tiles, 0, plan.width), plan.width)
            out[pl.ds(to, n), :] = jnp.take_along_axis(tiles, n - 1 - row, axis=0)

    unrolled(plan.run, STRIPS, strip)
    for copy in copies:
        copy.wait()


def first_kernel(plan, log_hbm, green_hbm, send, weighted, green, log_ref, done):
    pieces = done.shape[0] - 1
    size = plan.points // pieces
    copies = [pltpu.make_async_copy(log_hbm, log_ref, done.at[pieces])]
    for k in range(pieces):
        at = pl.ds(k * size, size)
        copies.append(pltpu.make_async_copy(green_hbm.at[at, :], green.at[at, :], done.at[k]))
    for copy in copies:
        copy.start()
    copies[0].wait()
    strength = columns_of(jnp.exp(log_ref[...]))
    for k in range(pieces):
        copies[1 + k].wait()
        for i in range(k * size // LANES, (k + 1) * size // LANES):
            weigh_rows(plan, green, strength, weighted, i)
    product(plan, 1 - plan.half(), green, weighted, send)


def own_product_kernel(plan, green, weighted, own):
    product(plan, plan.half(), green, weighted, own)


def own_contraction_kernel(plan, green, *refs):
    *tiles, total, kernel, stack = refs
    for k, ref in zip(plan.order, tiles):
        stack[k] = ref[...].astype(BF16)
    fill_half(plan, lambda slot, at: stack[slot, at : at + plan.width, :], kernel)
    total[...] = contraction(plan, plan.half(), green, kernel)


def new_log(plan, log_ref, green, total, kernel, log_out):
    total = total[...] + contraction(plan, 1 - plan.half(), green, kernel)
    log_now = log_ref[...]
    log_now = log_now - 0.5 * jnp.exp(log_now) * row_sums(total)
    log_out[...] = log_now
    return log_now


def middle_kernel(plan, log_ref, green, total, *refs):
    *tiles, send, weighted, log_out, kernel, stack, sums = refs
    for k, ref in zip(plan.order, tiles):
        stack[k] = ref[...]
    fill_half(plan, lambda slot, at: stack[slot, at : at + plan.width, :], kernel)
    strength = columns_of(jnp.exp(new_log(plan, log_ref, green, total, kernel, log_out)))
    for i in range(plan.points // LANES):
        weigh_rows(plan, green, strength, weighted, i)
    product(plan, 1 - plan.half(), green, weighted, sums)
    scale(plan, sums, send)


def last_kernel(plan, log_ref, green, total, owners, places, *refs):
    *refs, log_out, residual, kernel, tiles, sums = refs
    mine, others = refs[: plan.ways], refs[plan.ways :]
    half, z, owned = plan.half(), plan.corner(), lax.axis_index("wide") * plan.slots
    n, w, c = plan.group, plan.width, plan.chunk
    for k, left, right in zip(plan.order, mine, others):
        tiles[half, k * c : (k + 1) * c, :] = left[...]
        tiles[1 - half, k * c : (k + 1) * c, :] = right[...]
    fill_half(
        plan,
        lambda slot, at: tiles[1 - half, pl.ds(pl.multiple_of(slot * c + at, w), w), :],
        kernel,
    )
    run = lax.broadcasted_iota(jnp.int32, (w, LANES), 1) // w

    def rows_of(first, count):
        found = [None, None]
        for m in range(count):
            place = places[owners[owned + first + m]]
            at = pl.multiple_of(((place >> 16) ^ z) * c + ((place >> 4) & 4095), w)
            shift = ((n - 1 - m - (place & 15)) & (n - 1)) * w
            for h in range(2):
                value = pltpu.roll(tiles[h, pl.ds(at, w), :], shift, 1)
                found[h] = value if m == 0 else jnp.where(run == n - 1 - m, value, found[h])
        parts = [found[h][k * n : (k + 1) * n] for h in range(2) for k in range(w // n)]
        return [settle(lean(x, 0, w), w) for x in parts]

    def batch(i):
        first = i * n if isinstance(i, int) else pl.multiple_of(i * n, n)
        for k, piece in enumerate(rows_of(first, n)):
            residual[pl.ds(first, n), k * LANES : (k + 1) * LANES] = piece

    whole = plan.slots // n
    steps = plan.points // BLOCK
    batches, rows = whole // steps, BLOCK // LANES

    def step(p, carry):
        at = pl.ds(pl.multiple_of(p * BLOCK, BLOCK), BLOCK)
        part = row_sums(total[at, :] + contraction(plan, 1 - half, green, kernel, at))
        for i in range(rows):
            sums[pl.ds(p * rows + i, 1), :] = part[i : i + 1, :]
        for k in range(batches):
            batch(p * batches + k)
        return carry

    rest = plan.slots - whole * n
    if rest:
        for k, piece in enumerate(rows_of(whole * n, rest)):
            residual[whole * n :, k * LANES : (k + 1) * LANES] = piece[:rest]
    lax.fori_loop(0, steps, step, 0)
    for i in range(batches * steps, whole):
        batch(i)
    log_now = log_ref[...]
    log_out[...] = log_now - 0.5 * jnp.exp(log_now) * sums[...]


def scale(plan, send, out):
    c = plan.chunk
    factor = jnp.exp(send[0, c : c + 1, :] * -LN2)
    for k in range(plan.ways):
        out[k, :c, :] = send[k, :c, :] * factor
        out[k, c:, :] = send[k, c:, :]


def join_kernel(plan, own, recv, *messages):
    c = plan.chunk
    mine, other = own[0, c : c + 1, :], recv[0, c : c + 1, :]
    level = jnp.maximum(mine, other) + 1.0
    factor, wider = jnp.exp(level * -LN2), jnp.exp((other - level) * LN2)
    for k, out in enumerate(messages):
        out[:c, :] = own[k, :c, :] * factor + recv[k, :c, :] * wider
        out[c:, :] = jnp.broadcast_to(level, (SUB, LANES))


def sum_kernel(plan, *refs):
    c = plan.chunk
    *messages, out = refs
    levels = [x[c : c + 1, :] for x in messages]
    level = levels[0]
    for x in levels[1:]:
        level = jnp.maximum(level, x)
    level = level + float(math.ceil(math.log2(len(messages))))
    out[:c, :] = sum(x[:c, :] * jnp.exp((at - level) * LN2) for x, at in zip(messages, levels))
    out[c:, :] = jnp.broadcast_to(level, (SUB, LANES))


def tanh_kernel(plan, target, *refs):
    *parts, out = refs
    c = plan.chunk
    total = sum(x[:c, :] * jnp.exp(x[c : c + 1, :] * LN2) for x in parts)
    out[...] = jnp.tanh(total - target[...])


def call(kernel, plan, out_shape, scratch, arguments, specs, out_specs=None):
    def body(*refs):
        kernel(plan, *refs)

    return pl.pallas_call(
        body,
        in_specs=specs,
        out_specs=out_specs or jax.tree.map(lambda _: VMEM, out_shape),
        out_shape=out_shape,
        scratch_shapes=scratch,
        compiler_params=pltpu.CompilerParams(vmem_limit_bytes=24 * 1024 * 1024),
    )(*arguments)


def swap_cores(x):
    return lax.ppermute(x, "tile", [(0, 1), (1, 0)])


def exchange(plan, x, mask):
    dz, dx = divmod(mask, plan.narrow)
    mask = 2 * mask + ((dx ^ dz) & 1)
    pairs = [(i, i ^ mask) for i in range(2 * plan.wide * plan.narrow)]
    return lax.ppermute(x, ("wide", "narrow", "tile"), pairs)


def to_half(x):
    return lax.reduce_precision(x, exponent_bits=5, mantissa_bits=10)


def bounded_residual(plan, own, recv, target):
    sums = [own[k] + recv[k] for k in range(plan.ways)]
    total = sums[0]
    for x in [exchange(plan, sums[k].astype(F16), plan.near[k]) for k in plan.sums1]:
        total = total + x.astype(F32)
    for mask in plan.far:
        total = to_half(total)
        total = total + exchange(plan, total.astype(F16), mask).astype(F32)
    return jnp.tanh(total - target)


def scaled_residual(plan, own, recv, target):
    message = jax.ShapeDtypeStruct((plan.chunk + SUB, LANES), F32)

    def join(*parts):
        return call(sum_kernel, plan, message, [], parts, [VMEM] * len(parts))

    sums = call(join_kernel, plan, (message,) * plan.ways, [], (own, recv), [VMEM] * 2)
    parts = [sums[0]]
    for k in plan.sums2:
        parts.append(exchange(plan, sums[k].astype(F16), plan.near[k]).astype(F32))
    parts = [join(*parts)]
    for mask in plan.far:
        total = to_half(join(*parts) if len(parts) > 1 else parts[0])
        parts = [total, exchange(plan, total.astype(F16), mask).astype(F32)]
    return call(
        tanh_kernel, plan, jax.ShapeDtypeStruct(target.shape, F32), [],
        (target, *parts), [VMEM] * (1 + len(parts)),
    )


def spread(plan, chunk):
    mine = [chunk] + [exchange(plan, chunk, plan.near[k]) for k in plan.order[1:]]
    return mine, [swap_cores(x) for x in mine]


def on_device(mesh, green, log_strength, observed, owner_map):
    plan = Plan(mesh, green, observed, owner_map)
    shape = jax.ShapeDtypeStruct
    log_now = log_strength.reshape(-1, LANES)
    log_shape = shape(log_now.shape, F32)
    weighted_shape = shape((2, plan.points, plan.stations), BF16)
    total_shape = shape((plan.points, LANES), F32)
    kernel = pltpu.VMEM((plan.stations, plan.stations), BF16)
    stack = pltpu.VMEM((plan.ways, plan.chunk, LANES), BF16)

    def own_product(weighted, like):
        return call(own_product_kernel, plan, shape(like.shape, F32), [], (green, weighted), [VMEM] * 2)

    def own_contraction(tiles):
        return call(
            own_contraction_kernel, plan, total_shape, [kernel, stack], (green, *tiles),
            [VMEM] * (1 + len(tiles)),
        )

    places = jnp.asarray(plan.tile_places())
    tables = [pltpu.SMEM(x.shape, jnp.int32) for x in (owner_map, places)]
    target, *tables = call(
        observed_kernel, plan, (shape((plan.chunk, LANES), F32), *tables),
        [pltpu.SemaphoreType.DMA((2,))],
        (jnp.asarray(plan.strip_table()), observed, owner_map, places), [SMEM, VMEM, HBM, HBM],
        (VMEM, SMEM, SMEM),
    )
    send, weighted, green = call(
        first_kernel, plan,
        (shape((plan.ways, plan.chunk, LANES), F32), weighted_shape, shape(green.shape, BF16)),
        [
            pltpu.VMEM(log_now.shape, F32),
            pltpu.SemaphoreType.DMA((PIECES + 1,)),
        ],
        [pltpu.with_memory_space_constraint(x, pltpu.MemorySpace.HBM) for x in (log_now, green)],
        [HBM] * 2,
    )
    recv = swap_cores(send.astype(F16)).astype(F32)
    residual = bounded_residual(plan, own_product(weighted, send), recv, target)
    for _ in range(STEPS - 1):
        mine, others = spread(plan, residual.astype(BF16))
        levelled = shape((plan.ways, plan.chunk + SUB, LANES), F32)
        send, weighted, log_now = call(
            middle_kernel, plan, (levelled, weighted_shape, log_shape),
            [kernel, stack, pltpu.VMEM(levelled.shape, F32)],
            (log_now, green, own_contraction(mine), *others), [VMEM] * (3 + len(others)),
        )
        recv = swap_cores(send.astype(F16)).astype(F32)
        residual = scaled_residual(plan, own_product(weighted, send), recv, target)
    mine, others = spread(plan, to_half(residual).astype(F16))
    mine = [x.astype(F32) for x in mine]
    log_now, owned = call(
        last_kernel, plan, (log_shape, shape((plan.slots, observed.shape[1]), F32)),
        [
            kernel, pltpu.VMEM((2, plan.ways * plan.chunk, LANES), F32),
            pltpu.VMEM(log_now.shape, F32),
        ],
        (
            log_now, green, own_contraction(mine), *tables,
            *mine, *[x.astype(F32) for x in others],
        ),
        [VMEM] * 3 + [SMEM] * 2 + [VMEM] * (2 * plan.ways),
    )
    return log_now.reshape(-1), owned


def solution(mesh):
    points = P(("grp", "wide", "narrow", "tile"))
    in_specs = (P(("grp", "wide", "narrow", "tile"), None), points, P("grp", None), P("grp"))
    out_specs = (points, P(("grp", "wide"), None))

    def program(green, log_strength, observed, owner_map):
        return on_device(mesh, green, log_strength, observed, owner_map)

    return jax.shard_map(
        program, mesh=mesh, in_specs=in_specs, out_specs=out_specs, check_vma=False
    )
```
